32 devices in a mesh: section: 4 (over y, x), dp: 8 (over z, core).
Axes of the slice: x: 2, y: 2, z: 4, core: 2. Of those that a mesh axis runs over, the one named last changes fastest.
Arguments:
- voxel_feats: bfloat16 [8, 16384, 64], P(None, 'dp'), may hold values from -6 to 6
- down_map: int32 [8, 8, 4096], P(None, None, 'dp'), may hold values from 0 to 2048, as said below
- neighbours: int32 [8, 27, 4096], P(None, None, 'dp'), may hold values from 0 to 512, as said below
- w_down: bfloat16 [8, 64, 128], replicated, may hold values from -0.25 to 0.25
- w_first: bfloat16 [27, 128, 128], replicated, may hold values from -0.109375 to 0.109375
- w_second: bfloat16 [27, 128, 128], replicated, may hold values from -0.109375 to 0.109375
- bn_scale: float32 [3, 128], replicated, may hold values from 0.25 to 1.75
- bn_shift: float32 [3, 128], replicated, may hold values from -3 to 3
- out_grad: bfloat16 [8, 4096, 128], P(None, 'dp'), may hold values from -6 to 6
Outputs:
- features: bfloat16 [8, 4096, 128], P('section', 'dp')
- input_grad: bfloat16 [8, 16384, 64], P('section', 'dp')
- grad_down: float32 [8, 64, 128], replicated
- grad_first: float32 [27, 128, 128], replicated
- grad_second: float32 [27, 128, 128], replicated
- grad_scale: float32 [3, 128], replicated
- grad_shift: float32 [3, 128], replicated
The draws below stay inside these ranges and needn't reach their ends.
Inputs may be any that keep to these rules, and one draw needn't show every extreme that they name: Offset k stands for the step (k // 9 - 1, (k // 3) % 3 - 1, k % 3 - 1) on the coarse grid. Entries index rows of the same bucket. The live rows of a bucket are its first ones; a live row r has neighbours[m, 13, r] = r, and every entry of a row that is not live is 512. The map is symmetric: where neighbours[m, k, p] = q, neighbours[m, 26 - k, q] = p. A bucket has 32 live rows or more, and in each micro-batch one bucket has all 512 live. `down_map`: entries index fine rows of the same bucket; 2048 marks an absent child. Each fine row is named at most once in a micro-batch. A live coarse row has 1 to 7 children and a row that is not live has none; the children of a bucket's live rows are its first 4 times as many fine rows, grouped by coarse row in order. In each micro-batch one bucket uses all 2048 fine rows.
All inputs are finite; a program needn't handle non-finite values.
Results may differ from the reference program's by a relative error of at most 0.012.
Values may be sent and summed in bfloat16 or wider, within the bound.
No kernel may reach another device: no remote copies, remote signals or barrier semaphores. Data moves between devices by JAX's collectives and lax.ppermute only.
A program may use at most 64 MiB of HBM per device.

```python
import jax
import jax.numpy as jnp
from jax import lax

C_IN = 64
C_MID = 128
VC_DEV = 512
MICRO = 8
VF_DEV = 2048
VC = 4096
VF = 16384
N_DP = 8


def voxel_block(block_key, rank):
    jitter_key, order_key, coin_key, pair_key, rank_key = jax.random.split(block_key, 5)
    top = N_DP - 1
    jitter = jax.random.randint(jitter_key, (), 0, VC_DEV // 64 + 1)
    jitter = jnp.where(rank == top, 0, jitter)
    live = 2 * (VC_DEV // 16 + 7 * (VC_DEV // 16) * rank * rank // (top * top) - jitter)
    depth = VC_DEV // 64
    order = jax.random.permutation(order_key, VC_DEV)
    place = jnp.argsort(order)
    cell = jnp.arange(VC_DEV)
    offset = jnp.arange(27)
    next_x = (cell // 64)[None, :] + (offset // 9 - 1)[:, None]
    next_y = (cell // 8 % 8)[None, :] + (offset // 3 % 3 - 1)[:, None]
    next_z = (cell % 8)[None, :] + (offset % 3 - 1)[:, None]
    inside = (next_x >= 0) & (next_x < depth) & (next_y >= 0) & (next_y < 8) & (next_z >= 0) & (next_z < 8)
    target = jnp.where(inside, next_x * 64 + next_y * 8 + next_z, 0)
    coins = jax.random.randint(coin_key, (27, VC_DEV), 0, 4) > 0
    mirrored = coins[26 - offset[:, None], target]
    linked = jnp.where(offset[:, None] > 13, coins, jnp.where(offset[:, None] < 13, mirrored, True)) & inside
    target_label = order[target]
    alive = linked & (target_label < live) & (order < live)[None, :]
    by_cell = jnp.where(alive, target_label, VC_DEV)
    near = by_cell[:, place]
    leading_sizes = jax.random.randint(pair_key, (VC_DEV // 2,), 1, 8)
    label = jnp.arange(VC_DEV)
    leading = leading_sizes[label // 2]
    kids = jnp.where(label % 2 == 0, leading, 8 - leading)
    start = 8 * (label // 2) + label % 2 * leading
    scores = jax.random.randint(rank_key, (VC_DEV, 8), 0, 1 << 20) * 8 + jnp.arange(8)[None, :]
    ranks = jnp.argsort(jnp.argsort(scores, axis=1), axis=1)
    child = (ranks < kids[:, None]) & (label < live)[:, None]
    below = jnp.where(child, start[:, None] + ranks, VF_DEV).T
    return (near.astype(jnp.int32), below.astype(jnp.int32))


def voxel_layout(key):
    spin = jax.random.randint(jax.random.fold_in(key, 11), (MICRO,), 0, N_DP)
    block_keys = jax.random.split(jax.random.fold_in(key, 13), MICRO * N_DP)
    rank_grid = (spin[:, None] + jnp.arange(N_DP)[None, :]) % N_DP
    near, below = jax.vmap(voxel_block)(block_keys, rank_grid.reshape(-1))
    near = near.reshape(MICRO, N_DP, 27, VC_DEV).transpose(0, 2, 1, 3).reshape(MICRO, 27, N_DP * VC_DEV)
    below = below.reshape(MICRO, N_DP, 8, VC_DEV).transpose(0, 2, 1, 3).reshape(MICRO, 8, N_DP * VC_DEV)
    return (near, below)


def draw_neighbours(key, part):
    shared = voxel_layout(key)
    return shared[0]


def draw_down_map(key, part):
    shared = voxel_layout(key)
    return shared[1]


def level_of(own_key, extent, shards, low, largest):
    level, own = 1.0, jax.random.fold_in(own_key, 6)
    for position, shards_of in shards:
        heights = jnp.exp(jax.random.uniform(jax.random.fold_in(own, position), (shards_of,), jnp.float32, low / len(shards), largest / len(shards)))
        level = level * jnp.repeat(heights, extent[position] // shards_of).reshape([-1 if axis == position else 1 for axis in range(len(extent))])
    return level


def centred(rng, dims, deviation, most, cuts=(), kind=jnp.bfloat16):
    factor_of = level_of(rng, dims, cuts, -0.22, 0.18) if cuts else 1.0
    array = jax.random.normal(rng, dims, jnp.float32) * deviation * factor_of
    return jnp.minimum(jnp.maximum(array, -most), most).astype(kind)


def setup_inputs(seed: int = 0) -> dict:
    seeds = jax.random.split(jax.random.key(seed), 10)
    return {
        "voxel_feats": centred(seeds[0], (MICRO, VF, C_IN), 1.0, 6.0, ((1, 8),)),
        "down_map": draw_down_map(jax.random.fold_in(seeds[9], 71), 0),
        "neighbours": draw_neighbours(jax.random.fold_in(seeds[9], 71), 0),
        "w_down": centred(seeds[3], (8, C_IN, C_MID), (8 * C_IN) ** -0.5, 0.25),
        "w_first": centred(seeds[4], (27, C_MID, C_MID), (27 * C_MID) ** -0.5, 0.109375),
        "w_second": centred(seeds[5], (27, C_MID, C_MID), (27 * C_MID) ** -0.5, 0.109375),
        "bn_scale": jnp.clip(1.0 + 0.15 * jax.random.normal(seeds[6], (3, C_MID), jnp.float32), 0.25, 1.75),
        "bn_shift": centred(seeds[7], (3, C_MID), 0.5, 3.0, (), jnp.float32),
        "out_grad": centred(seeds[8], (MICRO, VC, C_MID), 1.0, 6.0, ((1, 8),)),
    }


EPSILON = 1e-05
HIGHEST = lax.Precision.HIGHEST

@jax.custom_vjp
def low(v):
    return lax.optimization_barrier(v.astype(jnp.bfloat16)).astype(jnp.float32)

@jax.custom_vjp
def low_back(v):
    return v

def low_keep(v):
    return (low(v), None)

def low_pass(kept, grad):
    return (grad,)

def back_keep(v):
    return (v, None)

def back_low(kept, grad):
    return (low(grad),)
low.defvjp(low_keep, low_pass)
low_back.defvjp(back_keep, back_low)

def gather_rows(source, place_index):
    padded = jnp.concatenate([source, jnp.zeros((1, source.shape[1]), source.dtype)], axis=0)
    return padded[place_index]

def offset_apply(source, place_index, weight):
    return jnp.einsum('kpc,kco->po', gather_rows(source, place_index), weight, precision=HIGHEST)

def batch_norm(hidden, live_rows, gain_row, shift_row):
    count = jnp.sum(live_rows)
    mean_row = lax.optimization_barrier(jnp.sum(live_rows * hidden, axis=(0, 1))) / count
    spread = lax.optimization_barrier(jnp.sum(live_rows * hidden * hidden, axis=(0, 1))) / count - mean_row * mean_row
    return (hidden - mean_row) * lax.rsqrt(spread + EPSILON) * gain_row + shift_row

def micro_forward(params, features, down_maps, near_maps):
    w_down, w_first, w_second, bn_scale, bn_shift = params
    live_rows = (near_maps[:, 13, :] < VC_DEV).astype(jnp.float32)[:, :, None]
    per_bucket = jax.vmap(offset_apply, in_axes=(0, 0, None))
    hidden_zero = low_back(per_bucket(features, down_maps, w_down))
    act_zero = low(live_rows * jax.nn.silu(batch_norm(hidden_zero, live_rows, bn_scale[0], bn_shift[0])))
    conv_input = low_back(act_zero)
    skip_input = low_back(act_zero)
    hidden_one = low_back(per_bucket(conv_input, near_maps, w_first))
    act_one = low_back(low(live_rows * jax.nn.silu(batch_norm(hidden_one, live_rows, bn_scale[1], bn_shift[1]))))
    hidden_two = low_back(low(per_bucket(act_one, near_maps, w_second)))
    summed = batch_norm(hidden_two, live_rows, bn_scale[2], bn_shift[2]) + skip_input
    return live_rows * jax.nn.silu(summed)

def reference(voxel_feats, down_map, neighbours, w_down, w_first, w_second, bn_scale, bn_shift, out_grad):
    features = voxel_feats.astype(jnp.float32).reshape(MICRO, N_DP, VF_DEV, C_IN)
    down_maps = down_map.reshape(MICRO, 8, N_DP, VC_DEV).transpose(0, 2, 1, 3)
    near_maps = neighbours.reshape(MICRO, 27, N_DP, VC_DEV).transpose(0, 2, 1, 3)
    upstream = out_grad.astype(jnp.float32).reshape(MICRO, N_DP, VC_DEV, C_MID)
    params = (w_down.astype(jnp.float32), w_first.astype(jnp.float32), w_second.astype(jnp.float32), bn_scale, bn_shift)
    checked = jax.checkpoint(micro_forward)

    def whole(weights, inputs):
        return lax.map(lambda bundle: checked(weights, bundle[0], bundle[1], bundle[2]), (inputs, down_maps, near_maps))
    shown, pull = jax.vjp(whole, params, features)
    param_grads, feature_grads = pull(upstream)
    return (shown.reshape(MICRO, N_DP * VC_DEV, C_MID).astype(jnp.bfloat16), feature_grads.reshape(MICRO, N_DP * VF_DEV, C_IN).astype(jnp.bfloat16), param_grads[0], param_grads[1], param_grads[2], param_grads[3], param_grads[4])
```

```python
import functools

import jax
import jax.numpy as jnp
from jax import lax
from jax.experimental import pallas as pl
from jax.experimental.pallas import tpu as pltpu
from jax.sharding import PartitionSpec as P

EPSILON = 1e-05
F32 = jnp.float32
BF16 = jnp.bfloat16
VMEM_BYTES = 48 << 20


def mm(left, right):
    return jnp.dot(left, right, preferred_element_type=F32)


def mm_t(left, right):
    return lax.dot_general(left, right, (((1,), (1,)), ((), ())), preferred_element_type=F32)


def hits(index_row, rows):
    places = lax.broadcasted_iota(jnp.int16, (rows, index_row.shape[1]), 0)
    return jnp.where(places == index_row, jnp.bfloat16(1), jnp.bfloat16(0))


def near_hits(near_ref, offset):
    rows = near_ref.shape[2]
    return hits(near_ref[0, offset : offset + 1, :].astype(jnp.int16), rows)


def live_mask(near_ref, channels):
    rows = near_ref.shape[2]
    centre = near_ref[0, 13:14, :]
    count = jnp.sum((centre < rows).astype(F32), axis=1, keepdims=True)
    places = lax.broadcasted_iota(jnp.int32, (rows, channels), 0).astype(F32)
    return (places < count).astype(F32), count


def tree_sum(parts):
    parts = list(parts)
    while len(parts) > 1:
        parts = [parts[i] + parts[i + 1] for i in range(0, len(parts), 2)]
    return parts[0]


def moments(totals):
    count = totals[2:3]
    mean_row = totals[0:1] / count
    inv_std = lax.rsqrt(totals[1:2] / count - mean_row * mean_row + EPSILON)
    return mean_row, inv_std, count


def sigmoid(values):
    return 1.0 / (1.0 + jnp.exp(-values))


def put_sums(out_ref, first, second, count):
    channels = first.shape[1]
    third = jnp.broadcast_to(count, (1, channels))
    out_ref[0] = jnp.concatenate(
        [first, second, third, jnp.zeros((5, channels), F32)], axis=0
    )


def col_sum(values):
    return jnp.sum(values, axis=0, keepdims=True)


def parent_rows(down_ref, fine_rows):
    table = down_ref[0]
    first = jnp.min(table, axis=0, keepdims=True)
    children = jnp.sum((table < fine_rows).astype(jnp.int32), axis=0, keepdims=True)
    return table, first, first + children


def parent_hits(first, last, fine_rows, at, size):
    places = lax.broadcasted_iota(jnp.int16, (size, first.shape[1]), 0) + jnp.int16(at)
    inside = (places >= first.astype(jnp.int16)) & (places < last.astype(jnp.int16))
    return jnp.where(inside, jnp.bfloat16(1), jnp.bfloat16(0))


def down_kernel(where_ref, feats_ref, down_ref, near_ref, weight_ref, hidden_ref, sums_ref, kids_ref, which_ref, spread_ref):
    fine_rows, in_channels = feats_ref.shape[1], feats_ref.shape[2]
    offsets, coarse_rows = down_ref.shape[1], down_ref.shape[2]
    channels = weight_ref.shape[1]
    table, first, last = parent_rows(down_ref, fine_rows)
    rank = table - first
    numbers = lax.broadcasted_iota(jnp.int32, (offsets, coarse_rows), 0) + 1
    rows = [
        jnp.sum(jnp.where(rank == r, numbers, 0), axis=0, keepdims=True) for r in range(8)
    ]
    safe_first = jnp.where(first < fine_rows, first, 0)
    rows += [(safe_first // 16) * 16, safe_first % 16] + [jnp.zeros_like(first)] * 6
    lookup = jnp.concatenate(rows, axis=0).astype(F32).astype(BF16)
    step = 512
    for at in range(0, fine_rows, step):
        found = mm_t(parent_hits(first, last, fine_rows, at, step), lookup)
        begin = found[:, 8:9] + found[:, 9:10]
        place = lax.broadcasted_iota(jnp.int32, (step, 16), 0).astype(F32) + float(at)
        column = lax.broadcasted_iota(jnp.int32, (step, 16), 1).astype(F32)
        which = jnp.sum(
            jnp.where((column == place - begin) & (column < 8.0), found, 0.0), axis=1, keepdims=True
        )
        lane_half = (lax.broadcasted_iota(jnp.int32, (step, 2 * in_channels), 1) // in_channels).astype(F32)
        code = jnp.broadcast_to(which, (step, 2 * in_channels)) - lane_half
        which_ref[0, at : at + step] = code.astype(BF16)
        pair = jnp.concatenate([feats_ref[0, at : at + step]] * 2, axis=1)
        blank = jnp.zeros_like(pair)
        for j in range(offsets // 2):
            spread_ref[at : at + step, 2 * in_channels * j : 2 * in_channels * (j + 1)] = jnp.where(
                code == float(2 * j + 1), pair, blank
            )
    edges = jnp.concatenate([first, last, jnp.zeros((6, coarse_rows), jnp.int32)], axis=0).astype(F32)
    edges = jnp.transpose(edges)
    lanes = lax.broadcasted_iota(jnp.int32, (1, fine_rows), 1).astype(F32)
    part = 128
    total = jnp.zeros((1, channels), F32)
    square = jnp.zeros((1, channels), F32)
    for at in range(0, coarse_rows, part):
        low, high = edges[at : at + part, 0:1], edges[at : at + part, 1:2]
        owns = jnp.where((lanes >= low) & (lanes < high), 1.0, 0.0).astype(BF16)
        kids = mm(owns, spread_ref[...]).astype(BF16)
        kids_ref[0, at : at + part] = kids
        hidden = mm(kids, weight_ref[...])
        hidden_ref[0, at : at + part] = hidden
        total = total + col_sum(hidden)
        square = square + col_sum(hidden * hidden)
    _, count = live_mask(near_ref, channels)
    put_sums(sums_ref, total, square, count)


def conv_all(source, near_ref, weight_ref):
    out = mm(source, weight_ref[13])
    for j in range(0, 13):
        rows = [
            mm(near_hits(near_ref, 26 - k), source).astype(BF16) for k in (j, 26 - j)
        ]
        weight = jnp.concatenate([weight_ref[j], weight_ref[26 - j]], axis=0)
        out = out + mm(jnp.concatenate(rows, axis=1), weight)
    return out


def forward_kernel(norm_at, rounded, where_ref, hidden_ref, near_ref, weight_ref, scale_ref, shift_ref, *refs):
    part_refs, (act_ref, next_ref, sums_ref) = refs[:-3], refs[-3:]
    mean_row, inv_std, _ = moments(tree_sum([ref[0] for ref in part_refs]))
    live, count = live_mask(near_ref, hidden_ref.shape[2])
    value = (hidden_ref[0] - mean_row) * inv_std * scale_ref[norm_at : norm_at + 1] + shift_ref[norm_at : norm_at + 1]
    act = (live * (value * sigmoid(value))).astype(BF16)
    act_ref[0] = act
    hidden = conv_all(act, near_ref, weight_ref)
    if rounded:
        hidden = hidden.astype(BF16)
    next_ref[0] = hidden
    hidden = hidden.astype(F32)
    put_sums(sums_ref, col_sum(hidden), col_sum(hidden * hidden), count)


def output_kernel(where_ref, hidden_ref, act_ref, grad_ref, near_ref, scale_ref, shift_ref, *refs):
    part_refs, (features_ref, slope_ref, sums_ref) = refs[:-3], refs[-3:]
    mean_row, inv_std, _ = moments(tree_sum([ref[0] for ref in part_refs]))
    live, count = live_mask(near_ref, hidden_ref.shape[2])
    centred = (hidden_ref[0].astype(F32) - mean_row) * inv_std
    value = centred * scale_ref[2:3] + shift_ref[2:3] + act_ref[0].astype(F32)
    gate = sigmoid(value)
    features_ref[0] = (live * (value * gate)).astype(BF16)
    upstream = grad_ref[0].astype(F32) * live * (gate * (1.0 + value * (1.0 - gate)))
    slope_ref[0] = upstream
    put_sums(sums_ref, col_sum(upstream), col_sum(upstream * centred), count)


def norm_back(upstream, centred, live, inv_std, gain_row, back, count):
    return live * (inv_std * gain_row) * (upstream - back[0:1] / count - centred * (back[1:2] / count))


def backward_kernel(norm_at, with_skip, ways, where_ref, *refs):
    upstream_ref, hidden_ref, lower_ref, act_ref, near_ref, weight_ref, scale_ref, shift_ref = refs[:8]
    own_refs = refs[8 : 8 + ways]
    back_refs = refs[8 + ways : 8 + 2 * ways]
    below_refs = refs[8 + 2 * ways : 8 + 3 * ways]
    rest = refs[8 + 3 * ways :]
    skip_ref = rest[0] if with_skip else None
    next_ref, sums_ref, grad_ref = rest[-3:]
    mean_row, inv_std, count = moments(tree_sum([ref[0] for ref in own_refs]))
    back = tree_sum([ref[0] for ref in back_refs])
    live, own_count = live_mask(near_ref, hidden_ref.shape[2])
    centred = (hidden_ref[0].astype(F32) - mean_row) * inv_std
    rows_grad = norm_back(
        upstream_ref[0], centred, live, inv_std, scale_ref[norm_at : norm_at + 1], back, count
    ).astype(BF16)

    @pl.when(pl.program_id(0) == 0)
    def _():
        grad_ref[...] = jnp.zeros_like(grad_ref)

    channels = hidden_ref.shape[2]
    act_t = jnp.transpose(act_ref[0])
    below = mm_t(rows_grad, weight_ref[13])
    grad_ref[13] += mm(act_t, rows_grad)
    for j in range(13):
        moved = jnp.concatenate(
            [mm(near_hits(near_ref, k), rows_grad).astype(BF16) for k in (j, 26 - j)], axis=1
        )
        weight = jnp.concatenate([weight_ref[j], weight_ref[26 - j]], axis=1)
        below = below + mm_t(moved, weight)
        pair = mm(act_t, moved)
        grad_ref[j] += pair[:, :channels]
        grad_ref[26 - j] += pair[:, channels:]
    below = below.astype(BF16).astype(F32)
    if with_skip:
        below = below + skip_ref[0].astype(BF16).astype(F32)
    low_mean, low_std, _ = moments(tree_sum([ref[0] for ref in below_refs]))
    low_centred = (lower_ref[0] - low_mean) * low_std
    value = low_centred * scale_ref[norm_at - 1 : norm_at] + shift_ref[norm_at - 1 : norm_at]
    gate = sigmoid(value)
    upstream = below * live * (gate * (1.0 + value * (1.0 - gate)))
    next_ref[0] = upstream
    put_sums(sums_ref, col_sum(upstream), col_sum(upstream * low_centred), own_count)


def input_kernel(ways, where_ref, upstream_ref, hidden_ref, kids_ref, which_ref, down_ref, near_ref, weight_ref, scale_ref, *refs):
    own_refs, back_refs = refs[:ways], refs[ways : 2 * ways]
    input_ref, grad_ref = refs[2 * ways :]
    mean_row, inv_std, count = moments(tree_sum([ref[0] for ref in own_refs]))
    back = tree_sum([ref[0] for ref in back_refs])
    live, _ = live_mask(near_ref, hidden_ref.shape[2])
    centred = (hidden_ref[0] - mean_row) * inv_std
    rows_grad = norm_back(
        upstream_ref[0], centred, live, inv_std, scale_ref[0:1], back, count
    ).astype(BF16)

    @pl.when(pl.program_id(0) == 0)
    def _():
        grad_ref[...] = jnp.zeros_like(grad_ref)

    grad_ref[...] += jnp.transpose(mm(jnp.transpose(rows_grad), kids_ref[0]))
    pieces = mm_t(rows_grad, weight_ref[...]).astype(BF16)
    fine_rows, in_channels = input_ref.shape[1], input_ref.shape[2]
    _, first, last = parent_rows(down_ref, fine_rows)
    wide = 2 * in_channels
    step = 256
    for at in range(0, fine_rows, step):
        full = mm(parent_hits(first, last, fine_rows, at, step), pieces)
        code = which_ref[0, at : at + step].astype(F32)
        out = jnp.zeros((step, wide), F32)
        for j in range(full.shape[1] // wide):
            out = out + jnp.where(code == float(2 * j + 1), full[:, wide * j : wide * (j + 1)], 0.0)
        input_ref[0, at : at + step] = (out[:, :in_channels] + out[:, in_channels:]).astype(BF16)


def whole(array):
    return pl.BlockSpec(array.shape, lambda b, where: (0,) * array.ndim)


def per_micro(array, picked):
    block = (1,) + array.shape[1:]
    rest = (0,) * (array.ndim - 1)
    if picked:
        return pl.BlockSpec(block, lambda b, where: (where[0] + b,) + rest)
    return pl.BlockSpec(block, lambda b, where: (b,) + rest)


def call(kernel, steps, where, operands, kinds, outs, out_kinds, scratch=()):
    def spec(array, kind):
        if kind == "all":
            return whole(array)
        return per_micro(array, kind == "pick")

    return pl.pallas_call(
        kernel,
        grid_spec=pltpu.PrefetchScalarGridSpec(
            num_scalar_prefetch=1,
            grid=(steps,),
            in_specs=[spec(a, k) for a, k in zip(operands, kinds)],
            out_specs=[spec(a, k) for a, k in zip(outs, out_kinds)],
            scratch_shapes=list(scratch),
        ),
        out_shape=outs,
        compiler_params=pltpu.CompilerParams(
            vmem_limit_bytes=VMEM_BYTES, dimension_semantics=("arbitrary",)
        ),
    )(where, *operands)


def bucket_sums(value, axis):
    count = lax.axis_size(axis)
    value = value + lax.ppermute(value, axis, [(i, i ^ 1) for i in range(count)])
    return [value] + [
        lax.ppermute(value, axis, [(i, i ^ step) for i in range(count)])
        for step in range(2, count, 2)
    ]


def local(
    voxel_feats, down_map, neighbours, w_down, w_first, w_second, bn_scale, bn_shift, out_grad
):
    sections = lax.axis_size("section")
    mine = voxel_feats.shape[0] // sections
    where = jnp.reshape(lax.axis_index("section") * mine, (1,)).astype(jnp.int32)
    fine_rows, in_channels = voxel_feats.shape[1:]
    coarse_rows = neighbours.shape[2]
    channels = w_first.shape[2]
    offsets = down_map.shape[1]
    wide = offsets * in_channels
    flat_down = w_down.reshape(wide, channels)
    shape = jax.ShapeDtypeStruct
    rows_f32 = shape((mine, coarse_rows, channels), F32)
    rows_bf16 = shape((mine, coarse_rows, channels), BF16)
    sums = shape((mine, 8, channels), F32)

    hidden_zero, part_zero, kids, which = call(
        down_kernel, mine, where,
        [voxel_feats, down_map, neighbours, flat_down],
        ["pick", "pick", "pick", "all"],
        [rows_f32, sums, shape((mine, coarse_rows, wide), BF16), shape((mine, fine_rows, 2 * in_channels), BF16)],
        ["own"] * 4,
        [pltpu.VMEM((fine_rows, wide), BF16)],
    )
    stats_zero = bucket_sums(part_zero, "dp")
    ways = len(stats_zero)
    act_zero, hidden_one, part_one = call(
        functools.partial(forward_kernel, 0, False), mine, where,
        [hidden_zero, neighbours, w_first, bn_scale, bn_shift] + stats_zero,
        ["own", "pick", "all", "all", "all"] + ["own"] * ways,
        [rows_bf16, rows_f32, sums], ["own"] * 3,
    )
    stats_one = bucket_sums(part_one, "dp")
    act_one, hidden_two, part_two = call(
        functools.partial(forward_kernel, 1, True), mine, where,
        [hidden_one, neighbours, w_second, bn_scale, bn_shift] + stats_one,
        ["own", "pick", "all", "all", "all"] + ["own"] * ways,
        [rows_bf16, rows_bf16, sums], ["own"] * 3,
    )
    stats_two = bucket_sums(part_two, "dp")
    features, up_two, back_part = call(
        output_kernel, mine, where,
        [hidden_two, act_zero, out_grad, neighbours, bn_scale, bn_shift] + stats_two,
        ["own", "own", "pick", "pick", "all", "all"] + ["own"] * ways,
        [rows_bf16, rows_f32, sums], ["own"] * 3,
    )
    back_two = bucket_sums(back_part, "dp")
    grad_shape = shape(w_first.shape, F32)
    up_one, back_part, grad_second = call(
        functools.partial(backward_kernel, 2, False, ways), mine, where,
        [up_two, hidden_two, hidden_one, act_one, neighbours, w_second, bn_scale, bn_shift]
        + stats_two + back_two + stats_one,
        ["own"] * 4 + ["pick"] + ["all"] * 3 + ["own"] * (3 * ways),
        [rows_f32, sums, grad_shape], ["own", "own", "all"],
    )
    back_one = bucket_sums(back_part, "dp")
    up_zero, back_part, grad_first = call(
        functools.partial(backward_kernel, 1, True, ways), mine, where,
        [up_one, hidden_one, hidden_zero, act_zero, neighbours, w_first, bn_scale, bn_shift]
        + stats_one + back_one + stats_zero + [up_two],
        ["own"] * 4 + ["pick"] + ["all"] * 3 + ["own"] * (3 * ways + 1),
        [rows_f32, sums, grad_shape], ["own", "own", "all"],
    )
    back_zero = bucket_sums(back_part, "dp")
    input_grad, grad_down = call(
        functools.partial(input_kernel, ways), mine, where,
        [up_zero, hidden_zero, kids, which, down_map, neighbours, flat_down, bn_scale]
        + stats_zero + back_zero,
        ["own"] * 4 + ["pick"] * 2 + ["all"] * 2 + ["own"] * (2 * ways),
        [shape((mine, fine_rows, in_channels), BF16), shape((wide, channels), F32)], ["own", "all"],
    )
    norm_sums = jnp.stack(
        [jnp.sum(tree_sum(parts)[:, :2], axis=0) for parts in (back_zero, back_one, back_two)]
    )
    norm_sums = lax.psum(norm_sums, "section")
    grad_down, grad_first, grad_second = lax.psum((grad_down, grad_first, grad_second), ("section", "dp"))
    return (
        features,
        input_grad,
        grad_down.reshape(w_down.shape),
        grad_first,
        grad_second,
        norm_sums[:, 1],
        norm_sums[:, 0],
    )


def solution(mesh):
    in_specs = (
        P(None, "dp", None),
        P(None, None, "dp"),
        P(None, None, "dp"),
        P(),
        P(),
        P(),
        P(),
        P(),
        P(None, "dp", None),
    )
    out_specs = (P("section", "dp", None), P("section", "dp", None), P(), P(), P(), P(), P())
    return jax.shard_map(local, mesh=mesh, in_specs=in_specs, out_specs=out_specs, check_vma=False)
```

```python
import functools

import jax
import jax.numpy as jnp
from jax import lax
from jax.experimental import pallas as pl
from jax.experimental.pallas import tpu as pltpu
from jax.sharding import PartitionSpec as P

EPSILON = 1e-05
F32 = jnp.float32
BF16 = jnp.bfloat16
VMEM_BYTES = 48 << 20


def mm(left, right):
    return jnp.dot(left, right, preferred_element_type=F32)


def mm_t(left, right):
    return lax.dot_general(left, right, (((1,), (1,)), ((), ())), preferred_element_type=F32)


def hits(index_row, rows):
    places = lax.broadcasted_iota(jnp.int16, (rows, index_row.shape[1]), 0)
    return jnp.where(places == index_row, jnp.bfloat16(1), jnp.bfloat16(0))


def near_row(where_ref, near_ref, offset):
    return near_ref[offset, pl.ds(where_ref[0] + pl.program_id(0), 1), :]


def near_hits(where_ref, near_ref, offset):
    row = near_row(where_ref, near_ref, offset)
    return hits(row.astype(jnp.int16), row.shape[1])


def live_mask(where_ref, near_ref, channels):
    rows = near_ref.shape[2]
    centre = near_row(where_ref, near_ref, 13)
    count = jnp.sum((centre < rows).astype(F32), axis=1, keepdims=True)
    places = lax.broadcasted_iota(jnp.int32, (rows, channels), 0).astype(F32)
    return (places < count).astype(F32), count


def tree_sum(parts):
    parts = list(parts)
    while len(parts) > 1:
        parts = [parts[i] + parts[i + 1] for i in range(0, len(parts), 2)]
    return parts[0]


def moments(totals):
    count = totals[2:3]
    mean_row = totals[0:1] / count
    inv_std = lax.rsqrt(totals[1:2] / count - mean_row * mean_row + EPSILON)
    return mean_row, inv_std, count


def sigmoid(values):
    return 1.0 / (1.0 + jnp.exp(-values))


def put_sums(out_ref, first, second, count):
    channels = first.shape[1]
    third = jnp.broadcast_to(count, (1, channels))
    out_ref[0] = jnp.concatenate(
        [first, second, third, jnp.zeros((5, channels), F32)], axis=0
    )


def col_sum(values):
    return jnp.sum(values, axis=0, keepdims=True)


def parent_rows(down_ref, fine_rows):
    table = down_ref[0]
    first = jnp.min(table, axis=0, keepdims=True)
    children = jnp.sum((table < fine_rows).astype(jnp.int32), axis=0, keepdims=True)
    return table, first, first + children


def parent_hits(first, last, fine_rows, at, size):
    places = lax.broadcasted_iota(jnp.int16, (size, first.shape[1]), 0) + jnp.int16(at)
    inside = (places >= first.astype(jnp.int16)) & (places < last.astype(jnp.int16))
    return jnp.where(inside, jnp.bfloat16(1), jnp.bfloat16(0))


def down_kernel(where_ref, feats_ref, down_ref, near_ref, weight_ref, hidden_ref, sums_ref, kids_ref, which_ref, spread_ref, parent_ref):
    in_channels, fine_rows = feats_ref.shape[1], feats_ref.shape[2]
    offsets, coarse_rows = down_ref.shape[1], down_ref.shape[2]
    channels = weight_ref.shape[1]
    table, first, last = parent_rows(down_ref, fine_rows)
    rank = table - first
    numbers = lax.broadcasted_iota(jnp.int32, (offsets, coarse_rows), 0) + 1
    rows = [
        jnp.sum(jnp.where(rank == r, numbers, 0), axis=0, keepdims=True) for r in range(8)
    ]
    safe_first = jnp.where(first < fine_rows, first, 0)
    rows += [(safe_first // 16) * 16, safe_first % 16] + [jnp.zeros_like(first)] * 6
    lookup = jnp.concatenate(rows, axis=0).astype(F32).astype(BF16)
    step = 512
    for at in range(0, fine_rows, step):
        parent_ref[at : at + step] = parent_hits(first, last, fine_rows, at, step)
    found = mm_t(lookup, parent_ref[...])
    place = lax.broadcasted_iota(jnp.int32, (8, fine_rows), 1).astype(F32) - (found[8:9] + found[9:10])
    column = lax.broadcasted_iota(jnp.int32, (8, fine_rows), 0).astype(F32)
    which = jnp.sum(jnp.where(column == place, found[:8], 0.0), axis=0, keepdims=True)
    which_ref[0] = jnp.broadcast_to(which, (8, fine_rows))
    code = jnp.broadcast_to(which, (in_channels, fine_rows)).astype(BF16)
    feats = feats_ref[0]
    for k in range(offsets):
        spread_ref[in_channels * k : in_channels * (k + 1)] = jnp.where(
            code == jnp.bfloat16(k + 1), feats, jnp.zeros_like(feats)
        )
    kids = mm(spread_ref[...], parent_ref[...]).astype(BF16)
    kids_ref[0] = kids
    hidden = jnp.transpose(mm(jnp.transpose(weight_ref[...]), kids))
    hidden_ref[0] = hidden
    _, count = live_mask(where_ref, near_ref, channels)
    put_sums(sums_ref, col_sum(hidden), col_sum(hidden * hidden), count)


def conv_all(where_ref, source, near_ref, weight_ref):
    out = mm(source, weight_ref[13])
    for j in range(0, 13):
        rows = [
            mm(near_hits(where_ref, near_ref, 26 - k), source).astype(BF16) for k in (j, 26 - j)
        ]
        weight = jnp.concatenate([weight_ref[j], weight_ref[26 - j]], axis=0)
        out = out + mm(jnp.concatenate(rows, axis=1), weight)
    return out


def forward_kernel(norm_at, rounded, where_ref, hidden_ref, near_ref, weight_ref, scale_ref, shift_ref, *refs):
    part_refs, (act_ref, next_ref, sums_ref) = refs[:-3], refs[-3:]
    mean_row, inv_std, _ = moments(tree_sum([ref[0] for ref in part_refs]))
    live, count = live_mask(where_ref, near_ref, hidden_ref.shape[2])
    value = (hidden_ref[0] - mean_row) * inv_std * scale_ref[norm_at : norm_at + 1] + shift_ref[norm_at : norm_at + 1]
    act = (live * (value * sigmoid(value))).astype(BF16)
    act_ref[0] = act
    hidden = conv_all(where_ref, act, near_ref, weight_ref)
    if rounded:
        hidden = hidden.astype(BF16)
    next_ref[0] = hidden
    hidden = hidden.astype(F32)
    put_sums(sums_ref, col_sum(hidden), col_sum(hidden * hidden), count)


def output_kernel(where_ref, hidden_ref, act_ref, grad_ref, near_ref, scale_ref, shift_ref, *refs):
    part_refs, (features_ref, slope_ref, sums_ref) = refs[:-3], refs[-3:]
    mean_row, inv_std, _ = moments(tree_sum([ref[0] for ref in part_refs]))
    live, count = live_mask(where_ref, near_ref, hidden_ref.shape[2])
    centred = (hidden_ref[0].astype(F32) - mean_row) * inv_std
    value = centred * scale_ref[2:3] + shift_ref[2:3] + act_ref[0].astype(F32)
    gate = sigmoid(value)
    features_ref[0] = (live * (value * gate)).astype(BF16)
    upstream = grad_ref[0].astype(F32) * live * (gate * (1.0 + value * (1.0 - gate)))
    slope_ref[0] = upstream
    put_sums(sums_ref, col_sum(upstream), col_sum(upstream * centred), count)


def norm_back(upstream, centred, live, inv_std, gain_row, back, count):
    return live * (inv_std * gain_row) * (upstream - back[0:1] / count - centred * (back[1:2] / count))


def backward_kernel(norm_at, with_skip, ways, where_ref, *refs):
    upstream_ref, hidden_ref, lower_ref, act_ref, near_ref, weight_ref, scale_ref, shift_ref = refs[:8]
    own_refs = refs[8 : 8 + ways]
    back_refs = refs[8 + ways : 8 + 2 * ways]
    below_refs = refs[8 + 2 * ways : 8 + 3 * ways]
    rest = refs[8 + 3 * ways :]
    skip_ref = rest[0] if with_skip else None
    next_ref, sums_ref, keep_ref, send_ref, grad_ref = rest[-5:]
    mean_row, inv_std, count = moments(tree_sum([ref[0] for ref in own_refs]))
    back = tree_sum([ref[0] for ref in back_refs])
    live, own_count = live_mask(where_ref, near_ref, hidden_ref.shape[2])
    centred = (hidden_ref[0].astype(F32) - mean_row) * inv_std
    rows_grad = norm_back(
        upstream_ref[0], centred, live, inv_std, scale_ref[norm_at : norm_at + 1], back, count
    ).astype(BF16)

    @pl.when(pl.program_id(0) == 0)
    def _():
        grad_ref[...] = jnp.zeros_like(grad_ref)

    channels = hidden_ref.shape[2]
    act_t = jnp.transpose(act_ref[0])
    below = mm_t(rows_grad, weight_ref[13])
    grad_ref[13 * channels : 14 * channels] += mm(act_t, rows_grad)
    for j in range(13):
        moved = jnp.concatenate(
            [mm(near_hits(where_ref, near_ref, k), rows_grad).astype(BF16) for k in (j, 26 - j)], axis=1
        )
        weight = jnp.concatenate([weight_ref[j], weight_ref[26 - j]], axis=1)
        below = below + mm_t(moved, weight)
        pair = mm(act_t, moved)
        grad_ref[j * channels : (j + 1) * channels] += pair[:, :channels]
        grad_ref[(26 - j) * channels : (27 - j) * channels] += pair[:, channels:]
    below = below.astype(BF16).astype(F32)
    if with_skip:
        below = below + skip_ref[0].astype(BF16).astype(F32)
    low_mean, low_std, _ = moments(tree_sum([ref[0] for ref in below_refs]))
    low_centred = (lower_ref[0] - low_mean) * low_std
    value = low_centred * scale_ref[norm_at - 1 : norm_at] + shift_ref[norm_at - 1 : norm_at]
    gate = sigmoid(value)
    upstream = below * live * (gate * (1.0 + value * (1.0 - gate)))
    next_ref[0] = upstream
    put_sums(sums_ref, col_sum(upstream), col_sum(upstream * low_centred), own_count)
    put_halves(where_ref, grad_ref, keep_ref, send_ref)


def put_halves(where_ref, grad_ref, keep_ref, send_ref):
    half = keep_ref.shape[0]
    core = where_ref[1]

    @pl.when(pl.program_id(0) == pl.num_programs(0) - 1)
    def _():
        keep_ref[...] = grad_ref[pl.ds(pl.multiple_of(core * half, 16), half)].astype(BF16)
        send_ref[...] = grad_ref[pl.ds(pl.multiple_of((1 - core) * half, 16), half)].astype(BF16)


def last_kernel(ways, where_ref, upstream_ref, hidden_ref, kids_ref, near_ref, scale_ref, *refs):
    own_refs, back_refs = refs[:ways], refs[ways : 2 * ways]
    rows_ref, keep_ref, send_ref, grad_ref = refs[2 * ways :]
    mean_row, inv_std, count = moments(tree_sum([ref[0] for ref in own_refs]))
    back = tree_sum([ref[0] for ref in back_refs])
    live, _ = live_mask(where_ref, near_ref, hidden_ref.shape[2])
    centred = (hidden_ref[0] - mean_row) * inv_std
    rows_grad = norm_back(
        upstream_ref[0], centred, live, inv_std, scale_ref[0:1], back, count
    ).astype(BF16)

    @pl.when(pl.program_id(0) == 0)
    def _():
        grad_ref[...] = jnp.zeros_like(grad_ref)

    rows_ref[0] = rows_grad
    grad_ref[: kids_ref.shape[1]] += mm(kids_ref[0], rows_grad)
    put_halves(where_ref, grad_ref, keep_ref, send_ref)


def input_kernel(where_ref, rows_ref, which_ref, down_ref, weight_ref, input_ref):
    pieces = mm_t(weight_ref[...], rows_ref[0]).astype(BF16)
    in_channels, fine_rows = input_ref.shape[1], input_ref.shape[2]
    _, first, last = parent_rows(down_ref, fine_rows)
    step = 256
    for at in range(0, fine_rows, step):
        full = mm_t(pieces, parent_hits(first, last, fine_rows, at, step))
        code = jnp.broadcast_to(which_ref[0, 0:1, at : at + step], (in_channels, step))
        out = jnp.zeros((in_channels, step), F32)
        for k in range(full.shape[0] // in_channels):
            out = out + jnp.where(code == float(k + 1), full[in_channels * k : in_channels * (k + 1)], 0.0)
        input_ref[0, :, at : at + step] = out.astype(BF16)


def as_f32(ref):
    return ref[...].astype(F32)


def split_kernel(sections, depths, parts, where_ref, *refs):
    pairs, outs = refs[: 2 * len(parts)], refs[2 * len(parts) :]
    section = where_ref[2]
    total = sum(parts)
    for j in range(sections):
        block = section ^ j
        base = 0
        for i, size in enumerate(parts):
            wide = depths * size
            rows = pl.ds(pl.multiple_of(block * wide, 16), wide)
            both = (pairs[2 * i][rows].astype(F32) + pairs[2 * i + 1][rows].astype(F32)).astype(BF16)
            for z in range(depths):
                outs[j][z * total + base : z * total + base + size] = both[z * size : (z + 1) * size]
            base += size


def spread_kernel(count, at, where_ref, *refs):
    sources, outs = refs[:-count], refs[-count:]
    place = where_ref[at]
    size = outs[0].shape[0]
    for j in range(count):
        rows = pl.ds(pl.multiple_of((place ^ j) * size, 16), size)
        outs[j][...] = tree_sum([ref[rows].astype(F32) for ref in sources]).astype(BF16)


def add_kernel(where_ref, *refs):
    refs[-1][...] = tree_sum([as_f32(ref) for ref in refs[:-1]]).astype(BF16)


def join_kernel(ways, where_ref, *refs):
    pieces, sums_refs, out_ref = refs[: -3 * ways - 1], refs[-3 * ways - 1 : -1], refs[-1]
    size = pieces[0].shape[0]
    for j, ref in enumerate(pieces):
        out_ref[pl.ds(pl.multiple_of((where_ref[3] ^ j) * size, 16), size)] = ref[...]
    rows = []
    for t in range(3):
        totals = tree_sum([ref[...] for ref in sums_refs[t * ways : (t + 1) * ways]])
        rows.append(jnp.sum(totals, axis=0)[0:2])
    exact = jnp.concatenate(rows + [jnp.zeros((2, rows[0].shape[1]), F32)], axis=0)
    high = exact.astype(BF16)
    low = (exact - high.astype(F32)).astype(BF16)
    out_ref[len(pieces) * size :] = jnp.concatenate([high, low], axis=0)


def gather_kernel(where_ref, *refs):
    pieces, (out_ref, sums_ref) = refs[:-2], refs[-2:]
    size = pieces[0].shape[0] - 16
    for j, ref in enumerate(pieces):
        out_ref[pl.ds(pl.multiple_of((where_ref[2] ^ j) * size, 16), size)] = ref[:size]
    tails = [ref[size:].astype(F32) for ref in pieces]
    sums_ref[...] = tree_sum([tail[:8] + tail[8:] for tail in tails])


def final_kernel(parts, where_ref, own_ref, other_ref, *outs):
    first_core = where_ref[1] == 0
    total = sum(parts)
    half = own_ref.shape[0]
    blocks = half // total
    for core in range(2):
        base = 0
        for size, out in zip(parts, outs):
            for t in range(blocks):
                start = (core * blocks + t) * size
                count = min(size, out.shape[0] - start)
                if count > 0:
                    rows = slice(t * total + base, t * total + base + count)
                    mine, theirs = own_ref[rows], other_ref[rows]
                    pick = first_core if core == 0 else jnp.logical_not(first_core)
                    out[start : start + count] = jnp.where(pick, mine, theirs).astype(F32)
            base += size


def whole(array):
    return pl.BlockSpec(array.shape, lambda b, where: (0,) * array.ndim)


def per_micro(array, picked):
    block = (1,) + array.shape[1:]
    rest = (0,) * (array.ndim - 1)
    if picked:
        return pl.BlockSpec(block, lambda b, where: (where[0] + b,) + rest)
    return pl.BlockSpec(block, lambda b, where: (b,) + rest)


def call(kernel, steps, where, operands, kinds, outs, out_kinds, scratch=()):
    def spec(array, kind):
        if kind == "all":
            return whole(array)
        return per_micro(array, kind == "pick")

    return pl.pallas_call(
        kernel,
        grid_spec=pltpu.PrefetchScalarGridSpec(
            num_scalar_prefetch=1,
            grid=(steps,),
            in_specs=[spec(a, k) for a, k in zip(operands, kinds)],
            out_specs=[spec(a, k) for a, k in zip(outs, out_kinds)],
            scratch_shapes=list(scratch),
        ),
        out_shape=outs,
        compiler_params=pltpu.CompilerParams(
            vmem_limit_bytes=VMEM_BYTES, dimension_semantics=("arbitrary",)
        ),
    )(where, *operands)


def simple(kernel, where, operands, outs, cost=None):
    return pl.pallas_call(
        kernel,
        in_specs=[pl.BlockSpec(memory_space=pltpu.SMEM)] + [pl.BlockSpec(memory_space=pltpu.VMEM)] * len(operands),
        out_specs=[pl.BlockSpec(memory_space=pltpu.VMEM)] * len(outs),
        out_shape=outs,
        compiler_params=pltpu.CompilerParams(vmem_limit_bytes=VMEM_BYTES),
    )(where, *operands)


def swapped(value, axis, step):
    count = lax.axis_size(axis)
    return lax.ppermute(value, axis, [(i, i ^ step) for i in range(count)])


def bucket_sums(value, axis):
    count = lax.axis_size(axis)
    value = value + lax.ppermute(value, axis, [(i, i ^ 1) for i in range(count)])
    return [value] + [
        lax.ppermute(value, axis, [(i, i ^ step) for i in range(count)])
        for step in range(2, count, 2)
    ]


def local(
    voxel_feats, down_map, neighbours, w_down, w_first, w_second, bn_scale, bn_shift, out_grad
):
    sections = lax.axis_size("section")
    mine = voxel_feats.shape[0] // sections
    voxel_feats = jnp.swapaxes(voxel_feats, 1, 2)
    neighbours = jnp.swapaxes(neighbours, 0, 1)
    section, bucket = lax.axis_index("section"), lax.axis_index("dp")
    depths = lax.axis_size("dp") // 2
    where = jnp.stack([section * mine, bucket % 2, section, bucket // 2]).astype(jnp.int32)
    in_channels, fine_rows = voxel_feats.shape[1:]
    coarse_rows = neighbours.shape[2]
    channels = w_first.shape[2]
    offsets = down_map.shape[1]
    wide = offsets * in_channels
    flat_down = w_down.reshape(wide, channels)
    shape = jax.ShapeDtypeStruct
    rows_f32 = shape((mine, coarse_rows, channels), F32)
    rows_bf16 = shape((mine, coarse_rows, channels), BF16)
    sums = shape((mine, 8, channels), F32)

    hidden_zero, part_zero, kids, which = call(
        down_kernel, mine, where,
        [voxel_feats, down_map, neighbours, flat_down],
        ["pick", "pick", "all", "all"],
        [rows_f32, sums, shape((mine, wide, coarse_rows), BF16), shape((mine, 8, fine_rows), F32)],
        ["own"] * 4,
        [pltpu.VMEM((wide, fine_rows), BF16), pltpu.VMEM((fine_rows, coarse_rows), BF16)],
    )
    stats_zero = bucket_sums(part_zero, "dp")
    ways = len(stats_zero)
    act_zero, hidden_one, part_one = call(
        functools.partial(forward_kernel, 0, False), mine, where,
        [hidden_zero, neighbours, w_first, bn_scale, bn_shift] + stats_zero,
        ["own", "all", "all", "all", "all"] + ["own"] * ways,
        [rows_bf16, rows_f32, sums], ["own"] * 3,
    )
    stats_one = bucket_sums(part_one, "dp")
    act_one, hidden_two, part_two = call(
        functools.partial(forward_kernel, 1, True), mine, where,
        [hidden_one, neighbours, w_second, bn_scale, bn_shift] + stats_one,
        ["own", "all", "all", "all", "all"] + ["own"] * ways,
        [rows_bf16, rows_bf16, sums], ["own"] * 3,
    )
    stats_two = bucket_sums(part_two, "dp")
    features, up_two, back_part = call(
        output_kernel, mine, where,
        [hidden_two, act_zero, out_grad, neighbours, bn_scale, bn_shift] + stats_two,
        ["own", "own", "pick", "all", "all", "all"] + ["own"] * ways,
        [rows_bf16, rows_f32, sums], ["own"] * 3,
    )
    back_two = bucket_sums(back_part, "dp")

    def part_rows(rows):
        return -(-rows // (2 * sections * depths * 16)) * 16

    conv_rows = w_first.shape[0] * channels
    parts = [part_rows(conv_rows), part_rows(conv_rows), part_rows(wide)]

    def halves(size):
        return shape((sections * depths * size, channels), BF16)

    def accumulator(size):
        return [pltpu.VMEM((2 * sections * depths * size, channels), F32)]

    up_one, back_part, keep_second, send_second = call(
        functools.partial(backward_kernel, 2, False, ways), mine, where,
        [up_two, hidden_two, hidden_one, act_one, neighbours, w_second, bn_scale, bn_shift]
        + stats_two + back_two + stats_one,
        ["own"] * 4 + ["all"] * 4 + ["own"] * (3 * ways),
        [rows_f32, sums, halves(parts[0]), halves(parts[0])], ["own", "own", "all", "all"],
        accumulator(parts[0]),
    )
    back_one = bucket_sums(back_part, "dp")
    got_second = swapped(send_second, "dp", 1)
    up_zero, back_part, keep_first, send_first = call(
        functools.partial(backward_kernel, 1, True, ways), mine, where,
        [up_one, hidden_one, hidden_zero, act_zero, neighbours, w_first, bn_scale, bn_shift]
        + stats_one + back_one + stats_zero + [up_two],
        ["own"] * 4 + ["all"] * 4 + ["own"] * (3 * ways + 1),
        [rows_f32, sums, halves(parts[1]), halves(parts[1])], ["own", "own", "all", "all"],
        accumulator(parts[1]),
    )
    back_zero = bucket_sums(back_part, "dp")
    got_first = swapped(send_first, "dp", 1)
    rows_zero, keep_down, send_down = call(
        functools.partial(last_kernel, ways), mine, where,
        [up_zero, hidden_zero, kids, neighbours, bn_scale] + stats_zero + back_zero,
        ["own"] * 3 + ["all"] * 2 + ["own"] * (2 * ways),
        [rows_bf16, halves(parts[2]), halves(parts[2])], ["own", "all", "all"],
        accumulator(parts[2]),
    )
    got_down = swapped(send_down, "dp", 1)
    total = sum(parts)
    sections_out = simple(
        functools.partial(split_kernel, sections, depths, parts), where,
        [keep_second, got_second, keep_first, got_first, keep_down, got_down],
        [shape((depths * total, channels), BF16)] * sections,
    )
    arrived = [sections_out[0]] + [swapped(sections_out[j], "section", j) for j in range(1, sections)]
    (input_grad,) = call(
        input_kernel, mine, where,
        [rows_zero, which, down_map, flat_down],
        ["own", "own", "pick", "all"],
        [shape((mine, in_channels, fine_rows), BF16)], ["own"],
    )
    depth_out = simple(
        functools.partial(spread_kernel, depths, 3), where, arrived,
        [shape((total, channels), BF16)] * depths,
    )
    arrived = [depth_out[0]] + [swapped(depth_out[j], "dp", 2 * j) for j in range(1, depths)]
    (summed,) = simple(add_kernel, where, arrived, [shape((total, channels), BF16)])
    arrived = [summed] + [swapped(summed, "dp", 2 * j) for j in range(1, depths)]
    (joined,) = simple(
        functools.partial(join_kernel, ways), where, arrived + back_zero + back_one + back_two,
        [shape((depths * total + 16, channels), BF16)],
    )
    arrived = [joined] + [swapped(joined, "section", j) for j in range(1, sections)]
    half, norm_sums = simple(
        gather_kernel, where, arrived,
        [shape((sections * depths * total, channels), BF16), shape((8, channels), F32)],
    )
    other = swapped(half, "dp", 1)
    grad_second, grad_first, grad_down = simple(
        functools.partial(final_kernel, parts), where, [half, other],
        [shape((conv_rows, channels), F32), shape((conv_rows, channels), F32), shape((wide, channels), F32)],
    )
    return (
        features,
        jnp.swapaxes(input_grad, 1, 2),
        grad_down.reshape(w_down.shape),
        grad_first.reshape(w_first.shape),
        grad_second.reshape(w_second.shape),
        norm_sums[1:6:2],
        norm_sums[0:6:2],
    )


def solution(mesh):
    in_specs = (
        P(None, "dp", None),
        P(None, None, "dp"),
        P(None, None, "dp"),
        P(),
        P(),
        P(),
        P(),
        P(),
        P(None, "dp", None),
    )
    out_specs = (P("section", "dp", None), P("section", "dp", None), P(), P(), P(), P(), P())
    return jax.shard_map(local, mesh=mesh, in_specs=in_specs, out_specs=out_specs, check_vma=False)
```

```python
import functools

import jax
import jax.numpy as jnp
from jax import lax
from jax.experimental import pallas as pl
from jax.experimental.pallas import tpu as pltpu
from jax.sharding import PartitionSpec as P

EPSILON = 1e-05
F32 = jnp.float32
BF16 = jnp.bfloat16
F8 = jnp.float8_e4m3fn
VMEM_BYTES = 48 << 20


def mm(left, right):
    return jnp.dot(left, right, preferred_element_type=F32)


def mm_t(left, right):
    return lax.dot_general(left, right, (((1,), (1,)), ((), ())), preferred_element_type=F32)


def hits(index_row, rows):
    places = lax.broadcasted_iota(jnp.int16, (rows, index_row.shape[1]), 0)
    return jnp.where(places == index_row, jnp.bfloat16(1), jnp.bfloat16(0)).astype(F8)


def power_for(largest):
    power = jnp.full_like(largest, 2.0**-60)
    for exponent in (64, 32, 16, 8, 4, 2, 1):
        raised = power * (2.0**exponent)
        power = jnp.where(largest * raised <= 224.0, raised, power)
    return power


def two_parts(scaled):
    high = scaled.astype(F8)
    low = (scaled - high.astype(F32)).astype(F8)
    return jnp.concatenate([high, low], axis=1)


def moved_rows(where_ref, near_ref, offset, pair):
    both = mm(near_hits(where_ref, near_ref, offset), pair)
    channels = pair.shape[1] // 2
    return (both[:, :channels] + both[:, channels:]).astype(BF16)


def near_row(where_ref, near_ref, offset):
    return near_ref[offset, pl.ds(where_ref[0] + pl.program_id(0), 1), :]


def near_hits(where_ref, near_ref, offset):
    row = near_row(where_ref, near_ref, offset)
    return hits(row.astype(jnp.int16), row.shape[1])


def live_mask(where_ref, near_ref, channels):
    rows = near_ref.shape[2]
    centre = near_row(where_ref, near_ref, 13)
    count = jnp.sum((centre < rows).astype(F32), axis=1, keepdims=True)
    places = lax.broadcasted_iota(jnp.int32, (rows, channels), 0).astype(F32)
    return (places < count).astype(F32), count


def tree_sum(parts):
    parts = list(parts)
    while len(parts) > 1:
        parts = [parts[i] + parts[i + 1] for i in range(0, len(parts), 2)]
    return parts[0]


def moments(totals):
    count = totals[2:3]
    mean_row = totals[0:1] / count
    inv_std = lax.rsqrt(totals[1:2] / count - mean_row * mean_row + EPSILON)
    return mean_row, inv_std, count


def sigmoid(values):
    return 1.0 / (1.0 + jnp.exp(-values))


def put_sums(out_ref, first, second, count):
    channels = first.shape[1]
    third = jnp.broadcast_to(count, (1, channels))
    out_ref[0] = jnp.concatenate(
        [first, second, third, jnp.zeros((5, channels), F32)], axis=0
    )


def col_sum(values):
    return jnp.sum(values, axis=0, keepdims=True)


def parent_rows(down_ref, fine_rows):
    table = down_ref[0]
    first = jnp.min(table, axis=0, keepdims=True)
    children = jnp.sum((table < fine_rows).astype(jnp.int32), axis=0, keepdims=True)
    return table, first, first + children


def parent_hits(first, last, fine_rows, at, size):
    places = lax.broadcasted_iota(jnp.int16, (size, first.shape[1]), 0) + jnp.int16(at)
    inside = (places >= first.astype(jnp.int16)) & (places < last.astype(jnp.int16))
    return jnp.where(inside, jnp.bfloat16(1), jnp.bfloat16(0))


def down_kernel(where_ref, feats_hbm, down_hbm, weight_ref, hidden_ref, sums_ref, kids_ref, which_ref, spread_ref, parent_ref, feats_all, down_all, arrivals):
    micro = pl.program_id(0)

    def copies(b):
        return (
            pltpu.make_async_copy(down_hbm.at[where_ref[0] + b], down_all.at[b], arrivals.at[b, 0]),
            pltpu.make_async_copy(feats_hbm.at[where_ref[0] + b], feats_all.at[b], arrivals.at[b, 1]),
        )

    @pl.when(micro == 0)
    def _():
        for b in range(feats_all.shape[0]):
            for copy in copies(b):
                copy.start()

    for copy in copies(micro):
        copy.wait()
    feats_ref, down_ref = feats_all.at[pl.ds(micro, 1)], down_all.at[pl.ds(micro, 1)]
    in_channels, fine_rows = feats_ref.shape[1], feats_ref.shape[2]
    offsets, coarse_rows = down_ref.shape[1], down_ref.shape[2]
    channels = weight_ref.shape[1]
    table, first, last = parent_rows(down_ref, fine_rows)
    rank = table - first
    numbers = lax.broadcasted_iota(jnp.int32, (offsets, coarse_rows), 0) + 1
    rows = [
        jnp.sum(jnp.where(rank == r, numbers, 0), axis=0, keepdims=True) for r in range(8)
    ]
    safe_first = jnp.where(first < fine_rows, first, 0)
    rows += [(safe_first // 16) * 16, safe_first % 16] + [jnp.zeros_like(first)] * 6
    lookup = jnp.concatenate(rows, axis=0).astype(F32).astype(BF16)
    step = 512
    for at in range(0, fine_rows, step):
        parent_ref[at : at + step] = parent_hits(first, last, fine_rows, at, step)
    found = mm_t(lookup, parent_ref[...])
    place = lax.broadcasted_iota(jnp.int32, (8, fine_rows), 1).astype(F32) - (found[8:9] + found[9:10])
    column = lax.broadcasted_iota(jnp.int32, (8, fine_rows), 0).astype(F32)
    which = jnp.sum(jnp.where(column == place, found[:8], 0.0), axis=0, keepdims=True)
    which_ref[0] = jnp.broadcast_to(which, (8, fine_rows))
    code = jnp.broadcast_to(which, (in_channels, fine_rows)).astype(BF16)
    feats = feats_ref[0]
    for k in range(offsets):
        spread_ref[in_channels * k : in_channels * (k + 1)] = jnp.where(
            code == jnp.bfloat16(k + 1), feats, jnp.zeros_like(feats)
        )
    kids = mm(spread_ref[...], parent_ref[...]).astype(BF16)
    kids_ref[0] = kids
    hidden = jnp.transpose(mm(jnp.transpose(weight_ref[...]), kids))
    hidden_ref[0] = hidden
    count = jnp.sum((last > first).astype(F32), axis=1, keepdims=True)
    put_sums(sums_ref, col_sum(hidden), col_sum(hidden * hidden), count)


def conv_all(where_ref, source, near_ref, weight_ref):
    values = source.astype(F32)
    largest = jnp.max(jnp.max(jnp.abs(values), axis=0, keepdims=True), axis=1, keepdims=True)
    power = power_for(largest)
    scaled = values * power
    pair = two_parts(scaled)
    out = None
    for group in ((0, 1), (2, 3), (4, 5), (6, 7), (8, 9), (10, 11), (12, 13)):
        offsets = [k for j in group for k in ((j, 26 - j) if j < 13 else (13,))]
        rows = [
            scaled.astype(BF16) if k == 13 else moved_rows(where_ref, near_ref, 26 - k, pair)
            for k in offsets
        ]
        weight = jnp.concatenate([weight_ref[k] for k in offsets], axis=0)
        term = mm(jnp.concatenate(rows, axis=1), weight)
        out = term if out is None else out + term
    return out * (1.0 / power)


def forward_kernel(norm_at, rounded, where_ref, hidden_ref, near_ref, weight_ref, scale_ref, shift_ref, *refs):
    part_refs, (act_ref, next_ref, sums_ref) = refs[:-3], refs[-3:]
    mean_row, inv_std, _ = moments(tree_sum([ref[0] for ref in part_refs]))
    live, count = live_mask(where_ref, near_ref, hidden_ref.shape[2])
    value = (hidden_ref[0] - mean_row) * inv_std * scale_ref[norm_at : norm_at + 1] + shift_ref[norm_at : norm_at + 1]
    act = (live * (value * sigmoid(value))).astype(BF16)
    act_ref[0] = act
    hidden = conv_all(where_ref, act, near_ref, weight_ref)
    if rounded:
        hidden = hidden.astype(BF16)
    next_ref[0] = hidden
    hidden = hidden.astype(F32)
    put_sums(sums_ref, col_sum(hidden), col_sum(hidden * hidden), count)


def output_kernel(where_ref, hidden_ref, act_ref, grad_ref, near_ref, scale_ref, shift_ref, *refs):
    part_refs, (features_ref, slope_ref, sums_ref) = refs[:-3], refs[-3:]
    mean_row, inv_std, _ = moments(tree_sum([ref[0] for ref in part_refs]))
    live, count = live_mask(where_ref, near_ref, hidden_ref.shape[2])
    centred = (hidden_ref[0].astype(F32) - mean_row) * inv_std
    value = centred * scale_ref[2:3] + shift_ref[2:3] + act_ref[0].astype(F32)
    gate = sigmoid(value)
    features_ref[0] = (live * (value * gate)).astype(BF16)
    upstream = grad_ref[0].astype(F32) * live * (gate * (1.0 + value * (1.0 - gate)))
    slope_ref[0] = upstream
    put_sums(sums_ref, col_sum(upstream), col_sum(upstream * centred), count)


def norm_back(upstream, centred, live, inv_std, gain_row, back, count):
    return live * (inv_std * gain_row) * (upstream - back[0:1] / count - centred * (back[1:2] / count))


def backward_kernel(norm_at, with_skip, ways, where_ref, *refs):
    upstream_ref, hidden_ref, lower_ref, act_ref, near_ref, weight_ref, scale_ref, shift_ref = refs[:8]
    own_refs = refs[8 : 8 + ways]
    back_refs = refs[8 + ways : 8 + 2 * ways]
    below_refs = refs[8 + 2 * ways : 8 + 3 * ways]
    rest = refs[8 + 3 * ways :]
    skip_ref = rest[0] if with_skip else None
    next_ref, sums_ref, keep_ref, send_ref, grad_ref = rest[-5:]
    mean_row, inv_std, count = moments(tree_sum([ref[0] for ref in own_refs]))
    back = tree_sum([ref[0] for ref in back_refs])
    live, own_count = live_mask(where_ref, near_ref, hidden_ref.shape[2])
    centred = (hidden_ref[0].astype(F32) - mean_row) * inv_std
    rows_grad = norm_back(
        upstream_ref[0], centred, live, inv_std, scale_ref[norm_at : norm_at + 1], back, count
    ).astype(BF16)

    @pl.when(pl.program_id(0) == 0)
    def _():
        grad_ref[...] = jnp.zeros_like(grad_ref)

    channels = hidden_ref.shape[2]
    act_t = jnp.transpose(act_ref[0])
    values = rows_grad.astype(F32)
    power = power_for(jnp.max(jnp.abs(values), axis=0, keepdims=True))
    undo = 1.0 / power
    undo_low = undo.astype(BF16)
    scaled = values * power
    pair = two_parts(scaled)
    below = None
    for group in ((0, 1), (2, 3), (4, 5), (6, 7), (8, 9), (10, 11), (12, 13)):
        offsets = [k for j in group for k in ((j, 26 - j) if j < 13 else (13,))]
        moved = jnp.concatenate(
            [
                scaled.astype(BF16) if k == 13 else moved_rows(where_ref, near_ref, k, pair)
                for k in offsets
            ],
            axis=1,
        )
        weight = jnp.concatenate([weight_ref[k] * undo_low for k in offsets], axis=1)
        term = mm_t(moved, weight)
        below = term if below is None else below + term
        products = mm(act_t, moved)
        for i, k in enumerate(offsets):
            grad_ref[k * channels : (k + 1) * channels] += (
                products[:, i * channels : (i + 1) * channels] * undo
            )
    below = below.astype(BF16).astype(F32)
    if with_skip:
        below = below + skip_ref[0].astype(BF16).astype(F32)
    low_mean, low_std, _ = moments(tree_sum([ref[0] for ref in below_refs]))
    low_centred = (lower_ref[0] - low_mean) * low_std
    value = low_centred * scale_ref[norm_at - 1 : norm_at] + shift_ref[norm_at - 1 : norm_at]
    gate = sigmoid(value)
    upstream = below * live * (gate * (1.0 + value * (1.0 - gate)))
    next_ref[0] = upstream
    put_sums(sums_ref, col_sum(upstream), col_sum(upstream * low_centred), own_count)
    put_halves(where_ref, grad_ref, keep_ref, send_ref)


def put_halves(where_ref, grad_ref, keep_ref, send_ref):
    half = keep_ref.shape[0]
    core = where_ref[1]

    @pl.when(pl.program_id(0) == pl.num_programs(0) - 1)
    def _():
        keep_ref[...] = grad_ref[pl.ds(pl.multiple_of(core * half, 16), half)].astype(BF16)
        send_ref[...] = grad_ref[pl.ds(pl.multiple_of((1 - core) * half, 16), half)].astype(BF16)


def last_kernel(ways, where_ref, upstream_ref, hidden_ref, kids_ref, near_ref, scale_ref, *refs):
    own_refs, back_refs = refs[:ways], refs[ways : 2 * ways]
    rows_ref, keep_ref, send_ref, grad_ref = refs[2 * ways :]
    mean_row, inv_std, count = moments(tree_sum([ref[0] for ref in own_refs]))
    back = tree_sum([ref[0] for ref in back_refs])
    live, _ = live_mask(where_ref, near_ref, hidden_ref.shape[2])
    centred = (hidden_ref[0] - mean_row) * inv_std
    rows_grad = norm_back(
        upstream_ref[0], centred, live, inv_std, scale_ref[0:1], back, count
    ).astype(BF16)

    @pl.when(pl.program_id(0) == 0)
    def _():
        grad_ref[...] = jnp.zeros_like(grad_ref)

    rows_ref[0] = rows_grad
    grad_ref[: kids_ref.shape[1]] += mm(kids_ref[0], rows_grad)
    put_halves(where_ref, grad_ref, keep_ref, send_ref)


def input_kernel(where_ref, rows_ref, which_ref, down_ref, weight_ref, input_ref):
    pieces = mm_t(weight_ref[...], rows_ref[0]).astype(BF16)
    in_channels, fine_rows = input_ref.shape[1], input_ref.shape[2]
    _, first, last = parent_rows(down_ref, fine_rows)
    step = 256
    for at in range(0, fine_rows, step):
        full = mm_t(pieces, parent_hits(first, last, fine_rows, at, step))
        code = jnp.broadcast_to(which_ref[0, 0:1, at : at + step], (in_channels, step))
        out = jnp.zeros((in_channels, step), F32)
        for k in range(full.shape[0] // in_channels):
            out = out + jnp.where(code == float(k + 1), full[in_channels * k : in_channels * (k + 1)], 0.0)
        input_ref[0, :, at : at + step] = out.astype(BF16)


def as_f32(ref):
    return ref[...].astype(F32)


def split_kernel(sections, depths, parts, where_ref, *refs):
    pairs, outs = refs[: 2 * len(parts)], refs[2 * len(parts) :]
    section = where_ref[2]
    total = sum(parts)
    for j in range(sections):
        block = section ^ j
        base = 0
        for i, size in enumerate(parts):
            wide = depths * size
            rows = pl.ds(pl.multiple_of(block * wide, 16), wide)
            both = (pairs[2 * i][rows].astype(F32) + pairs[2 * i + 1][rows].astype(F32)).astype(BF16)
            for z in range(depths):
                outs[j][z * total + base : z * total + base + size] = both[z * size : (z + 1) * size]
            base += size


def spread_kernel(depths, sources, where_ref, *refs):
    blocks, halves, outs = refs[:sources], refs[sources : sources + 2], refs[sources + 2 :]
    place = where_ref[3]
    small = halves[0].shape[0] // depths
    size = outs[0].shape[0] - small
    for j in range(depths):
        rows = pl.ds(pl.multiple_of((place ^ j) * size, 16), size)
        outs[j][:size] = tree_sum([ref[rows].astype(F32) for ref in blocks]).astype(BF16)
        rows = pl.ds(pl.multiple_of((place ^ j) * small, 16), small)
        outs[j][size:] = (halves[0][rows].astype(F32) + halves[1][rows].astype(F32)).astype(BF16)


def add_kernel(where_ref, *refs):
    refs[-1][...] = tree_sum([as_f32(ref) for ref in refs[:-1]]).astype(BF16)


def join_kernel(ways, small, where_ref, *refs):
    pieces, sums_refs, out_ref = refs[: -3 * ways - 1], refs[-3 * ways - 1 : -1], refs[-1]
    size = pieces[0].shape[0] - small
    base = len(pieces) * size
    for j, ref in enumerate(pieces):
        place = where_ref[3] ^ j
        out_ref[pl.ds(pl.multiple_of(place * size, 16), size)] = ref[:size]
        out_ref[pl.ds(pl.multiple_of(base + place * small, 16), small)] = ref[size:]
    rows = []
    for t in range(3):
        totals = tree_sum([ref[...] for ref in sums_refs[t * ways : (t + 1) * ways]])
        rows.append(jnp.sum(totals, axis=0)[0:2])
    exact = jnp.concatenate(rows + [jnp.zeros((2, rows[0].shape[1]), F32)], axis=0)
    high = exact.astype(BF16)
    low = (exact - high.astype(F32)).astype(BF16)
    out_ref[base + len(pieces) * small :] = jnp.concatenate([high, low], axis=0)


def gather_kernel(size, where_ref, *refs):
    pieces, (out_ref, scale_ref, shift_ref) = refs[:-3], refs[-3:]
    for j, ref in enumerate(pieces):
        out_ref[pl.ds(pl.multiple_of((where_ref[2] ^ j) * size, 16), size)] = ref[:size]
    tails = [ref[size:].astype(F32) for ref in pieces]
    middle = tails[0].shape[0] - 16
    out_ref[len(pieces) * size :] = tree_sum([tail[:middle] for tail in tails]).astype(BF16)
    sums = tree_sum([tail[middle : middle + 8] + tail[middle + 8 :] for tail in tails])
    shift_ref[...] = jnp.concatenate([sums[2 * t : 2 * t + 1] for t in range(3)], axis=0)
    scale_ref[...] = jnp.concatenate([sums[2 * t + 1 : 2 * t + 2] for t in range(3)], axis=0)


def final_kernel(parts, blocks, where_ref, own_ref, other_ref, *outs):
    first_core = where_ref[1] == 0
    total = sum(parts)
    small = own_ref.shape[0] - blocks * total
    for core in range(2):
        pick = first_core if core == 0 else jnp.logical_not(first_core)

        def put(out, start, at, size):
            count = min(size, out.shape[0] - start)
            if count > 0:
                rows = slice(at, at + count)
                out[start : start + count] = jnp.where(pick, own_ref[rows], other_ref[rows]).astype(F32)

        base = 0
        for size, out in zip(parts, outs):
            for t in range(blocks):
                put(out, (core * blocks + t) * size, t * total + base, size)
            base += size
        put(outs[-1], core * small, blocks * total, small)


def whole(array):
    return pl.BlockSpec(array.shape, lambda b, where: (0,) * array.ndim)


def per_micro(array, picked):
    block = (1,) + array.shape[1:]
    rest = (0,) * (array.ndim - 1)
    if picked:
        return pl.BlockSpec(block, lambda b, where: (where[0] + b,) + rest)
    return pl.BlockSpec(block, lambda b, where: (b,) + rest)


def call(kernel, steps, where, operands, kinds, outs, out_kinds, scratch=()):
    def spec(array, kind):
        if kind == "hbm":
            return pl.BlockSpec(memory_space=pltpu.HBM)
        if kind == "all":
            return whole(array)
        return per_micro(array, kind == "pick")

    return pl.pallas_call(
        kernel,
        grid_spec=pltpu.PrefetchScalarGridSpec(
            num_scalar_prefetch=1,
            grid=(steps,),
            in_specs=[spec(a, k) for a, k in zip(operands, kinds)],
            out_specs=[spec(a, k) for a, k in zip(outs, out_kinds)],
            scratch_shapes=list(scratch),
        ),
        out_shape=outs,
        compiler_params=pltpu.CompilerParams(
            vmem_limit_bytes=VMEM_BYTES, dimension_semantics=("arbitrary",)
        ),
    )(where, *operands)


def simple(kernel, where, operands, outs, cost=None):
    return pl.pallas_call(
        kernel,
        in_specs=[pl.BlockSpec(memory_space=pltpu.SMEM)] + [pl.BlockSpec(memory_space=pltpu.VMEM)] * len(operands),
        out_specs=[pl.BlockSpec(memory_space=pltpu.VMEM)] * len(outs),
        out_shape=outs,
        compiler_params=pltpu.CompilerParams(vmem_limit_bytes=VMEM_BYTES),
    )(where, *operands)


def swapped(value, axis, step):
    count = lax.axis_size(axis)
    return lax.ppermute(value, axis, [(i, i ^ step) for i in range(count)])


def bucket_sums(value, axis):
    count = lax.axis_size(axis)
    value = value + lax.ppermute(value, axis, [(i, i ^ 1) for i in range(count)])
    return [value] + [
        lax.ppermute(value, axis, [(i, i ^ step) for i in range(count)])
        for step in range(2, count, 2)
    ]


def local(
    voxel_feats, down_map, neighbours, w_down, w_first, w_second, bn_scale, bn_shift, out_grad
):
    sections = lax.axis_size("section")
    mine = voxel_feats.shape[0] // sections
    voxel_feats = jnp.swapaxes(voxel_feats, 1, 2)
    neighbours = jnp.swapaxes(neighbours, 0, 1)
    section, bucket = lax.axis_index("section"), lax.axis_index("dp")
    depths = lax.axis_size("dp") // 2
    where = jnp.stack([section * mine, bucket % 2, section, bucket // 2]).astype(jnp.int32)
    in_channels, fine_rows = voxel_feats.shape[1:]
    coarse_rows = neighbours.shape[2]
    channels = w_first.shape[2]
    offsets = down_map.shape[1]
    wide = offsets * in_channels
    flat_down = w_down.reshape(wide, channels)
    shape = jax.ShapeDtypeStruct
    rows_f32 = shape((mine, coarse_rows, channels), F32)
    rows_bf16 = shape((mine, coarse_rows, channels), BF16)
    sums = shape((mine, 8, channels), F32)

    hidden_zero, part_zero, kids, which = call(
        down_kernel, mine, where,
        [voxel_feats, down_map, flat_down],
        ["hbm", "hbm", "all"],
        [rows_f32, sums, shape((mine, wide, coarse_rows), BF16), shape((mine, 8, fine_rows), F32)],
        ["own"] * 4,
        [
            pltpu.VMEM((wide, fine_rows), BF16),
            pltpu.VMEM((fine_rows, coarse_rows), BF16),
            pltpu.VMEM((mine, in_channels, fine_rows), BF16),
            pltpu.VMEM((mine, offsets, coarse_rows), jnp.int32),
            pltpu.SemaphoreType.DMA((mine, 2)),
        ],
    )
    stats_zero = bucket_sums(part_zero, "dp")
    ways = len(stats_zero)
    act_zero, hidden_one, part_one = call(
        functools.partial(forward_kernel, 0, False), mine, where,
        [hidden_zero, neighbours, w_first, bn_scale, bn_shift] + stats_zero,
        ["own", "all", "all", "all", "all"] + ["own"] * ways,
        [rows_bf16, rows_f32, sums], ["own"] * 3,
    )
    stats_one = bucket_sums(part_one, "dp")
    act_one, hidden_two, part_two = call(
        functools.partial(forward_kernel, 1, True), mine, where,
        [hidden_one, neighbours, w_second, bn_scale, bn_shift] + stats_one,
        ["own", "all", "all", "all", "all"] + ["own"] * ways,
        [rows_bf16, rows_bf16, sums], ["own"] * 3,
    )
    stats_two = bucket_sums(part_two, "dp")
    features, up_two, back_part = call(
        output_kernel, mine, where,
        [hidden_two, act_zero, out_grad, neighbours, bn_scale, bn_shift] + stats_two,
        ["own", "own", "pick", "all", "all", "all"] + ["own"] * ways,
        [rows_bf16, rows_f32, sums], ["own"] * 3,
    )
    back_two = bucket_sums(back_part, "dp")

    def part_rows(rows, pieces):
        return -(-rows // (pieces * 16)) * 16

    blocks = sections * depths
    conv_rows = w_first.shape[0] * channels
    parts = [part_rows(conv_rows, 2 * blocks)] * 2
    small = part_rows(wide, 2 * depths)

    def half_shape(rows):
        return shape((rows, channels), BF16)

    def accumulator(rows):
        return [pltpu.VMEM((2 * rows, channels), F32)]

    half = half_shape(blocks * parts[0])
    up_one, back_part, keep_second, send_second = call(
        functools.partial(backward_kernel, 2, False, ways), mine, where,
        [up_two, hidden_two, hidden_one, act_one, neighbours, w_second, bn_scale, bn_shift]
        + stats_two + back_two + stats_one,
        ["own"] * 4 + ["all"] * 4 + ["own"] * (3 * ways),
        [rows_f32, sums, half, half], ["own", "own", "all", "all"],
        accumulator(half.shape[0]),
    )
    back_one = bucket_sums(back_part, "dp")
    got_second = swapped(send_second, "dp", 1)
    up_zero, back_part, keep_first, send_first = call(
        functools.partial(backward_kernel, 1, True, ways), mine, where,
        [up_one, hidden_one, hidden_zero, act_zero, neighbours, w_first, bn_scale, bn_shift]
        + stats_one + back_one + stats_zero + [up_two],
        ["own"] * 4 + ["all"] * 4 + ["own"] * (3 * ways + 1),
        [rows_f32, sums, half, half], ["own", "own", "all", "all"],
        accumulator(half.shape[0]),
    )
    got_first = swapped(send_first, "dp", 1)
    total = sum(parts)
    section_out = simple(
        functools.partial(split_kernel, sections, depths, parts), where,
        [keep_second, got_second, keep_first, got_first],
        [half_shape(depths * total)] * sections,
    )
    arrived = [section_out[0]] + [swapped(section_out[j], "section", j) for j in range(1, sections)]
    back_zero = bucket_sums(back_part, "dp")
    small_half = half_shape(depths * small)
    rows_zero, keep_down, send_down = call(
        functools.partial(last_kernel, ways), mine, where,
        [up_zero, hidden_zero, kids, neighbours, bn_scale] + stats_zero + back_zero,
        ["own"] * 3 + ["all"] * 2 + ["own"] * (2 * ways),
        [rows_bf16, small_half, small_half], ["own", "all", "all"],
        accumulator(small_half.shape[0]),
    )
    got_down = swapped(send_down, "dp", 1)
    (input_grad,) = call(
        input_kernel, mine, where,
        [rows_zero, which, down_map, flat_down],
        ["own", "own", "pick", "all"],
        [shape((mine, in_channels, fine_rows), BF16)], ["own"],
    )
    depth_out = simple(
        functools.partial(spread_kernel, depths, sections), where, arrived + [keep_down, got_down],
        [half_shape(total + small)] * depths,
    )
    arrived = [depth_out[0]] + [swapped(depth_out[j], "dp", 2 * j) for j in range(1, depths)]
    (summed,) = simple(add_kernel, where, arrived, [half_shape(total + small)])
    arrived = [summed] + [swapped(summed, "dp", 2 * j) for j in range(1, depths)]
    (joined,) = simple(
        functools.partial(join_kernel, ways, small), where, arrived + back_zero + back_one + back_two,
        [half_shape(depths * (total + small) + 16)],
    )
    arrived = [joined] + [swapped(joined, "section", j) for j in range(1, sections)]
    norms = shape(bn_scale.shape, F32)
    gathered, grad_scale, grad_shift = simple(
        functools.partial(gather_kernel, depths * total), where, arrived,
        [half_shape(blocks * total + depths * small), norms, norms],
    )
    other = swapped(gathered, "dp", 1)
    grad_second, grad_first, grad_down = simple(
        functools.partial(final_kernel, parts, blocks), where, [gathered, other],
        [shape((conv_rows, channels), F32), shape((conv_rows, channels), F32), shape((wide, channels), F32)],
    )
    return (
        features,
        jnp.swapaxes(input_grad, 1, 2),
        grad_down.reshape(w_down.shape),
        grad_first.reshape(w_first.shape),
        grad_second.reshape(w_second.shape),
        grad_scale,
        grad_shift,
    )


def solution(mesh):
    in_specs = (
        P(None, "dp", None),
        P(None, None, "dp"),
        P(None, None, "dp"),
        P(),
        P(),
        P(),
        P(),
        P(),
        P(None, "dp", None),
    )
    out_specs = (P("section", "dp", None), P("section", "dp", None), P(), P(), P(), P(), P())
    return jax.shard_map(local, mesh=mesh, in_specs=in_specs, out_specs=out_specs, check_vma=False)
```

```python
import functools

import jax
import jax.numpy as jnp
from jax import lax
from jax.experimental import pallas as pl
from jax.experimental.pallas import tpu as pltpu
from jax.sharding import PartitionSpec as P

EPSILON = 1e-05
F32 = jnp.float32
BF16 = jnp.bfloat16
F8 = jnp.float8_e4m3fn
VMEM_BYTES = 40 << 20
GROUPS = ((0, 1), (2, 3), (4, 5), (6, 7), (8, 9), (10, 11), (12, 13))


def mm(left, right):
    return jnp.dot(left, right, preferred_element_type=F32)


def mm_t(left, right):
    return lax.dot_general(left, right, (((1,), (1,)), ((), ())), preferred_element_type=F32)


def col_sum(values):
    return jnp.sum(values, axis=0, keepdims=True)


def sigmoid(values):
    return 1.0 / (1.0 + jnp.exp(-values))


def tree_sum(parts):
    parts = list(parts)
    while len(parts) > 1:
        parts = [parts[i] + parts[i + 1] for i in range(0, len(parts), 2)]
    return parts[0]


def sum_refs(refs):
    return tree_sum([ref[...].astype(F32) for ref in refs])


def hits(index_row, rows):
    places = lax.broadcasted_iota(jnp.int16, (rows, index_row.shape[1]), 0)
    return jnp.where(places == index_row, jnp.bfloat16(1), jnp.bfloat16(0)).astype(F8)


def near_row(where_ref, near_ref, micro, offset):
    return near_ref[offset, pl.ds(where_ref[0] + micro, 1), :]


def live_mask(where_ref, near_ref, micro, channels):
    rows = near_ref.shape[2]
    centre = near_row(where_ref, near_ref, micro, 13)
    count = jnp.sum((centre < rows).astype(F32), axis=1, keepdims=True)
    places = lax.broadcasted_iota(jnp.int32, (rows, channels), 0).astype(F32)
    return (places < count).astype(F32), count


def power_for(largest):
    power = jnp.full_like(largest, 2.0**-60)
    for exponent in (64, 32, 16, 8, 4, 2, 1):
        raised = power * (2.0**exponent)
        power = jnp.where(largest * raised <= 224.0, raised, power)
    return power


def two_parts(scaled):
    high = scaled.astype(F8)
    low = (scaled - high.astype(F32)).astype(F8)
    return jnp.concatenate([high, low], axis=1)


def moved_rows(where_ref, near_ref, micro, offset, pair):
    row = near_row(where_ref, near_ref, micro, offset)
    both = mm(hits(row.astype(jnp.int16), row.shape[1]), pair)
    channels = pair.shape[1] // 2
    return (both[:, :channels] + both[:, channels:]).astype(BF16)


def group_offsets(group):
    return [k for j in group for k in ((j, 26 - j) if j < 13 else (13,))]


def moments(totals, micro):
    count = totals[4 * micro + 2 : 4 * micro + 3]
    mean_row = totals[4 * micro : 4 * micro + 1] / count
    square = totals[4 * micro + 1 : 4 * micro + 2] / count
    return mean_row, lax.rsqrt(square - mean_row * mean_row + EPSILON), count


def put_sums(out_ref, micro, first, second, count):
    third = jnp.broadcast_to(count, first.shape)
    rows = jnp.concatenate([first, second, third, jnp.zeros_like(first)], axis=0)
    out_ref[4 * micro : 4 * micro + 4] = rows


def norm_back(upstream, centred, live, inv_std, gain_row, back, micro, count):
    first = back[4 * micro : 4 * micro + 1] / count
    second = back[4 * micro + 1 : 4 * micro + 2] / count
    return live * (inv_std * gain_row) * (upstream - first - centred * second)


def parent_rows(table, fine_rows):
    first = jnp.min(table, axis=0, keepdims=True)
    children = jnp.sum((table < fine_rows).astype(jnp.int32), axis=0, keepdims=True)
    return first, first + children


def parent_hits(first, last, at, size):
    places = lax.broadcasted_iota(jnp.int16, (size, first.shape[1]), 0) + jnp.int16(at)
    inside = (places >= first.astype(jnp.int16)) & (places < last.astype(jnp.int16))
    return jnp.where(inside, jnp.bfloat16(1), jnp.bfloat16(0))


def down_kernel(
    where_ref, feats_hbm, down_hbm, weight_hbm,
    hidden_ref, sums_ref, kids_ref, which_ref,
    spread_ref, parent_ref, feats_all, down_all, weight_ref, arrivals,
):
    mine, in_channels, fine_rows = feats_all.shape
    offsets, coarse_rows = down_all.shape[1:]
    weight_copy = pltpu.make_async_copy(weight_hbm, weight_ref, arrivals.at[0, 2])
    copies = []
    for b in range(mine):
        copies.append(pltpu.make_async_copy(down_hbm.at[where_ref[0] + b], down_all.at[b], arrivals.at[b, 0]))
        copies.append(pltpu.make_async_copy(feats_hbm.at[where_ref[0] + b], feats_all.at[b], arrivals.at[b, 1]))
        copies[-2].start()
        copies[-1].start()
        if b == 0:
            weight_copy.start()
    for b in range(mine):
        copies[2 * b].wait()
        table = down_all[b]
        first, last = parent_rows(table, fine_rows)
        rank = table - first
        numbers = lax.broadcasted_iota(jnp.int32, (offsets, coarse_rows), 0) + 1
        rows = [jnp.sum(jnp.where(rank == r, numbers, 0), axis=0, keepdims=True) for r in range(8)]
        safe_first = jnp.where(first < fine_rows, first, 0)
        rows += [(safe_first // 16) * 16, safe_first % 16] + [jnp.zeros_like(first)] * 6
        lookup = jnp.concatenate(rows, axis=0).astype(F32).astype(BF16)
        step = 512
        for at in range(0, fine_rows, step):
            parent_ref[at : at + step] = parent_hits(first, last, at, step)
        found = mm_t(lookup, parent_ref[...])
        place = lax.broadcasted_iota(jnp.int32, (8, fine_rows), 1).astype(F32) - (found[8:9] + found[9:10])
        column = lax.broadcasted_iota(jnp.int32, (8, fine_rows), 0).astype(F32)
        which = jnp.sum(jnp.where(column == place, found[:8], 0.0), axis=0, keepdims=True)
        which_ref[b] = jnp.broadcast_to(which, (8, fine_rows))
        code = jnp.broadcast_to(which, (in_channels, fine_rows)).astype(BF16)
        copies[2 * b + 1].wait()
        feats = feats_all[b]
        for k in range(offsets):
            spread_ref[in_channels * k : in_channels * (k + 1)] = jnp.where(
                code == jnp.bfloat16(k + 1), feats, jnp.zeros_like(feats)
            )
        kids = mm(spread_ref[...], parent_ref[...]).astype(BF16)
        kids_ref[b] = kids
        if b == 0:
            weight_copy.wait()
        hidden = jnp.transpose(mm(jnp.transpose(weight_ref[...]), kids))
        hidden_ref[b] = hidden
        count = jnp.sum((last > first).astype(F32), axis=1, keepdims=True)
        put_sums(sums_ref, b, col_sum(hidden), col_sum(hidden * hidden), count)


def conv_all(where_ref, source, near_ref, micro, weight_ref):
    values = source.astype(F32)
    largest = jnp.max(jnp.max(jnp.abs(values), axis=0, keepdims=True), axis=1, keepdims=True)
    power = power_for(largest)
    scaled = values * power
    pair = two_parts(scaled)
    out = None
    for group in GROUPS:
        offsets = group_offsets(group)
        rows = [
            scaled.astype(BF16) if k == 13 else moved_rows(where_ref, near_ref, micro, 26 - k, pair)
            for k in offsets
        ]
        weight = jnp.concatenate([weight_ref[k] for k in offsets], axis=0)
        term = mm(jnp.concatenate(rows, axis=1), weight)
        out = term if out is None else out + term
    return out * (1.0 / power)


def forward_kernel(norm_at, rounded, where_ref, hidden_ref, near_ref, weight_ref, scale_ref, shift_ref, *refs):
    part_refs, (act_ref, next_ref, sums_ref) = refs[:-3], refs[-3:]
    totals = sum_refs(part_refs)
    for b in range(hidden_ref.shape[0]):
        mean_row, inv_std, _ = moments(totals, b)
        live, count = live_mask(where_ref, near_ref, b, hidden_ref.shape[2])
        centred = (hidden_ref[b] - mean_row) * inv_std
        value = centred * scale_ref[norm_at : norm_at + 1] + shift_ref[norm_at : norm_at + 1]
        act = (live * (value * sigmoid(value))).astype(BF16)
        act_ref[b] = act
        hidden = conv_all(where_ref, act, near_ref, b, weight_ref)
        if rounded:
            hidden = hidden.astype(BF16)
        next_ref[b] = hidden
        hidden = hidden.astype(F32)
        put_sums(sums_ref, b, col_sum(hidden), col_sum(hidden * hidden), count)


def output_kernel(where_ref, hidden_ref, act_ref, grad_ref, near_ref, scale_ref, shift_ref, *refs):
    part_refs, (features_ref, slope_ref, sums_ref) = refs[:-3], refs[-3:]
    totals = sum_refs(part_refs)
    for b in range(hidden_ref.shape[0]):
        mean_row, inv_std, _ = moments(totals, b)
        live, count = live_mask(where_ref, near_ref, b, hidden_ref.shape[2])
        centred = (hidden_ref[b].astype(F32) - mean_row) * inv_std
        value = centred * scale_ref[2:3] + shift_ref[2:3] + act_ref[b].astype(F32)
        gate = sigmoid(value)
        features_ref[b] = (live * (value * gate)).astype(BF16)
        upstream = grad_ref[where_ref[0] + b].astype(F32) * live * (gate * (1.0 + value * (1.0 - gate)))
        slope_ref[b] = upstream
        put_sums(sums_ref, b, col_sum(upstream), col_sum(upstream * centred), count)


def put_halves(where_ref, grad_ref, keep_ref, send_ref):
    half = keep_ref.shape[0]
    core = where_ref[1]
    keep_ref[...] = grad_ref[pl.ds(pl.multiple_of(core * half, 16), half)].astype(BF16)
    send_ref[...] = grad_ref[pl.ds(pl.multiple_of((1 - core) * half, 16), half)].astype(BF16)


def backward_kernel(norm_at, with_skip, ways, where_ref, *refs):
    upstream_ref, hidden_ref, lower_ref, act_ref, near_ref, weight_ref, scale_ref, shift_ref = refs[:8]
    own = sum_refs(refs[8 : 8 + ways])
    back = sum_refs(refs[8 + ways : 8 + 2 * ways])
    low = sum_refs(refs[8 + 2 * ways : 8 + 3 * ways])
    rest = refs[8 + 3 * ways :]
    next_ref, sums_ref, keep_ref, send_ref, grad_ref = rest[-5:]
    channels = hidden_ref.shape[2]
    used = weight_ref.shape[0] * channels
    grad_ref[used:] = jnp.zeros((grad_ref.shape[0] - used, channels), F32)
    for b in range(hidden_ref.shape[0]):
        mean_row, inv_std, count = moments(own, b)
        live, own_count = live_mask(where_ref, near_ref, b, channels)
        centred = (hidden_ref[b].astype(F32) - mean_row) * inv_std
        rows_grad = norm_back(
            upstream_ref[b], centred, live, inv_std, scale_ref[norm_at : norm_at + 1], back, b, count
        ).astype(BF16)
        act_t = jnp.transpose(act_ref[b])
        values = rows_grad.astype(F32)
        power = power_for(jnp.max(jnp.abs(values), axis=0, keepdims=True))
        undo = 1.0 / power
        undo_low = undo.astype(BF16)
        scaled = values * power
        pair = two_parts(scaled)
        below = None
        for group in GROUPS:
            offsets = group_offsets(group)
            rows = [
                scaled.astype(BF16) if k == 13 else moved_rows(where_ref, near_ref, b, k, pair)
                for k in offsets
            ]
            moved = jnp.concatenate(rows, axis=1)
            weight = jnp.concatenate([weight_ref[k] * undo_low for k in offsets], axis=1)
            term = mm_t(moved, weight)
            below = term if below is None else below + term
            products = mm(act_t, moved)
            for i, k in enumerate(offsets):
                product = products[:, i * channels : (i + 1) * channels] * undo
                if b > 0:
                    product = product + grad_ref[k * channels : (k + 1) * channels]
                grad_ref[k * channels : (k + 1) * channels] = product
        below = below.astype(BF16).astype(F32)
        if with_skip:
            below = below + rest[0][b].astype(BF16).astype(F32)
        low_mean, low_std, _ = moments(low, b)
        low_centred = (lower_ref[b] - low_mean) * low_std
        value = low_centred * scale_ref[norm_at - 1 : norm_at] + shift_ref[norm_at - 1 : norm_at]
        gate = sigmoid(value)
        upstream = below * live * (gate * (1.0 + value * (1.0 - gate)))
        next_ref[b] = upstream
        put_sums(sums_ref, b, col_sum(upstream), col_sum(upstream * low_centred), own_count)
    put_halves(where_ref, grad_ref, keep_ref, send_ref)


def last_kernel(ways, where_ref, upstream_ref, hidden_ref, kids_ref, near_ref, scale_ref, *refs):
    own, back = sum_refs(refs[:ways]), sum_refs(refs[ways : 2 * ways])
    rows_ref, keep_ref, send_ref, grad_ref = refs[2 * ways :]
    channels = hidden_ref.shape[2]
    used = kids_ref.shape[1]
    if grad_ref.shape[0] > used:
        grad_ref[used:] = jnp.zeros((grad_ref.shape[0] - used, channels), F32)
    total = None
    for b in range(hidden_ref.shape[0]):
        mean_row, inv_std, count = moments(own, b)
        live, _ = live_mask(where_ref, near_ref, b, channels)
        centred = (hidden_ref[b] - mean_row) * inv_std
        rows_grad = norm_back(
            upstream_ref[b], centred, live, inv_std, scale_ref[0:1], back, b, count
        ).astype(BF16)
        rows_ref[b] = rows_grad
        product = mm(kids_ref[b], rows_grad)
        total = product if total is None else total + product
    grad_ref[:used] = total
    put_halves(where_ref, grad_ref, keep_ref, send_ref)


def input_kernel(where_ref, rows_ref, which_ref, down_ref, weight_ref, input_ref):
    in_channels, fine_rows = input_ref.shape[1:]
    step = 256
    pieces = mm_t(weight_ref[...], rows_ref[0]).astype(BF16)
    first, last = parent_rows(down_ref[0], fine_rows)
    for at in range(0, fine_rows, step):
        full = mm_t(pieces, parent_hits(first, last, at, step))
        code = jnp.broadcast_to(which_ref[0, 0:1, at : at + step], (in_channels, step))
        out = jnp.zeros((in_channels, step), F32)
        for k in range(full.shape[0] // in_channels):
            out = out + jnp.where(code == float(k + 1), full[in_channels * k : in_channels * (k + 1)], 0.0)
        input_ref[0, :, at : at + step] = out.astype(BF16)


def split_kernel(sections, depths, parts, where_ref, *refs):
    pairs, outs = refs[: 2 * len(parts)], refs[2 * len(parts) :]
    total = sum(parts)
    for j in range(sections):
        block = where_ref[2] ^ j
        base = 0
        for i, size in enumerate(parts):
            wide = depths * size
            rows = pl.ds(pl.multiple_of(block * wide, 16), wide)
            both = (pairs[2 * i][rows].astype(F32) + pairs[2 * i + 1][rows].astype(F32)).astype(BF16)
            for z in range(depths):
                outs[j][z * total + base : z * total + base + size] = both[z * size : (z + 1) * size]
            base += size


def spread_kernel(depths, sources, where_ref, *refs):
    blocks, halves, outs = refs[:sources], refs[sources : sources + 2], refs[sources + 2 :]
    small = halves[0].shape[0] // depths
    size = outs[0].shape[0] - small
    for j in range(depths):
        place = where_ref[3] ^ j
        rows = pl.ds(pl.multiple_of(place * size, 16), size)
        outs[j][:size] = tree_sum([ref[rows].astype(F32) for ref in blocks]).astype(BF16)
        rows = pl.ds(pl.multiple_of(place * small, 16), small)
        outs[j][size:] = (halves[0][rows].astype(F32) + halves[1][rows].astype(F32)).astype(BF16)


def add_kernel(where_ref, *refs):
    refs[-1][...] = sum_refs(refs[:-1]).astype(BF16)


def join_kernel(ways, small, mine, where_ref, *refs):
    pieces, sums_refs, out_ref = refs[: -3 * ways - 1], refs[-3 * ways - 1 : -1], refs[-1]
    size = pieces[0].shape[0] - small
    base = len(pieces) * size
    for j, ref in enumerate(pieces):
        place = where_ref[3] ^ j
        out_ref[pl.ds(pl.multiple_of(place * size, 16), size)] = ref[:size]
        out_ref[pl.ds(pl.multiple_of(base + place * small, 16), small)] = ref[size:]
    rows = []
    for t in range(3):
        totals = sum_refs(sums_refs[t * ways : (t + 1) * ways])
        rows.append(sum(totals[4 * b : 4 * b + 2] for b in range(mine)))
    exact = jnp.concatenate(rows + [jnp.zeros_like(rows[0])], axis=0)
    high = exact.astype(BF16)
    low = (exact - high.astype(F32)).astype(BF16)
    out_ref[base + len(pieces) * small :] = jnp.concatenate([high, low], axis=0)


def gather_kernel(size, where_ref, *refs):
    pieces, (out_ref, scale_ref, shift_ref) = refs[:-3], refs[-3:]
    for j, ref in enumerate(pieces):
        out_ref[pl.ds(pl.multiple_of((where_ref[2] ^ j) * size, 16), size)] = ref[:size]
    tails = [ref[size:].astype(F32) for ref in pieces]
    middle = tails[0].shape[0] - 16
    out_ref[len(pieces) * size :] = tree_sum([tail[:middle] for tail in tails]).astype(BF16)
    sums = tree_sum([tail[middle : middle + 8] + tail[middle + 8 :] for tail in tails])
    shift_ref[...] = jnp.concatenate([sums[2 * t : 2 * t + 1] for t in range(3)], axis=0)
    scale_ref[...] = jnp.concatenate([sums[2 * t + 1 : 2 * t + 2] for t in range(3)], axis=0)


def final_kernel(parts, blocks, flip, where_ref, half_ref, *refs):
    count = len(parts) + 1
    outs, scratches, leaving = refs[-2 * count - 1 : -count - 1], refs[-count - 1 : -1], refs[-1]
    core = where_ref[1]
    place = 1 - core if flip else core
    total = sum(parts)
    base = 0
    copies = []
    for i in range(count):
        scratch, out = scratches[i], outs[i]
        half = scratch.shape[0]
        if i < len(parts):
            size = parts[i]
            for t in range(blocks):
                scratch[t * size : (t + 1) * size] = half_ref[t * total + base : t * total + base + size].astype(F32)
            base += size
        else:
            scratch[...] = half_ref[blocks * total :].astype(F32)
        sure = out.shape[0] - half
        copy = pltpu.make_async_copy(
            scratch.at[pl.ds(0, sure)],
            out.at[pl.ds(pl.multiple_of(place * half, 16), sure)],
            leaving.at[i, 0],
        )
        copy.start()
        copies.append(copy)
        if sure < half:
            more = pltpu.make_async_copy(
                scratch.at[pl.ds(sure, half - sure)], out.at[pl.ds(sure, half - sure)], leaving.at[i, 1]
            )

            @pl.when(place == 0)
            def _():
                more.start()
                more.wait()

    for copy in copies:
        copy.wait()


def run(kernel, where, operands, outs, scratch=(), hbm_in=(), hbm_out=False, aliases=None, flops=0, grid=None):
    def place(i):
        return pltpu.HBM if i in hbm_in else pltpu.VMEM

    return pl.pallas_call(
        kernel,
        in_specs=[pl.BlockSpec(memory_space=pltpu.SMEM)]
        + [pl.BlockSpec(memory_space=place(i)) for i in range(len(operands))],
        out_specs=[pl.BlockSpec(memory_space=pltpu.HBM if hbm_out else pltpu.VMEM)] * len(outs),
        out_shape=outs,
        scratch_shapes=list(scratch),
        input_output_aliases=aliases or {},
        compiler_params=pltpu.CompilerParams(vmem_limit_bytes=VMEM_BYTES),
        cost_estimate=pl.CostEstimate(flops=flops, bytes_accessed=1 << 20, transcendentals=0),
    )(where, *operands)


def swapped(value, axis, step):
    count = lax.axis_size(axis)
    return lax.ppermute(value, axis, [(i, i ^ step) for i in range(count)])


def bucket_sums(value):
    value = value + swapped(value, "dp", 1)
    return [value] + [swapped(value, "dp", step) for step in range(2, lax.axis_size("dp"), 2)]


def local(
    voxel_feats, down_map, neighbours, w_down, w_first, w_second, bn_scale, bn_shift, out_grad
):
    sections = lax.axis_size("section")
    depths = lax.axis_size("dp") // 2
    mine = voxel_feats.shape[0] // sections
    section, bucket = lax.axis_index("section"), lax.axis_index("dp")
    where = jnp.stack([section * mine, bucket % 2, section, bucket // 2]).astype(jnp.int32)
    voxel_feats = jnp.swapaxes(voxel_feats, 1, 2)
    near = jnp.swapaxes(neighbours, 0, 1)
    in_channels, fine_rows = voxel_feats.shape[1:]
    coarse_rows = neighbours.shape[2]
    channels = w_first.shape[2]
    offsets = down_map.shape[1]
    wide = offsets * in_channels
    flat_down = w_down.reshape(wide, channels)
    shape = jax.ShapeDtypeStruct
    rows_f32 = shape((mine, coarse_rows, channels), F32)
    rows_bf16 = shape((mine, coarse_rows, channels), BF16)
    sums = shape((4 * mine, channels), F32)
    conv_flops = 8 * mine * w_first.shape[0] * coarse_rows * coarse_rows * channels

    def in_hbm(value):
        return pltpu.with_memory_space_constraint(value, pltpu.HBM)

    hidden_zero, part_zero, kids, which = run(
        down_kernel, where,
        [in_hbm(voxel_feats), in_hbm(down_map), in_hbm(flat_down)],
        [rows_f32, sums, shape((mine, wide, coarse_rows), BF16), shape((mine, 8, fine_rows), F32)],
        [
            pltpu.VMEM((wide, fine_rows), BF16),
            pltpu.VMEM((fine_rows, coarse_rows), BF16),
            pltpu.VMEM((mine, in_channels, fine_rows), BF16),
            pltpu.VMEM((mine, offsets, coarse_rows), jnp.int32),
            pltpu.VMEM((wide, channels), BF16),
            pltpu.SemaphoreType.DMA((mine, 3)),
        ],
        hbm_in=(0, 1, 2),
        flops=4 * 10**9,
    )
    stats_zero = bucket_sums(part_zero)
    ways = len(stats_zero)
    act_zero, hidden_one, part_one = run(
        functools.partial(forward_kernel, 0, False), where,
        [hidden_zero, near, w_first, bn_scale, bn_shift] + stats_zero,
        [rows_bf16, rows_f32, sums],
        flops=conv_flops,
    )
    stats_one = bucket_sums(part_one)
    act_one, hidden_two, part_two = run(
        functools.partial(forward_kernel, 1, True), where,
        [hidden_one, near, w_second, bn_scale, bn_shift] + stats_one,
        [rows_bf16, rows_bf16, sums],
        flops=conv_flops,
    )
    stats_two = bucket_sums(part_two)
    features, up_two, back_part = run(
        output_kernel, where,
        [hidden_two, act_zero, out_grad, near, bn_scale, bn_shift] + stats_two,
        [rows_bf16, rows_f32, sums],
        flops=10**9,
    )
    back_two = bucket_sums(back_part)

    def part_rows(rows, pieces):
        return -(-rows // (pieces * 16)) * 16

    def half_shape(rows):
        return shape((rows, channels), BF16)

    def accumulator(rows):
        return [pltpu.VMEM((2 * rows, channels), F32)]

    blocks = sections * depths
    conv_rows = w_first.shape[0] * channels
    parts = [part_rows(conv_rows, 2 * blocks)] * 2
    small = part_rows(wide, 2 * depths)
    total = sum(parts)
    half = half_shape(blocks * parts[0])
    small_half = half_shape(depths * small)
    up_one, back_part, keep_second, send_second = run(
        functools.partial(backward_kernel, 2, False, ways), where,
        [up_two, hidden_two, hidden_one, act_one, near, w_second, bn_scale, bn_shift]
        + stats_two + back_two + stats_one,
        [rows_f32, sums, half, half],
        accumulator(half.shape[0]),
        flops=conv_flops,
    )
    back_one = bucket_sums(back_part)
    got_second = swapped(send_second, "dp", 1)
    up_zero, back_part, keep_first, send_first = run(
        functools.partial(backward_kernel, 1, True, ways), where,
        [up_one, hidden_one, hidden_zero, act_zero, near, w_first, bn_scale, bn_shift]
        + stats_one + back_one + stats_zero + [up_two],
        [rows_f32, sums, half, half],
        accumulator(half.shape[0]),
        flops=conv_flops,
    )
    got_first = swapped(send_first, "dp", 1)
    section_out = run(
        functools.partial(split_kernel, sections, depths, parts), where,
        [keep_second, got_second, keep_first, got_first],
        [half_shape(depths * total)] * sections,
    )
    arrived = [section_out[0]] + [swapped(section_out[j], "section", j) for j in range(1, sections)]
    back_zero = bucket_sums(back_part)
    rows_zero, keep_down, send_down = run(
        functools.partial(last_kernel, ways), where,
        [up_zero, hidden_zero, kids, near, bn_scale] + stats_zero + back_zero,
        [rows_bf16, small_half, small_half],
        accumulator(small_half.shape[0]),
        flops=10**9,
    )
    got_down = swapped(send_down, "dp", 1)
    depth_out = run(
        functools.partial(spread_kernel, depths, sections), where, arrived + [keep_down, got_down],
        [half_shape(total + small)] * depths,
    )
    arrived = [depth_out[0]] + [swapped(depth_out[j], "dp", 2 * j) for j in range(1, depths)]
    (summed,) = run(add_kernel, where, arrived, [half_shape(total + small)])
    arrived = [summed] + [swapped(summed, "dp", 2 * j) for j in range(1, depths)]
    (joined,) = run(
        functools.partial(join_kernel, ways, small, mine), where,
        arrived + back_zero + back_one + back_two,
        [half_shape(depths * (total + small) + 16)],
    )
    joined, rows_zero = lax.optimization_barrier((joined, rows_zero))
    arrived = [joined] + [swapped(joined, "section", j) for j in range(1, sections)]
    input_shape = shape((mine, in_channels, fine_rows), BF16)
    (input_grad,) = pl.pallas_call(
        input_kernel,
        grid_spec=pltpu.PrefetchScalarGridSpec(
            num_scalar_prefetch=1,
            grid=(mine,),
            in_specs=[
                pl.BlockSpec((1, coarse_rows, channels), lambda b, at: (b, 0, 0)),
                pl.BlockSpec((1, 8, fine_rows), lambda b, at: (b, 0, 0)),
                pl.BlockSpec((1, offsets, coarse_rows), lambda b, at: (at[0] + b, 0, 0)),
                pl.BlockSpec((wide, channels), lambda b, at: (0, 0)),
            ],
            out_specs=[pl.BlockSpec((1, in_channels, fine_rows), lambda b, at: (b, 0, 0))],
        ),
        out_shape=[input_shape],
        compiler_params=pltpu.CompilerParams(vmem_limit_bytes=VMEM_BYTES),
        cost_estimate=pl.CostEstimate(flops=4 * 10**9, bytes_accessed=1 << 20, transcendentals=0),
    )(where, rows_zero, which, down_map, flat_down)
    arrived, input_grad = lax.optimization_barrier((arrived, input_grad))
    norms = shape(bn_scale.shape, F32)
    gathered, grad_scale, grad_shift = run(
        functools.partial(gather_kernel, depths * total), where, arrived,
        [half_shape(blocks * total + depths * small), norms, norms],
    )
    other = swapped(gathered, "dp", 1)
    grads = [shape((conv_rows, channels), F32)] * 2 + [shape((wide, channels), F32)]
    staging = [pltpu.VMEM((half.shape[0], channels), F32)] * 2 + [
        pltpu.VMEM((small_half.shape[0], channels), F32),
        pltpu.SemaphoreType.DMA((3, 2)),
    ]
    grads_out = run(
        functools.partial(final_kernel, parts, blocks, False), where, [gathered], grads, staging,
        hbm_out=True, flops=10**9,
    )
    grad_second, grad_first, grad_down = run(
        functools.partial(final_kernel, parts, blocks, True), where, [other] + list(grads_out), grads, staging,
        hbm_in=(1, 2, 3), hbm_out=True, aliases={2: 0, 3: 1, 4: 2}, flops=10**9,
    )
    return (
        features,
        jnp.swapaxes(input_grad, 1, 2),
        grad_down.reshape(w_down.shape),
        grad_first.reshape(w_first.shape),
        grad_second.reshape(w_second.shape),
        grad_scale,
        grad_shift,
    )


def solution(mesh):
    in_specs = (
        P(None, "dp", None),
        P(None, None, "dp"),
        P(None, None, "dp"),
        P(),
        P(),
        P(),
        P(),
        P(),
        P(None, "dp", None),
    )
    out_specs = (P("section", "dp", None), P("section", "dp", None), P(), P(), P(), P(), P())
    return jax.shard_map(local, mesh=mesh, in_specs=in_specs, out_specs=out_specs, check_vma=False)
```

```python
import functools

import jax
import jax.numpy as jnp
from jax import lax
from jax.experimental import pallas as pl
from jax.experimental.pallas import tpu as pltpu
from jax.sharding import PartitionSpec as P

EPSILON = 1e-05
F32 = jnp.float32
BF16 = jnp.bfloat16
F8 = jnp.float8_e4m3fn
VMEM_BYTES = 40 << 20
UNROLL_FORWARD = False
UNROLL_BACKWARD = True
GROUPS = ((0, 1), (2, 3), (4, 5), (6, 7), (8, 9), (10, 11), (12, 13))


def mm(left, right):
    return jnp.dot(left, right, preferred_element_type=F32)


def mm_t(left, right):
    return lax.dot_general(left, right, (((1,), (1,)), ((), ())), preferred_element_type=F32)


def col_sum(values):
    return jnp.sum(values, axis=0, keepdims=True)


def sigmoid(values):
    return 1.0 / (1.0 + jnp.exp(-values))


def tree_sum(parts):
    parts = list(parts)
    while len(parts) > 1:
        parts = [parts[i] + parts[i + 1] for i in range(0, len(parts), 2)]
    return parts[0]


def sum_refs(refs):
    return tree_sum([ref[...].astype(F32) for ref in refs])


def hits(index_row, rows):
    places = lax.broadcasted_iota(jnp.int16, (rows, index_row.shape[1]), 0)
    return jnp.where(places == index_row, jnp.bfloat16(1), jnp.bfloat16(0)).astype(F8)


def live_mask(near_ref, bucket, channels):
    rows = near_ref.shape[2]
    centre = near_ref[bucket, 13:14, :]
    count = jnp.sum((centre < rows).astype(F32), axis=1, keepdims=True)
    places = lax.broadcasted_iota(jnp.int32, (rows, channels), 0).astype(F32)
    return (places < count).astype(F32), count


def power_for(largest):
    power = jnp.full_like(largest, 2.0**-60)
    for exponent in (64, 32, 16, 8, 4, 2, 1):
        raised = power * (2.0**exponent)
        power = jnp.where(largest * raised <= 224.0, raised, power)
    return power


def two_parts(scaled):
    high = scaled.astype(F8)
    low = (scaled - high.astype(F32)).astype(F8)
    return jnp.concatenate([high, low], axis=1)


def moved_rows(near_ref, bucket, offset, pair):
    row = near_ref[bucket, offset : offset + 1, :]
    both = mm(hits(row.astype(jnp.int16), row.shape[1]), pair)
    channels = pair.shape[1] // 2
    return (both[:, :channels] + both[:, channels:]).astype(BF16)


def group_offsets(group):
    return [k for j in group for k in ((j, 26 - j) if j < 13 else (13,))]


def moments(totals):
    count = totals[2:3]
    mean_row = totals[0:1] / count
    square = totals[1:2] / count
    return mean_row, lax.rsqrt(square - mean_row * mean_row + EPSILON), count


def add_sums(out_ref, first, second, count):
    third = jnp.broadcast_to(count, first.shape)
    rows = [first, second, third, jnp.zeros((out_ref.shape[0] - 3, first.shape[1]), F32)]
    out_ref[...] += jnp.concatenate(rows, axis=0)


def norm_back(upstream, centred, live, inv_std, gain_row, back, count):
    return live * (inv_std * gain_row) * (upstream - back[0:1] / count - centred * (back[1:2] / count))


def parent_rows(table, fine_rows):
    first = jnp.min(table, axis=0, keepdims=True)
    children = jnp.sum((table < fine_rows).astype(jnp.int32), axis=0, keepdims=True)
    return first, first + children


def parent_hits(first, last, at, size):
    places = lax.broadcasted_iota(jnp.int16, (size, first.shape[1]), 0) + jnp.int16(at)
    inside = (places >= first.astype(jnp.int16)) & (places < last.astype(jnp.int16))
    return jnp.where(inside, jnp.bfloat16(1), jnp.bfloat16(0))


def pack_kernel(
    where_ref, feats_hbm, down_hbm, weight_hbm,
    feats_send, table_send, feats_own, table_own, weight_ref, arrivals,
):
    copies = [
        pltpu.make_async_copy(source, target, arrivals.at[i])
        for i, (source, target) in enumerate(
            (
                (feats_hbm.at[where_ref[4]], feats_send),
                (down_hbm.at[where_ref[4]], table_send),
                (down_hbm.at[where_ref[0]], table_own),
                (feats_hbm.at[where_ref[0]], feats_own),
                (weight_hbm, weight_ref),
            )
        )
    ]
    for copy in copies:
        copy.start()
    for copy in copies:
        copy.wait()


def down_rows(table, feats_ref, weight_ref, which_ref, spread_ref, parent_ref):
    in_channels, fine_rows = feats_ref.shape
    offsets, coarse_rows = table.shape
    first, last = parent_rows(table, fine_rows)
    rank = table - first
    numbers = lax.broadcasted_iota(jnp.int32, (offsets, coarse_rows), 0) + 1
    rows = [jnp.sum(jnp.where(rank == r, numbers, 0), axis=0, keepdims=True) for r in range(8)]
    safe_first = jnp.where(first < fine_rows, first, 0)
    rows += [(safe_first // 16) * 16, safe_first % 16] + [jnp.zeros_like(first)] * 6
    lookup = jnp.concatenate(rows, axis=0).astype(F32).astype(BF16)
    step = 512
    for at in range(0, fine_rows, step):
        parent_ref[at : at + step] = parent_hits(first, last, at, step)
    found = mm_t(lookup, parent_ref[...])
    place = lax.broadcasted_iota(jnp.int32, (8, fine_rows), 1).astype(F32) - (found[8:9] + found[9:10])
    column = lax.broadcasted_iota(jnp.int32, (8, fine_rows), 0).astype(F32)
    which = jnp.sum(jnp.where(column == place, found[:8], 0.0), axis=0, keepdims=True)
    which_ref[...] = jnp.broadcast_to(which, which_ref.shape)
    code = jnp.broadcast_to(which, (in_channels, fine_rows)).astype(BF16)
    feats = feats_ref[...]
    for k in range(offsets):
        spread_ref[in_channels * k : in_channels * (k + 1)] = jnp.where(
            code == jnp.bfloat16(k + 1), feats, jnp.zeros_like(feats)
        )
    kids = mm(spread_ref[...], parent_ref[...]).astype(BF16)
    hidden = jnp.transpose(mm(jnp.transpose(weight_ref[...]), kids))
    count = jnp.sum((last > first).astype(F32), axis=1, keepdims=True)
    return kids, hidden, count


def down_kernel(
    where_ref, feats_ref, table_ref, weight_ref, near_ref,
    hidden_ref, sums_ref, kids_ref, which_ref, near_own, near_send,
    spread_ref, parent_ref,
):
    for k in range(near_own.shape[0]):
        near_own[k : k + 1] = near_ref[k, pl.ds(where_ref[0], 1), :]
        near_send[k : k + 1] = near_ref[k, pl.ds(where_ref[4], 1), :]
    kids, hidden, count = down_rows(
        table_ref[...], feats_ref, weight_ref, which_ref, spread_ref, parent_ref
    )
    kids_ref[...] = kids
    hidden_ref[...] = hidden
    sums_ref[...] = jnp.zeros_like(sums_ref)
    add_sums(sums_ref, col_sum(hidden), col_sum(hidden * hidden), count)


def down_other_kernel(
    where_ref, feats_ref, table_ref, weight_ref, own_hidden, own_sums, own_kids, own_which, own_table,
    hidden_ref, sums_ref, kids_ref, which_ref, tables_ref,
    spread_ref, parent_ref,
):
    kids, hidden, count = down_rows(
        table_ref[...], feats_ref, weight_ref, which_ref.at[1], spread_ref, parent_ref
    )
    kids_ref[1] = kids
    hidden_ref[1] = hidden
    tables_ref[1] = table_ref[...]
    for both, own in ((kids_ref, own_kids), (hidden_ref, own_hidden), (which_ref, own_which), (tables_ref, own_table)):
        both[0] = own[...]
    sums_ref[...] = own_sums[...]
    add_sums(sums_ref, col_sum(hidden), col_sum(hidden * hidden), count)


def conv_all(source, near_ref, bucket, weight_ref):
    values = source.astype(F32)
    largest = jnp.max(jnp.max(jnp.abs(values), axis=0, keepdims=True), axis=1, keepdims=True)
    power = power_for(largest)
    scaled = values * power
    pair = two_parts(scaled)
    out = None
    for group in GROUPS:
        offsets = group_offsets(group)
        rows = [
            scaled.astype(BF16) if k == 13 else moved_rows(near_ref, bucket, 26 - k, pair)
            for k in offsets
        ]
        weight = jnp.concatenate([weight_ref[k] for k in offsets], axis=0)
        term = mm(jnp.concatenate(rows, axis=1), weight)
        out = term if out is None else out + term
    return out * (1.0 / power)


def each_bucket(count, body, unrolled):
    if unrolled:
        for b in range(count):
            body(b)
        return

    def step(b, carry):
        body(b)
        return carry

    lax.fori_loop(0, count, step, 0)


def near_kernel(where_ref, own_ref, other_ref, near_ref):
    near_ref[0] = own_ref[...]
    near_ref[1] = other_ref[...]


def forward_kernel(norm_at, rounded, where_ref, hidden_ref, near_ref, weight_ref, scale_ref, shift_ref, *refs):
    part_refs, (act_ref, next_ref, sums_ref) = refs[:-3], refs[-3:]
    mean_row, inv_std, _ = moments(sum_refs(part_refs))
    sums_ref[...] = jnp.zeros_like(sums_ref)

    def bucket(b):
        live, count = live_mask(near_ref, b, hidden_ref.shape[2])
        centred = (hidden_ref[b] - mean_row) * inv_std
        value = centred * scale_ref[norm_at : norm_at + 1] + shift_ref[norm_at : norm_at + 1]
        act = (live * (value * sigmoid(value))).astype(BF16)
        act_ref[b] = act
        hidden = conv_all(act, near_ref, b, weight_ref)
        if rounded:
            hidden = hidden.astype(BF16)
        next_ref[b] = hidden
        hidden = hidden.astype(F32)
        add_sums(sums_ref, col_sum(hidden), col_sum(hidden * hidden), count)

    each_bucket(hidden_ref.shape[0], bucket, UNROLL_FORWARD)


def grad_kernel(where_ref, grad_ref, own_ref, send_ref):
    own_ref[...] = grad_ref[where_ref[0]]
    send_ref[...] = grad_ref[where_ref[4]]


def output_kernel(where_ref, hidden_ref, act_ref, own_grad, other_grad, near_ref, scale_ref, shift_ref, *refs):
    part_refs, (own_ref, send_ref, slope_ref, sums_ref) = refs[:-4], refs[-4:]
    mean_row, inv_std, _ = moments(sum_refs(part_refs))
    sums_ref[...] = jnp.zeros_like(sums_ref)
    for b, (grad_ref, features_ref) in enumerate(((own_grad, own_ref), (other_grad, send_ref))):
        live, count = live_mask(near_ref, b, hidden_ref.shape[2])
        centred = (hidden_ref[b].astype(F32) - mean_row) * inv_std
        value = centred * scale_ref[2:3] + shift_ref[2:3] + act_ref[b].astype(F32)
        gate = sigmoid(value)
        features_ref[...] = (live * (value * gate)).astype(BF16)
        upstream = grad_ref[...].astype(F32) * live * (gate * (1.0 + value * (1.0 - gate)))
        slope_ref[b] = upstream
        add_sums(sums_ref, col_sum(upstream), col_sum(upstream * centred), count)


def put_halves(where_ref, grad_ref, keep_ref, send_ref):
    half = keep_ref.shape[0]
    core = where_ref[1]
    keep_ref[...] = grad_ref[pl.ds(pl.multiple_of(core * half, 16), half)].astype(BF16)
    send_ref[...] = grad_ref[pl.ds(pl.multiple_of((1 - core) * half, 16), half)].astype(BF16)


def backward_kernel(norm_at, with_skip, ways, where_ref, *refs):
    upstream_ref, hidden_ref, lower_ref, act_ref, near_ref, weight_ref, scale_ref, shift_ref = refs[:8]
    own, back, low = (sum_refs(refs[8 + i * ways : 8 + (i + 1) * ways]) for i in range(3))
    rest = refs[8 + 3 * ways :]
    next_ref, sums_ref, keep_ref, send_ref, grad_ref = rest[-5:]
    mean_row, inv_std, count = moments(own)
    low_mean, low_std, _ = moments(low)
    channels = hidden_ref.shape[2]
    sums_ref[...] = jnp.zeros_like(sums_ref)
    grad_ref[...] = jnp.zeros_like(grad_ref)

    def bucket(b):
        live, own_count = live_mask(near_ref, b, channels)
        centred = (hidden_ref[b].astype(F32) - mean_row) * inv_std
        rows_grad = norm_back(
            upstream_ref[b], centred, live, inv_std, scale_ref[norm_at : norm_at + 1], back, count
        ).astype(BF16)
        act_t = jnp.transpose(act_ref[b])
        values = rows_grad.astype(F32)
        power = power_for(jnp.max(jnp.abs(values), axis=0, keepdims=True))
        undo = 1.0 / power
        undo_low = undo.astype(BF16)
        scaled = values * power
        pair = two_parts(scaled)
        below = None
        for group in GROUPS:
            offsets = group_offsets(group)
            rows = [
                scaled.astype(BF16) if k == 13 else moved_rows(near_ref, b, k, pair)
                for k in offsets
            ]
            moved = jnp.concatenate(rows, axis=1)
            weight = jnp.concatenate([weight_ref[k] * undo_low for k in offsets], axis=1)
            term = mm_t(moved, weight)
            below = term if below is None else below + term
            products = mm(act_t, moved)
            for i, k in enumerate(offsets):
                grad_ref[k * channels : (k + 1) * channels] += (
                    products[:, i * channels : (i + 1) * channels] * undo
                )
        below = below.astype(BF16).astype(F32)
        if with_skip:
            below = below + rest[0][b].astype(BF16).astype(F32)
        low_centred = (lower_ref[b] - low_mean) * low_std
        value = low_centred * scale_ref[norm_at - 1 : norm_at] + shift_ref[norm_at - 1 : norm_at]
        gate = sigmoid(value)
        upstream = below * live * (gate * (1.0 + value * (1.0 - gate)))
        next_ref[b] = upstream
        add_sums(sums_ref, col_sum(upstream), col_sum(upstream * low_centred), own_count)

    each_bucket(hidden_ref.shape[0], bucket, UNROLL_BACKWARD)
    put_halves(where_ref, grad_ref, keep_ref, send_ref)


def last_kernel(ways, where_ref, upstream_ref, hidden_ref, kids_ref, near_ref, scale_ref, *refs):
    rows_ref, keep_ref, send_ref, norms_ref, grad_ref = refs[4 * ways :]
    mean_row, inv_std, count = moments(sum_refs(refs[:ways]))
    backs = [sum_refs(refs[i * ways : (i + 1) * ways]) for i in (1, 2, 3)]
    back = backs[0]
    rows = [totals[0:2] for totals in backs]
    norms_ref[...] = jnp.concatenate(rows + [jnp.zeros_like(rows[0])], axis=0)
    channels = hidden_ref.shape[2]
    used = kids_ref.shape[1]
    if grad_ref.shape[0] > used:
        grad_ref[used:] = jnp.zeros((grad_ref.shape[0] - used, channels), F32)
    total = None
    for b in range(hidden_ref.shape[0]):
        live, _ = live_mask(near_ref, b, channels)
        centred = (hidden_ref[b] - mean_row) * inv_std
        rows_grad = norm_back(
            upstream_ref[b], centred, live, inv_std, scale_ref[0:1], back, count
        ).astype(BF16)
        rows_ref[b] = rows_grad
        product = mm(kids_ref[b], rows_grad)
        total = product if total is None else total + product
    grad_ref[:used] = total
    put_halves(where_ref, grad_ref, keep_ref, send_ref)


def input_kernel(where_ref, rows_ref, which_ref, tables_ref, weight_ref, own_ref, send_ref):
    in_channels, fine_rows = own_ref.shape
    step = 256
    for b, input_ref in enumerate((own_ref, send_ref)):
        pieces = mm_t(weight_ref[...], rows_ref[b]).astype(BF16)
        first, last = parent_rows(tables_ref[b], fine_rows)
        for at in range(0, fine_rows, step):
            full = mm_t(pieces, parent_hits(first, last, at, step))
            code = jnp.broadcast_to(which_ref[b, 0:1, at : at + step], (in_channels, step))
            out = jnp.zeros((in_channels, step), F32)
            for k in range(full.shape[0] // in_channels):
                out = out + jnp.where(code == float(k + 1), full[in_channels * k : in_channels * (k + 1)], 0.0)
            input_ref[:, at : at + step] = out.astype(BF16)


def place_outputs_kernel(where_ref, own_features, other_features, own_input, other_input, features, inputs, leaving):
    copies = [
        pltpu.make_async_copy(source, target.at[place], leaving.at[i])
        for i, (source, target, place) in enumerate(
            (
                (own_features, features, where_ref[1]),
                (other_features, features, 1 - where_ref[1]),
                (own_input, inputs, where_ref[1]),
                (other_input, inputs, 1 - where_ref[1]),
            )
        )
    ]
    for copy in copies:
        copy.start()
    for copy in copies:
        copy.wait()


def split_kernel(sections, depths, parts, where_ref, *refs):
    pairs, outs = refs[: 2 * len(parts)], refs[2 * len(parts) :]
    total = sum(parts)
    for j in range(sections):
        block = where_ref[2] ^ j
        base = 0
        for i, size in enumerate(parts):
            wide = depths * size
            rows = pl.ds(pl.multiple_of(block * wide, 16), wide)
            both = (pairs[2 * i][rows].astype(F32) + pairs[2 * i + 1][rows].astype(F32)).astype(BF16)
            for z in range(depths):
                outs[j][z * total + base : z * total + base + size] = both[z * size : (z + 1) * size]
            base += size


def spread_kernel(depths, sources, where_ref, *refs):
    blocks, halves, outs = refs[:sources], refs[sources : sources + 2], refs[sources + 2 :]
    small = halves[0].shape[0] // depths
    size = outs[0].shape[0] - small
    for j in range(depths):
        place = where_ref[3] ^ j
        rows = pl.ds(pl.multiple_of(place * size, 16), size)
        outs[j][:size] = tree_sum([ref[rows].astype(F32) for ref in blocks]).astype(BF16)
        rows = pl.ds(pl.multiple_of(place * small, 16), small)
        outs[j][size:] = (halves[0][rows].astype(F32) + halves[1][rows].astype(F32)).astype(BF16)


def add_kernel(where_ref, *refs):
    refs[-1][...] = sum_refs(refs[:-1]).astype(BF16)


def high_and_low(exact):
    high = exact.astype(BF16)
    low = (exact - high.astype(F32)).astype(BF16)
    return jnp.concatenate([high, low], axis=0)


def one_value(high_low):
    rows = high_low.shape[0] // 2
    return high_low[:rows].astype(F32) + high_low[rows:].astype(F32)


def join_kernel(small, where_ref, *refs):
    pieces, norm_refs, out_ref = refs[:-3], refs[-3:-1], refs[-1]
    size = pieces[0].shape[0] - small
    base = len(pieces) * size
    for j, ref in enumerate(pieces):
        place = where_ref[3] ^ j
        out_ref[pl.ds(pl.multiple_of(place * size, 16), size)] = ref[:size]
        out_ref[pl.ds(pl.multiple_of(base + place * small, 16), small)] = ref[size:]
    out_ref[base + len(pieces) * small :] = high_and_low(sum_refs(norm_refs))


def gather_kernel(size, where_ref, *refs):
    pieces, (out_ref, scale_ref, shift_ref) = refs[:-3], refs[-3:]
    for j, ref in enumerate(pieces):
        out_ref[pl.ds(pl.multiple_of((where_ref[2] ^ j) * size, 16), size)] = ref[:size]
    tails = [ref[size:].astype(F32) for ref in pieces]
    middle = tails[0].shape[0] - 16
    out_ref[len(pieces) * size :] = tree_sum([tail[:middle] for tail in tails]).astype(BF16)
    sums = tree_sum([one_value(tail[middle:]) for tail in tails])
    shift_ref[...] = jnp.concatenate([sums[2 * t : 2 * t + 1] for t in range(3)], axis=0)
    scale_ref[...] = jnp.concatenate([sums[2 * t + 1 : 2 * t + 2] for t in range(3)], axis=0)


def final_kernel(parts, blocks, flip, where_ref, half_ref, *refs):
    count = len(parts) + 1
    outs, scratches, leaving = refs[-2 * count - 1 : -count - 1], refs[-count - 1 : -1], refs[-1]
    core = where_ref[1]
    place = 1 - core if flip else core
    total = sum(parts)
    base = 0
    copies, extras = [], []
    for i in range(count):
        scratch, out = scratches[i], outs[i]
        half = scratch.shape[0]
        if i < len(parts):
            size = parts[i]
            for t in range(blocks):
                scratch[t * size : (t + 1) * size] = half_ref[t * total + base : t * total + base + size].astype(F32)
            base += size
        else:
            scratch[...] = half_ref[blocks * total :].astype(F32)
        sure = out.shape[0] - half
        copy = pltpu.make_async_copy(
            scratch.at[pl.ds(0, sure)],
            out.at[pl.ds(pl.multiple_of(place * half, 16), sure)],
            leaving.at[i, 0],
        )
        copy.start()
        copies.append(copy)
        if sure < half:
            extras.append(
                pltpu.make_async_copy(
                    scratch.at[pl.ds(sure, half - sure)], out.at[pl.ds(sure, half - sure)], leaving.at[i, 1]
                )
            )

    @pl.when(place == 0)
    def _():
        for copy in extras:
            copy.start()
        for copy in extras:
            copy.wait()

    for copy in copies:
        copy.wait()


def run(kernel, where, operands, outs, scratch=(), hbm_in=(), hbm_out=False, aliases=None, flops=0, grid=None):
    def place(i):
        return pltpu.HBM if i in hbm_in else pltpu.VMEM

    return pl.pallas_call(
        kernel,
        in_specs=[pl.BlockSpec(memory_space=pltpu.SMEM)]
        + [pl.BlockSpec(memory_space=place(i)) for i in range(len(operands))],
        out_specs=[pl.BlockSpec(memory_space=pltpu.HBM if hbm_out else pltpu.VMEM)] * len(outs),
        out_shape=outs,
        scratch_shapes=list(scratch),
        input_output_aliases=aliases or {},
        compiler_params=pltpu.CompilerParams(vmem_limit_bytes=VMEM_BYTES),
        cost_estimate=pl.CostEstimate(flops=flops, bytes_accessed=1 << 20, transcendentals=0),
    )(where, *operands)


def swapped(value, axis, step):
    count = lax.axis_size(axis)
    return lax.ppermute(value, axis, [(i, i ^ step) for i in range(count)])


def depth_sums(value):
    return [value] + [swapped(value, "dp", step) for step in range(2, lax.axis_size("dp"), 2)]


def local(
    voxel_feats, down_map, neighbours, w_down, w_first, w_second, bn_scale, bn_shift, out_grad
):
    sections = lax.axis_size("section")
    depths = lax.axis_size("dp") // 2
    mine = voxel_feats.shape[0] // sections
    section, bucket = lax.axis_index("section"), lax.axis_index("dp")
    core = bucket % 2
    base = section * mine
    where = jnp.stack([base + core, core, section, bucket // 2, base + 1 - core]).astype(jnp.int32)
    voxel_feats = jnp.swapaxes(voxel_feats, 1, 2)
    near = jnp.swapaxes(neighbours, 0, 1)
    in_channels, fine_rows = voxel_feats.shape[1:]
    coarse_rows = neighbours.shape[2]
    channels = w_first.shape[2]
    offsets = down_map.shape[1]
    wide = offsets * in_channels
    flat_down = w_down.reshape(wide, channels)
    shape = jax.ShapeDtypeStruct
    rows_f32 = shape((mine, coarse_rows, channels), F32)
    rows_bf16 = shape((mine, coarse_rows, channels), BF16)
    one_bf16 = shape((coarse_rows, channels), BF16)
    sums = shape((8, channels), F32)
    table = shape((offsets, coarse_rows), jnp.int32)
    near_one = shape((w_first.shape[0], coarse_rows), jnp.int32)
    conv_flops = 8 * mine * w_first.shape[0] * coarse_rows * coarse_rows * channels

    def in_hbm(value):
        return pltpu.with_memory_space_constraint(value, pltpu.HBM)

    def cores(value):
        return swapped(value, "dp", 1)

    feats_hbm, down_hbm = in_hbm(voxel_feats), in_hbm(down_map)
    feats_one = shape((in_channels, fine_rows), BF16)
    send_feats, send_table, own_feats, own_table, weight_down = run(
        pack_kernel, where, [feats_hbm, down_hbm, in_hbm(flat_down)],
        [feats_one, table, feats_one, table, shape((wide, channels), BF16)],
        [pltpu.SemaphoreType.DMA((5,))], hbm_in=(0, 1, 2),
    )
    got_feats, got_table = cores(send_feats), cores(send_table)
    down_scratch = [pltpu.VMEM((wide, fine_rows), BF16), pltpu.VMEM((fine_rows, coarse_rows), BF16)]
    own_hidden, own_sums, own_kids, own_which, near_own, near_send = run(
        down_kernel, where,
        [own_feats, own_table, weight_down, near],
        [
            shape((coarse_rows, channels), F32), sums, shape((wide, coarse_rows), BF16),
            shape((8, fine_rows), F32), near_one, near_one,
        ],
        down_scratch,
        flops=2 * 10**9,
    )
    hidden_zero, part_zero, kids, which, tables = run(
        down_other_kernel, where,
        [got_feats, got_table, weight_down, own_hidden, own_sums, own_kids, own_which, own_table],
        [
            rows_f32, sums, shape((mine, wide, coarse_rows), BF16), shape((mine, 8, fine_rows), F32),
            shape((mine, offsets, coarse_rows), jnp.int32),
        ],
        down_scratch,
        flops=2 * 10**9,
    )
    stats_zero = depth_sums(part_zero)
    ways = len(stats_zero)
    (nears,) = run(
        near_kernel, where, [near_own, cores(near_send)],
        [shape((mine, w_first.shape[0], coarse_rows), jnp.int32)],
    )
    act_zero, hidden_one, part_one = run(
        functools.partial(forward_kernel, 0, False), where,
        [hidden_zero, nears, w_first, bn_scale, bn_shift] + stats_zero,
        [rows_bf16, rows_f32, sums],
        flops=conv_flops,
    )
    stats_one = depth_sums(part_one)
    grad_own, grad_send = run(grad_kernel, where, [out_grad], [one_bf16, one_bf16])
    grad_other = cores(grad_send)
    act_one, hidden_two, part_two = run(
        functools.partial(forward_kernel, 1, True), where,
        [hidden_one, nears, w_second, bn_scale, bn_shift] + stats_one,
        [rows_bf16, rows_bf16, sums],
        flops=conv_flops,
    )
    stats_two = depth_sums(part_two)
    features_own, features_send, up_two, back_part = run(
        output_kernel, where,
        [hidden_two, act_zero, grad_own, grad_other, nears, bn_scale, bn_shift] + stats_two,
        [one_bf16, one_bf16, rows_f32, sums],
        flops=10**9,
    )
    back_two = depth_sums(back_part)

    def part_rows(rows, pieces):
        return -(-rows // (pieces * 16)) * 16

    def half_shape(rows):
        return shape((rows, channels), BF16)

    def accumulator(rows):
        return [pltpu.VMEM((2 * rows, channels), F32)]

    blocks = sections * depths
    conv_rows = w_first.shape[0] * channels
    parts = [part_rows(conv_rows, 2 * blocks)] * 2
    small = part_rows(wide, 2 * depths)
    total = sum(parts)
    half = half_shape(blocks * parts[0])
    small_half = half_shape(depths * small)
    up_one, back_part, keep_second, send_second = run(
        functools.partial(backward_kernel, 2, False, ways), where,
        [up_two, hidden_two, hidden_one, act_one, nears, w_second, bn_scale, bn_shift]
        + stats_two + back_two + stats_one,
        [rows_f32, sums, half, half],
        accumulator(half.shape[0]),
        flops=conv_flops,
    )
    back_one = depth_sums(back_part)
    got_second = cores(send_second)
    features_other = cores(features_send)
    features_other, up_one = lax.optimization_barrier((features_other, up_one))
    up_zero, back_part, keep_first, send_first = run(
        functools.partial(backward_kernel, 1, True, ways), where,
        [up_one, hidden_one, hidden_zero, act_zero, nears, w_first, bn_scale, bn_shift]
        + stats_one + back_one + stats_zero + [up_two],
        [rows_f32, sums, half, half],
        accumulator(half.shape[0]),
        flops=conv_flops,
    )
    got_first = cores(send_first)
    section_out = run(
        functools.partial(split_kernel, sections, depths, parts), where,
        [keep_second, got_second, keep_first, got_first],
        [half_shape(depths * total)] * sections,
    )
    arrived = [section_out[0]] + [swapped(section_out[j], "section", j) for j in range(1, sections)]
    back_zero = depth_sums(back_part)
    rows_zero, keep_down, send_down, norm_rows = run(
        functools.partial(last_kernel, ways), where,
        [up_zero, hidden_zero, kids, nears, bn_scale] + stats_zero + back_zero + back_one + back_two,
        [rows_bf16, small_half, small_half, sums],
        accumulator(small_half.shape[0]),
        flops=10**9,
    )
    got_down = cores(send_down)
    depth_out = run(
        functools.partial(spread_kernel, depths, sections), where, arrived + [keep_down, got_down],
        [half_shape(total + small)] * depths,
    )
    arrived = [depth_out[0]] + [swapped(depth_out[j], "dp", 2 * j) for j in range(1, depths)]
    (summed,) = run(add_kernel, where, arrived, [half_shape(total + small)])
    arrived = [summed] + [swapped(summed, "dp", 2 * j) for j in range(1, depths)]
    (joined,) = run(
        functools.partial(join_kernel, small), where, arrived + [norm_rows, cores(norm_rows)],
        [half_shape(depths * (total + small) + 16)],
    )
    joined, rows_zero = lax.optimization_barrier((joined, rows_zero))
    arrived = [joined] + [swapped(joined, "section", j) for j in range(1, sections)]
    input_own, input_send = run(
        input_kernel, where, [rows_zero, which, tables, weight_down], [feats_one, feats_one],
        flops=4 * 10**9,
    )
    features, input_grad = run(
        place_outputs_kernel, where,
        [features_own, features_other, input_own, cores(input_send)],
        [rows_bf16, shape((mine, in_channels, fine_rows), BF16)],
        [pltpu.SemaphoreType.DMA((4,))],
        hbm_out=True,
    )
    arrived, features, input_grad = lax.optimization_barrier((arrived, features, input_grad))
    norms = shape(bn_scale.shape, F32)
    gathered, grad_scale, grad_shift = run(
        functools.partial(gather_kernel, depths * total), where, arrived,
        [half_shape(blocks * total + depths * small), norms, norms],
    )
    other = cores(gathered)
    grads = [shape((conv_rows, channels), F32)] * 2 + [shape((wide, channels), F32)]
    staging = [pltpu.VMEM((half.shape[0], channels), F32)] * 2 + [
        pltpu.VMEM((small_half.shape[0], channels), F32),
        pltpu.SemaphoreType.DMA((3, 2)),
    ]
    grads_out = run(
        functools.partial(final_kernel, parts, blocks, False), where, [gathered], grads, staging,
        hbm_out=True, flops=10**9,
    )
    grad_second, grad_first, grad_down = run(
        functools.partial(final_kernel, parts, blocks, True), where, [other] + list(grads_out), grads, staging,
        hbm_in=(1, 2, 3), hbm_out=True, aliases={2: 0, 3: 1, 4: 2}, flops=10**9,
    )
    return (
        features,
        jnp.swapaxes(input_grad, 1, 2),
        grad_down.reshape(w_down.shape),
        grad_first.reshape(w_first.shape),
        grad_second.reshape(w_second.shape),
        grad_scale,
        grad_shift,
    )


def solution(mesh):
    in_specs = (
        P(None, "dp", None),
        P(None, None, "dp"),
        P(None, None, "dp"),
        P(),
        P(),
        P(),
        P(),
        P(),
        P(None, "dp", None),
    )
    out_specs = (P("section", "dp", None), P("section", "dp", None), P(), P(), P(), P(), P())
    return jax.shard_map(local, mesh=mesh, in_specs=in_specs, out_specs=out_specs, check_vma=False)
```

```python
import functools

import jax
import jax.numpy as jnp
from jax import lax
from jax.experimental import pallas as pl
from jax.experimental.pallas import tpu as pltpu
from jax.sharding import PartitionSpec as P

EPSILON = 1e-05
F32 = jnp.float32
BF16 = jnp.bfloat16
F8 = jnp.float8_e4m3fn
VMEM_BYTES = 40 << 20
UNROLL_FORWARD = False
UNROLL_BACKWARD = True
GROUPS = ((0, 1), (2, 3), (4, 5), (6, 7), (8, 9), (10, 11), (12, 13))


def mm(left, right):
    return jnp.dot(left, right, preferred_element_type=F32)


def mm_t(left, right):
    return lax.dot_general(left, right, (((1,), (1,)), ((), ())), preferred_element_type=F32)


def col_sum(values):
    return jnp.sum(values, axis=0, keepdims=True)


def sigmoid(values):
    return 1.0 / (1.0 + jnp.exp(-values))


def tree_sum(parts):
    parts = list(parts)
    while len(parts) > 1:
        parts = [parts[i] + parts[i + 1] for i in range(0, len(parts), 2)]
    return parts[0]


def sum_refs(refs):
    return tree_sum([ref[...].astype(F32) for ref in refs])


def hits(index_row, rows):
    places = lax.broadcasted_iota(jnp.int16, (rows, index_row.shape[1]), 0)
    return jnp.where(places == index_row, jnp.bfloat16(1), jnp.bfloat16(0)).astype(F8)


def live_mask(near_ref, bucket, channels):
    rows = near_ref.shape[2]
    centre = near_ref[bucket, 13:14, :]
    count = jnp.sum((centre < rows).astype(F32), axis=1, keepdims=True)
    places = lax.broadcasted_iota(jnp.int32, (rows, channels), 0).astype(F32)
    return (places < count).astype(F32), count


def power_for(largest):
    power = jnp.full_like(largest, 2.0**-60)
    for exponent in (64, 32, 16, 8, 4, 2, 1):
        raised = power * (2.0**exponent)
        power = jnp.where(largest * raised <= 224.0, raised, power)
    return power


def two_parts(scaled):
    high = scaled.astype(F8)
    low = (scaled - high.astype(F32)).astype(F8)
    return jnp.concatenate([high, low], axis=1)


def moved_rows(near_ref, bucket, offset, pair):
    row = near_ref[bucket, offset : offset + 1, :]
    both = mm(hits(row.astype(jnp.int16), row.shape[1]), pair)
    channels = pair.shape[1] // 2
    return (both[:, :channels] + both[:, channels:]).astype(BF16)


def group_offsets(group):
    return [k for j in group for k in ((j, 26 - j) if j < 13 else (13,))]


def moments(totals):
    count = totals[2:3]
    mean_row = totals[0:1] / count
    square = totals[1:2] / count
    return mean_row, lax.rsqrt(square - mean_row * mean_row + EPSILON), count


def add_sums(out_ref, first, second, count):
    third = jnp.broadcast_to(count, first.shape)
    rows = [first, second, third, jnp.zeros((out_ref.shape[0] - 3, first.shape[1]), F32)]
    out_ref[...] += jnp.concatenate(rows, axis=0)


def norm_back(upstream, centred, live, inv_std, gain_row, back, count):
    return live * (inv_std * gain_row) * (upstream - back[0:1] / count - centred * (back[1:2] / count))


def parent_rows(table, fine_rows):
    first = jnp.min(table, axis=0, keepdims=True)
    children = jnp.sum((table < fine_rows).astype(jnp.int32), axis=0, keepdims=True)
    return first, first + children


def parent_hits(first, last, at, size):
    places = lax.broadcasted_iota(jnp.int16, (size, first.shape[1]), 0) + jnp.int16(at)
    inside = (places >= first.astype(jnp.int16)) & (places < last.astype(jnp.int16))
    return jnp.where(inside, jnp.bfloat16(1), jnp.bfloat16(0))


def pack_kernel(
    where_ref, feats_hbm, down_hbm, weight_hbm,
    feats_send, table_send, feats_own, table_own, weight_ref, arrivals,
):
    copies = [
        pltpu.make_async_copy(source, target, arrivals.at[i])
        for i, (source, target) in enumerate(
            (
                (feats_hbm.at[where_ref[4]], feats_send),
                (down_hbm.at[where_ref[4]], table_send),
                (down_hbm.at[where_ref[0]], table_own),
                (feats_hbm.at[where_ref[0]], feats_own),
                (weight_hbm, weight_ref),
            )
        )
    ]
    for copy in copies:
        copy.start()
    for copy in copies:
        copy.wait()


def down_rows(table, feats_ref, weight_ref, which_ref, spread_ref, parent_ref):
    in_channels, fine_rows = feats_ref.shape
    offsets, coarse_rows = table.shape
    first, last = parent_rows(table, fine_rows)
    rank = table - first
    numbers = lax.broadcasted_iota(jnp.int32, (offsets, coarse_rows), 0) + 1
    rows = [jnp.sum(jnp.where(rank == r, numbers, 0), axis=0, keepdims=True) for r in range(8)]
    safe_first = jnp.where(first < fine_rows, first, 0)
    rows += [(safe_first // 16) * 16, safe_first % 16] + [jnp.zeros_like(first)] * 6
    lookup = jnp.concatenate(rows, axis=0).astype(F32).astype(BF16)
    step = 512
    for at in range(0, fine_rows, step):
        parent_ref[at : at + step] = parent_hits(first, last, at, step)
    found = mm_t(lookup, parent_ref[...])
    place = lax.broadcasted_iota(jnp.int32, (8, fine_rows), 1).astype(F32) - (found[8:9] + found[9:10])
    column = lax.broadcasted_iota(jnp.int32, (8, fine_rows), 0).astype(F32)
    which = jnp.sum(jnp.where(column == place, found[:8], 0.0), axis=0, keepdims=True)
    which_ref[...] = jnp.broadcast_to(which, which_ref.shape)
    code = jnp.broadcast_to(which, (in_channels, fine_rows)).astype(BF16)
    feats = feats_ref[...]
    for k in range(offsets):
        spread_ref[in_channels * k : in_channels * (k + 1)] = jnp.where(
            code == jnp.bfloat16(k + 1), feats, jnp.zeros_like(feats)
        )
    kids = mm(spread_ref[...], parent_ref[...]).astype(BF16)
    hidden = jnp.transpose(mm(jnp.transpose(weight_ref[...]), kids))
    count = jnp.sum((last > first).astype(F32), axis=1, keepdims=True)
    return kids, hidden, count


def down_kernel(
    where_ref, feats_ref, table_ref, weight_ref, near_ref,
    hidden_ref, sums_ref, kids_ref, which_ref, near_own, near_send,
    spread_ref, parent_ref,
):
    for k in range(near_own.shape[0]):
        near_own[k : k + 1] = near_ref[k, pl.ds(where_ref[0], 1), :]
        near_send[k : k + 1] = near_ref[k, pl.ds(where_ref[4], 1), :]
    kids, hidden, count = down_rows(
        table_ref[...], feats_ref, weight_ref, which_ref, spread_ref, parent_ref
    )
    kids_ref[...] = kids
    hidden_ref[...] = hidden
    sums_ref[...] = jnp.zeros_like(sums_ref)
    add_sums(sums_ref, col_sum(hidden), col_sum(hidden * hidden), count)


def down_other_kernel(
    where_ref, feats_ref, table_ref, weight_ref, own_hidden, own_sums, own_kids, own_which, own_table,
    hidden_ref, sums_ref, kids_ref, which_ref, tables_ref,
    spread_ref, parent_ref,
):
    kids, hidden, count = down_rows(
        table_ref[...], feats_ref, weight_ref, which_ref.at[1], spread_ref, parent_ref
    )
    kids_ref[1] = kids
    hidden_ref[1] = hidden
    tables_ref[1] = table_ref[...]
    for both, own in ((kids_ref, own_kids), (hidden_ref, own_hidden), (which_ref, own_which), (tables_ref, own_table)):
        both[0] = own[...]
    sums_ref[...] = own_sums[...]
    add_sums(sums_ref, col_sum(hidden), col_sum(hidden * hidden), count)


def conv_all(source, near_ref, bucket, weight_ref):
    values = source.astype(F32)
    largest = jnp.max(jnp.max(jnp.abs(values), axis=0, keepdims=True), axis=1, keepdims=True)
    power = power_for(largest)
    scaled = values * power
    pair = two_parts(scaled)
    out = None
    for group in GROUPS:
        offsets = group_offsets(group)
        rows = [
            scaled.astype(BF16) if k == 13 else moved_rows(near_ref, bucket, 26 - k, pair)
            for k in offsets
        ]
        weight = jnp.concatenate([weight_ref[k] for k in offsets], axis=0)
        term = mm(jnp.concatenate(rows, axis=1), weight)
        out = term if out is None else out + term
    return out * (1.0 / power)


def each_bucket(count, body, unrolled):
    if unrolled:
        for b in range(count):
            body(b)
        return

    def step(b, carry):
        body(b)
        return carry

    lax.fori_loop(0, count, step, 0)


def near_kernel(where_ref, own_ref, other_ref, near_ref):
    near_ref[0] = own_ref[...]
    near_ref[1] = other_ref[...]


def forward_kernel(norm_at, rounded, where_ref, hidden_ref, near_ref, weight_ref, scale_ref, shift_ref, *refs):
    part_refs, (act_ref, next_ref, sums_ref) = refs[:-3], refs[-3:]
    mean_row, inv_std, _ = moments(sum_refs(part_refs))
    sums_ref[...] = jnp.zeros_like(sums_ref)

    def bucket(b):
        live, count = live_mask(near_ref, b, hidden_ref.shape[2])
        centred = (hidden_ref[b] - mean_row) * inv_std
        value = centred * scale_ref[norm_at : norm_at + 1] + shift_ref[norm_at : norm_at + 1]
        act = (live * (value * sigmoid(value))).astype(BF16)
        act_ref[b] = act
        hidden = conv_all(act, near_ref, b, weight_ref)
        if rounded:
            hidden = hidden.astype(BF16)
        next_ref[b] = hidden
        hidden = hidden.astype(F32)
        add_sums(sums_ref, col_sum(hidden), col_sum(hidden * hidden), count)

    each_bucket(hidden_ref.shape[0], bucket, UNROLL_FORWARD)


def grad_kernel(where_ref, grad_ref, own_ref, send_ref):
    own_ref[...] = grad_ref[where_ref[0]]
    send_ref[...] = grad_ref[where_ref[4]]


def output_kernel(where_ref, hidden_ref, act_ref, own_grad, other_grad, near_ref, scale_ref, shift_ref, *refs):
    part_refs, (own_ref, send_ref, slope_ref, sums_ref) = refs[:-4], refs[-4:]
    mean_row, inv_std, _ = moments(sum_refs(part_refs))
    sums_ref[...] = jnp.zeros_like(sums_ref)
    for b, (grad_ref, features_ref) in enumerate(((own_grad, own_ref), (other_grad, send_ref))):
        live, count = live_mask(near_ref, b, hidden_ref.shape[2])
        centred = (hidden_ref[b].astype(F32) - mean_row) * inv_std
        value = centred * scale_ref[2:3] + shift_ref[2:3] + act_ref[b].astype(F32)
        gate = sigmoid(value)
        features_ref[...] = (live * (value * gate)).astype(BF16)
        upstream = grad_ref[...].astype(F32) * live * (gate * (1.0 + value * (1.0 - gate)))
        slope_ref[b] = upstream
        add_sums(sums_ref, col_sum(upstream), col_sum(upstream * centred), count)


def put_halves(where_ref, grad_ref, keep_ref, send_ref):
    half = keep_ref.shape[0]
    core = where_ref[1]
    keep_ref[...] = grad_ref[pl.ds(pl.multiple_of(core * half, 16), half)].astype(BF16)
    send_ref[...] = grad_ref[pl.ds(pl.multiple_of((1 - core) * half, 16), half)].astype(BF16)


def backward_kernel(norm_at, with_skip, ways, where_ref, *refs):
    upstream_ref, hidden_ref, lower_ref, act_ref, near_ref, weight_ref, scale_ref, shift_ref = refs[:8]
    own, back, low = (sum_refs(refs[8 + i * ways : 8 + (i + 1) * ways]) for i in range(3))
    rest = refs[8 + 3 * ways :]
    next_ref, sums_ref, keep_ref, send_ref, grad_ref = rest[-5:]
    mean_row, inv_std, count = moments(own)
    low_mean, low_std, _ = moments(low)
    channels = hidden_ref.shape[2]
    sums_ref[...] = jnp.zeros_like(sums_ref)
    grad_ref[...] = jnp.zeros_like(grad_ref)

    def bucket(b):
        live, own_count = live_mask(near_ref, b, channels)
        centred = (hidden_ref[b].astype(F32) - mean_row) * inv_std
        rows_grad = norm_back(
            upstream_ref[b], centred, live, inv_std, scale_ref[norm_at : norm_at + 1], back, count
        ).astype(BF16)
        act_t = jnp.transpose(act_ref[b])
        values = rows_grad.astype(F32)
        power = power_for(jnp.max(jnp.abs(values), axis=0, keepdims=True))
        undo = 1.0 / power
        undo_low = undo.astype(BF16)
        scaled = values * power
        pair = two_parts(scaled)
        below = None
        for group in GROUPS:
            offsets = group_offsets(group)
            rows = [
                scaled.astype(BF16) if k == 13 else moved_rows(near_ref, b, k, pair)
                for k in offsets
            ]
            moved = jnp.concatenate(rows, axis=1)
            weight = jnp.concatenate([weight_ref[k] * undo_low for k in offsets], axis=1)
            term = mm_t(moved, weight)
            below = term if below is None else below + term
            products = mm(act_t, moved)
            for i, k in enumerate(offsets):
                grad_ref[k * channels : (k + 1) * channels] += (
                    products[:, i * channels : (i + 1) * channels] * undo
                )
        below = below.astype(BF16).astype(F32)
        if with_skip:
            below = below + rest[0][b].astype(BF16).astype(F32)
        low_centred = (lower_ref[b] - low_mean) * low_std
        value = low_centred * scale_ref[norm_at - 1 : norm_at] + shift_ref[norm_at - 1 : norm_at]
        gate = sigmoid(value)
        upstream = below * live * (gate * (1.0 + value * (1.0 - gate)))
        next_ref[b] = upstream
        add_sums(sums_ref, col_sum(upstream), col_sum(upstream * low_centred), own_count)

    each_bucket(hidden_ref.shape[0], bucket, UNROLL_BACKWARD)
    put_halves(where_ref, grad_ref, keep_ref, send_ref)


def last_kernel(ways, where_ref, upstream_ref, hidden_ref, kids_ref, near_ref, scale_ref, *refs):
    rows_ref, keep_ref, send_ref, norms_ref, grad_ref = refs[4 * ways :]
    mean_row, inv_std, count = moments(sum_refs(refs[:ways]))
    backs = [sum_refs(refs[i * ways : (i + 1) * ways]) for i in (1, 2, 3)]
    back = backs[0]
    rows = [totals[0:2] for totals in backs]
    norms_ref[...] = jnp.concatenate(rows + [jnp.zeros_like(rows[0])], axis=0)
    channels = hidden_ref.shape[2]
    used = kids_ref.shape[1]
    if grad_ref.shape[0] > used:
        grad_ref[used:] = jnp.zeros((grad_ref.shape[0] - used, channels), F32)
    total = None
    for b in range(hidden_ref.shape[0]):
        live, _ = live_mask(near_ref, b, channels)
        centred = (hidden_ref[b] - mean_row) * inv_std
        rows_grad = norm_back(
            upstream_ref[b], centred, live, inv_std, scale_ref[0:1], back, count
        ).astype(BF16)
        rows_ref[b] = rows_grad
        product = mm(kids_ref[b], rows_grad)
        total = product if total is None else total + product
    grad_ref[:used] = total
    put_halves(where_ref, grad_ref, keep_ref, send_ref)


def input_kernel(where_ref, rows_ref, which_ref, tables_ref, weight_ref, own_ref, send_ref):
    in_channels, fine_rows = own_ref.shape
    step = 256
    for b, input_ref in enumerate((own_ref, send_ref)):
        pieces = mm_t(weight_ref[...], rows_ref[b]).astype(BF16)
        first, last = parent_rows(tables_ref[b], fine_rows)
        for at in range(0, fine_rows, step):
            full = mm_t(pieces, parent_hits(first, last, at, step))
            code = jnp.broadcast_to(which_ref[b, 0:1, at : at + step], (in_channels, step))
            out = jnp.zeros((in_channels, step), F32)
            for k in range(full.shape[0] // in_channels):
                out = out + jnp.where(code == float(k + 1), full[in_channels * k : in_channels * (k + 1)], 0.0)
            input_ref[:, at : at + step] = out.astype(BF16)


def place_outputs_kernel(where_ref, own_features, other_features, own_input, other_input, features, inputs, leaving):
    copies = [
        pltpu.make_async_copy(source, target.at[place], leaving.at[i])
        for i, (source, target, place) in enumerate(
            (
                (own_features, features, where_ref[1]),
                (other_features, features, 1 - where_ref[1]),
                (own_input, inputs, where_ref[1]),
                (other_input, inputs, 1 - where_ref[1]),
            )
        )
    ]
    for copy in copies:
        copy.start()
    for copy in copies:
        copy.wait()


def split_kernel(sections, depths, parts, where_ref, *refs):
    pairs, outs = refs[: 2 * len(parts)], refs[2 * len(parts) :]
    total = sum(parts)
    for j in range(sections):
        block = where_ref[2] ^ j
        base = 0
        for i, size in enumerate(parts):
            wide = depths * size
            rows = pl.ds(pl.multiple_of(block * wide, 16), wide)
            both = (pairs[2 * i][rows].astype(F32) + pairs[2 * i + 1][rows].astype(F32)).astype(BF16)
            for z in range(depths):
                outs[j][z * total + base : z * total + base + size] = both[z * size : (z + 1) * size]
            base += size


def spread_kernel(depths, sources, where_ref, *refs):
    blocks, halves, outs = refs[:sources], refs[sources : sources + 2], refs[sources + 2 :]
    small = halves[0].shape[0] // depths
    size = outs[0].shape[0] - small
    for j in range(depths):
        place = where_ref[3] ^ j
        rows = pl.ds(pl.multiple_of(place * size, 16), size)
        outs[j][:size] = tree_sum([ref[rows].astype(F32) for ref in blocks]).astype(BF16)
        rows = pl.ds(pl.multiple_of(place * small, 16), small)
        outs[j][size:] = (halves[0][rows].astype(F32) + halves[1][rows].astype(F32)).astype(BF16)


def add_kernel(where_ref, *refs):
    refs[-1][...] = sum_refs(refs[:-1]).astype(BF16)


def high_and_low(exact):
    high = exact.astype(BF16)
    low = (exact - high.astype(F32)).astype(BF16)
    return jnp.concatenate([high, low], axis=0)


def one_value(high_low):
    rows = high_low.shape[0] // 2
    return high_low[:rows].astype(F32) + high_low[rows:].astype(F32)


def join_kernel(small, where_ref, *refs):
    pieces, norm_refs, out_ref = refs[:-3], refs[-3:-1], refs[-1]
    size = pieces[0].shape[0] - small
    base = len(pieces) * size
    for j, ref in zip(partners(len(pieces)), pieces):
        place = where_ref[3] ^ j
        out_ref[pl.ds(pl.multiple_of(place * size, 16), size)] = ref[:size]
        out_ref[pl.ds(pl.multiple_of(base + place * small, 16), small)] = ref[size:]
    out_ref[base + len(pieces) * small :] = high_and_low(sum_refs(norm_refs))


def settle_blocks(items, parts, depths, sections, where_ref, pieces, outs, staging, leaving):
    total = sum(parts)
    copies = []
    for n, ((flip, j), piece) in enumerate(zip(items, pieces)):
        core = 1 - where_ref[1] if flip else where_ref[1]
        base = 0
        for i, size in enumerate(parts):
            wide = depths * size
            block = core * sections + (where_ref[2] ^ j)
            slot = staging.at[n, i]
            for z in range(depths):
                slot[z * size : (z + 1) * size] = piece[z * total + base : z * total + base + size].astype(F32)
            base += size
            last, rest = divmod(outs[i].shape[0], wide)
            start = pl.multiple_of(block * wide, 16)
            copies.append((block < last, pltpu.make_async_copy(slot, outs[i].at[pl.ds(start, wide)], leaving.at[n, i])))
            if rest:
                part_copy = pltpu.make_async_copy(
                    slot.at[pl.ds(0, rest)], outs[i].at[pl.ds(last * wide, rest)], leaving.at[n, i]
                )
                copies.append((block == last, part_copy))
    for when, copy in copies:
        pl.when(when)(copy.start)
    return copies


def finish(copies):
    for when, copy in copies:
        pl.when(when)(copy.wait)


def settle_rest_kernel(items, parts, depths, small, with_norms, where_ref, *refs):
    sections = len(items)
    pieces = refs[:sections]
    staging, down_staging, leaving, down_leaving = refs[-4:]
    outs = refs[-9:-4] if with_norms else refs[-7:-4]
    first, second, down = outs[:3]
    copies = settle_blocks(items, parts, depths, sections, where_ref, pieces, (first, second), staging, leaving)
    base = depths * sum(parts)
    wide = depths * small
    core = where_ref[1] if with_norms else 1 - where_ref[1]
    down_staging[...] = tree_sum([piece[base : base + wide].astype(F32) for piece in pieces])
    down_copy = pltpu.make_async_copy(
        down_staging, down.at[pl.ds(pl.multiple_of(core * wide, 16), wide)], down_leaving.at[0]
    )
    down_copy.start()
    if with_norms:
        sums = tree_sum([one_value(piece[base + wide :]) for piece in pieces])
        outs[4][...] = jnp.concatenate([sums[2 * t : 2 * t + 1] for t in range(3)], axis=0)
        outs[3][...] = jnp.concatenate([sums[2 * t + 1 : 2 * t + 2] for t in range(3)], axis=0)
    finish(copies)
    down_copy.wait()


def run(kernel, where, operands, outs, scratch=(), hbm_in=(), hbm_out=(), aliases=None, flops=0):
    def place(i, hbm):
        return pltpu.HBM if i in hbm else pltpu.VMEM

    return pl.pallas_call(
        kernel,
        in_specs=[pl.BlockSpec(memory_space=pltpu.SMEM)]
        + [pl.BlockSpec(memory_space=place(i, hbm_in)) for i in range(len(operands))],
        out_specs=[pl.BlockSpec(memory_space=place(i, hbm_out)) for i in range(len(outs))],
        out_shape=outs,
        scratch_shapes=list(scratch),
        input_output_aliases=aliases or {},
        compiler_params=pltpu.CompilerParams(vmem_limit_bytes=VMEM_BYTES),
        cost_estimate=pl.CostEstimate(flops=flops, bytes_accessed=(1 << 20) if flops else 1, transcendentals=0),
    )(where, *operands)


def swapped(value, axis, step):
    count = lax.axis_size(axis)
    return lax.ppermute(value, axis, [(i, i ^ step) for i in range(count)])


def partners(count):
    order = [0]
    step = 1
    while len(order) < count:
        order = order + [j ^ (count - step) for j in order]
        step *= 2
    return order


def from_depths(values):
    return [values[j] if j == 0 else swapped(values[j], "dp", 2 * j) for j in partners(len(values))]


def from_sections(values):
    return [values[j] if j == 0 else swapped(values[j], "section", j) for j in partners(len(values))]


def depth_sums(value):
    steps = range(2, lax.axis_size("dp"), 2)
    return [value] + [swapped(value, "dp", step) for step in steps]


def local(
    voxel_feats, down_map, neighbours, w_down, w_first, w_second, bn_scale, bn_shift, out_grad
):
    sections = lax.axis_size("section")
    depths = lax.axis_size("dp") // 2
    mine = voxel_feats.shape[0] // sections
    section, bucket = lax.axis_index("section"), lax.axis_index("dp")
    core = bucket % 2
    base = section * mine
    where = jnp.stack([base + core, core, section, bucket // 2, base + 1 - core]).astype(jnp.int32)
    voxel_feats = jnp.swapaxes(voxel_feats, 1, 2)
    near = jnp.swapaxes(neighbours, 0, 1)
    in_channels, fine_rows = voxel_feats.shape[1:]
    coarse_rows = neighbours.shape[2]
    channels = w_first.shape[2]
    offsets = down_map.shape[1]
    wide = offsets * in_channels
    flat_down = w_down.reshape(wide, channels)
    shape = jax.ShapeDtypeStruct
    rows_f32 = shape((mine, coarse_rows, channels), F32)
    rows_bf16 = shape((mine, coarse_rows, channels), BF16)
    one_bf16 = shape((coarse_rows, channels), BF16)
    sums = shape((8, channels), F32)
    table = shape((offsets, coarse_rows), jnp.int32)
    near_one = shape((w_first.shape[0], coarse_rows), jnp.int32)
    conv_flops = 8 * mine * w_first.shape[0] * coarse_rows * coarse_rows * channels

    def in_hbm(value):
        return pltpu.with_memory_space_constraint(value, pltpu.HBM)

    def cores(value):
        return swapped(value, "dp", 1)

    feats_hbm, down_hbm = in_hbm(voxel_feats), in_hbm(down_map)
    feats_one = shape((in_channels, fine_rows), BF16)
    send_feats, send_table, own_feats, own_table, weight_down = run(
        pack_kernel, where, [feats_hbm, down_hbm, in_hbm(flat_down)],
        [feats_one, table, feats_one, table, shape((wide, channels), BF16)],
        [pltpu.SemaphoreType.DMA((5,))], hbm_in=(0, 1, 2),
    )
    got_feats, got_table = cores(send_feats), cores(send_table)
    down_scratch = [pltpu.VMEM((wide, fine_rows), BF16), pltpu.VMEM((fine_rows, coarse_rows), BF16)]
    own_hidden, own_sums, own_kids, own_which, near_own, near_send = run(
        down_kernel, where,
        [own_feats, own_table, weight_down, near],
        [
            shape((coarse_rows, channels), F32), sums, shape((wide, coarse_rows), BF16),
            shape((8, fine_rows), F32), near_one, near_one,
        ],
        down_scratch,
        flops=2 * 10**9,
    )
    hidden_zero, part_zero, kids, which, tables = run(
        down_other_kernel, where,
        [got_feats, got_table, weight_down, own_hidden, own_sums, own_kids, own_which, own_table],
        [
            rows_f32, sums, shape((mine, wide, coarse_rows), BF16), shape((mine, 8, fine_rows), F32),
            shape((mine, offsets, coarse_rows), jnp.int32),
        ],
        down_scratch,
        flops=2 * 10**9,
    )
    stats_zero = depth_sums(part_zero)
    ways = len(stats_zero)
    (nears,) = run(
        near_kernel, where, [near_own, cores(near_send)],
        [shape((mine, w_first.shape[0], coarse_rows), jnp.int32)],
    )
    act_zero, hidden_one, part_one = run(
        functools.partial(forward_kernel, 0, False), where,
        [hidden_zero, nears, w_first, bn_scale, bn_shift] + stats_zero,
        [rows_bf16, rows_f32, sums],
        flops=conv_flops,
    )
    stats_one = depth_sums(part_one)
    grad_own, grad_send = run(grad_kernel, where, [out_grad], [one_bf16, one_bf16])
    grad_other = cores(grad_send)
    act_one, hidden_two, part_two = run(
        functools.partial(forward_kernel, 1, True), where,
        [hidden_one, nears, w_second, bn_scale, bn_shift] + stats_one,
        [rows_bf16, rows_bf16, sums],
        flops=conv_flops,
    )
    stats_two = depth_sums(part_two)
    features_own, features_send, up_two, back_part = run(
        output_kernel, where,
        [hidden_two, act_zero, grad_own, grad_other, nears, bn_scale, bn_shift] + stats_two,
        [one_bf16, one_bf16, rows_f32, sums],
        flops=10**9,
    )
    back_two = depth_sums(back_part)

    def part_rows(rows, pieces):
        return -(-rows // (pieces * 16)) * 16

    def half_shape(rows):
        return shape((rows, channels), BF16)

    def accumulator(rows):
        return [pltpu.VMEM((2 * rows, channels), F32)]

    blocks = sections * depths
    conv_rows = w_first.shape[0] * channels
    parts = [part_rows(conv_rows, 2 * blocks)] * 2
    small = part_rows(wide, 2 * depths)
    total = sum(parts)
    half = half_shape(blocks * parts[0])
    small_half = half_shape(depths * small)
    up_one, back_part, keep_second, send_second = run(
        functools.partial(backward_kernel, 2, False, ways), where,
        [up_two, hidden_two, hidden_one, act_one, nears, w_second, bn_scale, bn_shift]
        + stats_two + back_two + stats_one,
        [rows_f32, sums, half, half],
        accumulator(half.shape[0]),
        flops=conv_flops,
    )
    back_one = depth_sums(back_part)
    got_second = cores(send_second)
    features_other = cores(features_send)
    features_other, up_one = lax.optimization_barrier((features_other, up_one))
    up_zero, back_part, keep_first, send_first = run(
        functools.partial(backward_kernel, 1, True, ways), where,
        [up_one, hidden_one, hidden_zero, act_zero, nears, w_first, bn_scale, bn_shift]
        + stats_one + back_one + stats_zero + [up_two],
        [rows_f32, sums, half, half],
        accumulator(half.shape[0]),
        flops=conv_flops,
    )
    got_first = cores(send_first)
    section_out = run(
        functools.partial(split_kernel, sections, depths, parts), where,
        [keep_second, got_second, keep_first, got_first],
        [half_shape(depths * total)] * sections,
    )
    arrived = from_sections(section_out)
    back_zero = depth_sums(back_part)
    rows_zero, keep_down, send_down, norm_rows = run(
        functools.partial(last_kernel, ways), where,
        [up_zero, hidden_zero, kids, nears, bn_scale] + stats_zero + back_zero + back_one + back_two,
        [rows_bf16, small_half, small_half, sums],
        accumulator(small_half.shape[0]),
        flops=10**9,
    )
    got_down = cores(send_down)
    depth_out = run(
        functools.partial(spread_kernel, depths, sections), where, arrived + [keep_down, got_down],
        [half_shape(total + small)] * depths,
    )
    arrived = from_depths(depth_out)
    (summed,) = run(add_kernel, where, arrived, [half_shape(total + small)])
    arrived = from_depths([summed] * depths)
    (joined,) = run(
        functools.partial(join_kernel, small), where, arrived + [norm_rows, cores(norm_rows)],
        [half_shape(depths * (total + small) + 16)],
    )
    joined, rows_zero = lax.optimization_barrier((joined, rows_zero))
    arrived = from_sections([joined] * sections)
    across = cores(joined)
    input_own, input_send = run(
        input_kernel, where, [rows_zero, which, tables, weight_down], [feats_one, feats_one],
    )
    features, input_grad = run(
        place_outputs_kernel, where,
        [features_own, features_other, input_own, cores(input_send)],
        [rows_bf16, shape((mine, in_channels, fine_rows), BF16)],
        [pltpu.SemaphoreType.DMA((4,))],
        hbm_out=(0, 1),
    )
    block = (2, depths * parts[0], channels)
    convs = [shape((conv_rows, channels), F32)] * 2
    down_shape = shape((wide, channels), F32)
    norms = shape(bn_scale.shape, F32)

    def staging(count):
        return [pltpu.VMEM((count,) + block, F32)]

    def rest_scratch():
        return staging(sections) + [
            pltpu.VMEM((depths * small, channels), F32),
            pltpu.SemaphoreType.DMA((sections, 2)),
            pltpu.SemaphoreType.DMA((1,)),
        ]

    arrived, features, input_grad = lax.optimization_barrier((arrived, features, input_grad))
    others = [across] + [cores(piece) for piece in arrived[1:]]
    items = [(False, j) for j in partners(sections)]
    grad_second, grad_first, grad_down, grad_scale, grad_shift = run(
        functools.partial(settle_rest_kernel, items, parts, depths, small, True), where,
        arrived, convs + [down_shape, norms, norms], rest_scratch(),
        hbm_out=(0, 1, 2), flops=10**9,
    )
    items = [(True, j) for j in partners(sections)]
    grad_second, grad_first, grad_down = run(
        functools.partial(settle_rest_kernel, items, parts, depths, small, False), where,
        others + [grad_second, grad_first, grad_down], convs + [down_shape], rest_scratch(),
        hbm_in=(sections, sections + 1, sections + 2), hbm_out=(0, 1, 2),
        aliases={1 + sections: 0, 2 + sections: 1, 3 + sections: 2}, flops=10**9,
    )
    return (
        features,
        jnp.swapaxes(input_grad, 1, 2),
        grad_down.reshape(w_down.shape),
        grad_first.reshape(w_first.shape),
        grad_second.reshape(w_second.shape),
        grad_scale,
        grad_shift,
    )


def solution(mesh):
    in_specs = (
        P(None, "dp", None),
        P(None, None, "dp"),
        P(None, None, "dp"),
        P(),
        P(),
        P(),
        P(),
        P(),
        P(None, "dp", None),
    )
    out_specs = (P("section", "dp", None), P("section", "dp", None), P(), P(), P(), P(), P())
    return jax.shard_map(local, mesh=mesh, in_specs=in_specs, out_specs=out_specs, check_vma=False)
```

```python
import functools

import jax
import jax.numpy as jnp
from jax import lax
from jax.experimental import pallas as pl
from jax.experimental.pallas import tpu as pltpu
from jax.sharding import PartitionSpec as P

EPSILON = 1e-05
F32 = jnp.float32
BF16 = jnp.bfloat16
F8 = jnp.float8_e4m3fn
VMEM_BYTES = 40 << 20
GROUPS = ((0, 1), (2, 3), (4, 5), (6, 7), (8, 9), (10, 11), (12, 13))


def mm(left, right):
    return jnp.dot(left, right, preferred_element_type=F32)


def mm_t(left, right):
    return lax.dot_general(left, right, (((1,), (1,)), ((), ())), preferred_element_type=F32)


def col_sum(values):
    return jnp.sum(values, axis=0, keepdims=True)


def sigmoid(values):
    return 1.0 / (1.0 + jnp.exp(-values))


def tree_sum(parts):
    parts = list(parts)
    while len(parts) > 1:
        parts = [parts[i] + parts[i + 1] for i in range(0, len(parts), 2)]
    return parts[0]


def sum_refs(refs):
    return tree_sum([ref[...].astype(F32) for ref in refs])


def hits(index_row, rows):
    places = lax.broadcasted_iota(jnp.int16, (rows, index_row.shape[1]), 0)
    return jnp.where(places == index_row, jnp.bfloat16(1), jnp.bfloat16(0)).astype(F8)


def live_mask(near_ref, bucket, channels):
    rows = near_ref.shape[2]
    centre = near_ref[bucket, 13:14, :]
    count = jnp.sum((centre < rows).astype(F32), axis=1, keepdims=True)
    places = lax.broadcasted_iota(jnp.int32, (rows, channels), 0).astype(F32)
    return (places < count).astype(F32), count


def power_for(largest):
    power = jnp.full_like(largest, 2.0**-60)
    for exponent in (64, 32, 16, 8, 4, 2, 1):
        raised = power * (2.0**exponent)
        power = jnp.where(largest * raised <= 224.0, raised, power)
    return power


def two_parts(scaled):
    high = scaled.astype(F8)
    low = (scaled - high.astype(F32)).astype(F8)
    return jnp.concatenate([high, low], axis=1)


def moved_rows(near_ref, bucket, offset, pair):
    row = near_ref[bucket, offset : offset + 1, :]
    both = mm(hits(row.astype(jnp.int16), row.shape[1]), pair)
    channels = pair.shape[1] // 2
    return (both[:, :channels] + both[:, channels:]).astype(BF16)


def group_offsets(group):
    return [k for j in group for k in ((j, 26 - j) if j < 13 else (13,))]


def moments(totals):
    count = totals[2:3]
    mean_row = totals[0:1] / count
    square = totals[1:2] / count
    return mean_row, lax.rsqrt(square - mean_row * mean_row + EPSILON), count


def add_sums(out_ref, first, second, count):
    third = jnp.broadcast_to(count, first.shape)
    rows = [first, second, third, jnp.zeros((out_ref.shape[0] - 3, first.shape[1]), F32)]
    out_ref[...] += jnp.concatenate(rows, axis=0)


def norm_back(upstream, centred, live, inv_std, gain_row, back, count):
    return live * (inv_std * gain_row) * (upstream - back[0:1] / count - centred * (back[1:2] / count))


def parent_rows(table, fine_rows):
    first = jnp.min(table, axis=0, keepdims=True)
    children = jnp.sum((table < fine_rows).astype(jnp.int32), axis=0, keepdims=True)
    return first, first + children


def parent_hits(first, last, at, size):
    places = lax.broadcasted_iota(jnp.int16, (size, first.shape[1]), 0) + jnp.int16(at)
    inside = (places >= first.astype(jnp.int16)) & (places < last.astype(jnp.int16))
    return jnp.where(inside, jnp.bfloat16(1), jnp.bfloat16(0))


def pack_kernel(
    where_ref, feats_hbm, down_hbm, weight_hbm,
    send_ref, feats_own, table_own, weight_ref, table_ref, arrivals,
):
    channels, fine_rows = feats_own.shape
    copies = [
        pltpu.make_async_copy(source, target, arrivals.at[i])
        for i, (source, target) in enumerate(
            (
                (down_hbm.at[where_ref[4]], table_ref),
                (feats_hbm.at[where_ref[4]], send_ref.at[pl.ds(0, channels)]),
                (down_hbm.at[where_ref[0]], table_own),
                (feats_hbm.at[where_ref[0]], feats_own),
                (weight_hbm, weight_ref),
            )
        )
    ]
    for copy in copies:
        copy.start()
    copies[0].wait()
    table = table_ref[...]
    rows = [table // 16, table % 16]
    rows.append(jnp.zeros((table.shape[0], fine_rows - 2 * table.shape[1]), jnp.int32))
    rows = jnp.concatenate(rows, axis=1).astype(F32)
    rows = jnp.concatenate([rows, jnp.zeros((16 - table.shape[0], fine_rows), F32)], axis=0)
    send_ref[channels:] = rows.astype(BF16)
    for copy in copies[1:]:
        copy.wait()


def down_rows(table, feats_ref, weight_ref, which_ref, spread_ref, parent_ref):
    in_channels, fine_rows = feats_ref.shape
    offsets, coarse_rows = table.shape
    first, last = parent_rows(table, fine_rows)
    rank = table - first
    numbers = lax.broadcasted_iota(jnp.int32, (offsets, coarse_rows), 0) + 1
    rows = [jnp.sum(jnp.where(rank == r, numbers, 0), axis=0, keepdims=True) for r in range(8)]
    safe_first = jnp.where(first < fine_rows, first, 0)
    rows += [(safe_first // 16) * 16, safe_first % 16] + [jnp.zeros_like(first)] * 6
    lookup = jnp.concatenate(rows, axis=0).astype(F32).astype(BF16)
    step = 512
    for at in range(0, fine_rows, step):
        parent_ref[at : at + step] = parent_hits(first, last, at, step)
    found = mm_t(lookup, parent_ref[...])
    place = lax.broadcasted_iota(jnp.int32, (8, fine_rows), 1).astype(F32) - (found[8:9] + found[9:10])
    column = lax.broadcasted_iota(jnp.int32, (8, fine_rows), 0).astype(F32)
    which = jnp.sum(jnp.where(column == place, found[:8], 0.0), axis=0, keepdims=True)
    which_ref[...] = jnp.broadcast_to(which, which_ref.shape)
    code = jnp.broadcast_to(which, (in_channels, fine_rows)).astype(BF16)
    feats = feats_ref[...]
    for k in range(offsets):
        spread_ref[in_channels * k : in_channels * (k + 1)] = jnp.where(
            code == jnp.bfloat16(k + 1), feats, jnp.zeros_like(feats)
        )
    kids = mm(spread_ref[...], parent_ref[...]).astype(BF16)
    hidden = jnp.transpose(mm(jnp.transpose(weight_ref[...]), kids))
    count = jnp.sum((last > first).astype(F32), axis=1, keepdims=True)
    return kids, hidden, count


def down_kernel(
    where_ref, feats_ref, table_ref, weight_ref, near_ref,
    hidden_ref, sums_ref, kids_ref, which_ref, near_own, near_send,
    spread_ref, parent_ref,
):
    for k in range(near_own.shape[0]):
        near_own[k : k + 1] = near_ref[k, pl.ds(where_ref[0], 1), :]
        near_send[k : k + 1] = near_ref[k, pl.ds(where_ref[4], 1), :]
    kids, hidden, count = down_rows(
        table_ref[...], feats_ref, weight_ref, which_ref, spread_ref, parent_ref
    )
    kids_ref[...] = kids
    hidden_ref[...] = hidden
    sums_ref[...] = jnp.zeros_like(sums_ref)
    add_sums(sums_ref, col_sum(hidden), col_sum(hidden * hidden), count)


def down_other_kernel(
    where_ref, got_ref, weight_ref, own_hidden, own_sums, own_kids, own_which, own_table,
    hidden_ref, sums_ref, kids_ref, which_ref, tables_ref,
    spread_ref, parent_ref,
):
    offsets, coarse_rows = own_table.shape
    channels = got_ref.shape[0] - 16
    coded = got_ref[channels:].astype(F32)[:offsets, : 2 * coarse_rows]
    table = (coded[:, :coarse_rows] * 16.0 + coded[:, coarse_rows:]).astype(jnp.int32)
    kids, hidden, count = down_rows(
        table, got_ref.at[pl.ds(0, channels)], weight_ref, which_ref.at[1], spread_ref, parent_ref
    )
    kids_ref[1] = kids
    hidden_ref[1] = hidden
    tables_ref[1] = table
    for both, own in ((kids_ref, own_kids), (hidden_ref, own_hidden), (which_ref, own_which), (tables_ref, own_table)):
        both[0] = own[...]
    sums_ref[...] = own_sums[...]
    add_sums(sums_ref, col_sum(hidden), col_sum(hidden * hidden), count)


def conv_all(source, near_ref, bucket, weight_ref):
    values = source.astype(F32)
    largest = jnp.max(jnp.max(jnp.abs(values), axis=0, keepdims=True), axis=1, keepdims=True)
    power = power_for(largest)
    scaled = values * power
    pair = two_parts(scaled)
    out = None
    for group in GROUPS:
        offsets = group_offsets(group)
        rows = [
            scaled.astype(BF16) if k == 13 else moved_rows(near_ref, bucket, 26 - k, pair)
            for k in offsets
        ]
        weight = jnp.concatenate([weight_ref[k] for k in offsets], axis=0)
        term = mm(jnp.concatenate(rows, axis=1), weight)
        out = term if out is None else out + term
    return out * (1.0 / power)


def each_bucket(count, body, unrolled):
    if unrolled:
        for b in range(count):
            body(b)
        return

    def step(b, carry):
        body(b)
        return carry

    lax.fori_loop(0, count, step, 0)


def near_kernel(where_ref, own_ref, other_ref, near_ref):
    near_ref[0] = own_ref[...]
    near_ref[1] = other_ref[...]


def forward_kernel(norm_at, rounded, where_ref, hidden_ref, near_ref, weight_ref, scale_ref, shift_ref, *refs):
    part_refs, (act_ref, next_ref, sums_ref) = refs[:-3], refs[-3:]
    mean_row, inv_std, _ = moments(sum_refs(part_refs))
    sums_ref[...] = jnp.zeros_like(sums_ref)

    def bucket(b):
        live, count = live_mask(near_ref, b, hidden_ref.shape[2])
        centred = (hidden_ref[b] - mean_row) * inv_std
        value = centred * scale_ref[norm_at : norm_at + 1] + shift_ref[norm_at : norm_at + 1]
        act = (live * (value * sigmoid(value))).astype(BF16)
        act_ref[b] = act
        hidden = conv_all(act, near_ref, b, weight_ref)
        if rounded:
            hidden = hidden.astype(BF16)
        next_ref[b] = hidden
        hidden = hidden.astype(F32)
        add_sums(sums_ref, col_sum(hidden), col_sum(hidden * hidden), count)

    each_bucket(hidden_ref.shape[0], bucket, True)


def grad_kernel(where_ref, grad_ref, own_ref, send_ref):
    own_ref[...] = grad_ref[where_ref[0]]
    send_ref[...] = grad_ref[where_ref[4]]


def output_kernel(where_ref, hidden_ref, act_ref, own_grad, other_grad, near_ref, scale_ref, shift_ref, *refs):
    part_refs, (own_ref, send_ref, slope_ref, sums_ref) = refs[:-4], refs[-4:]
    mean_row, inv_std, _ = moments(sum_refs(part_refs))
    sums_ref[...] = jnp.zeros_like(sums_ref)
    for b, (grad_ref, features_ref) in enumerate(((own_grad, own_ref), (other_grad, send_ref))):
        live, count = live_mask(near_ref, b, hidden_ref.shape[2])
        centred = (hidden_ref[b].astype(F32) - mean_row) * inv_std
        value = centred * scale_ref[2:3] + shift_ref[2:3] + act_ref[b].astype(F32)
        gate = sigmoid(value)
        features_ref[...] = (live * (value * gate)).astype(BF16)
        upstream = grad_ref[...].astype(F32) * live * (gate * (1.0 + value * (1.0 - gate)))
        slope_ref[b] = upstream
        add_sums(sums_ref, col_sum(upstream), col_sum(upstream * centred), count)


def put_halves(where_ref, grad_ref, keep_ref, send_ref):
    half = keep_ref.shape[0]
    core = where_ref[1]
    keep_ref[...] = grad_ref[pl.ds(pl.multiple_of(core * half, 16), half)].astype(BF16)
    send_ref[...] = grad_ref[pl.ds(pl.multiple_of((1 - core) * half, 16), half)].astype(BF16)


def backward_kernel(norm_at, with_skip, ways, where_ref, *refs):
    upstream_ref, hidden_ref, lower_ref, act_ref, near_ref, weight_ref, scale_ref, shift_ref = refs[:8]
    own, back, low = (sum_refs(refs[8 + i * ways : 8 + (i + 1) * ways]) for i in range(3))
    rest = refs[8 + 3 * ways :]
    next_ref, sums_ref, keep_ref, send_ref, grad_ref = rest[-5:]
    mean_row, inv_std, count = moments(own)
    low_mean, low_std, _ = moments(low)
    channels = hidden_ref.shape[2]
    sums_ref[...] = jnp.zeros_like(sums_ref)
    grad_ref[...] = jnp.zeros_like(grad_ref)

    def bucket(b):
        live, own_count = live_mask(near_ref, b, channels)
        centred = (hidden_ref[b].astype(F32) - mean_row) * inv_std
        rows_grad = norm_back(
            upstream_ref[b], centred, live, inv_std, scale_ref[norm_at : norm_at + 1], back, count
        ).astype(BF16)
        act_t = jnp.transpose(act_ref[b])
        values = rows_grad.astype(F32)
        power = power_for(jnp.max(jnp.abs(values), axis=0, keepdims=True))
        undo = 1.0 / power
        undo_low = undo.astype(BF16)
        scaled = values * power
        pair = two_parts(scaled)
        below = None
        for group in GROUPS:
            offsets = group_offsets(group)
            rows = [
                scaled.astype(BF16) if k == 13 else moved_rows(near_ref, b, k, pair)
                for k in offsets
            ]
            moved = jnp.concatenate(rows, axis=1)
            weight = jnp.concatenate([weight_ref[k] * undo_low for k in offsets], axis=1)
            term = mm_t(moved, weight)
            below = term if below is None else below + term
            products = mm(act_t, moved)
            for i, k in enumerate(offsets):
                grad_ref[k * channels : (k + 1) * channels] += (
                    products[:, i * channels : (i + 1) * channels] * undo
                )
        below = below.astype(BF16).astype(F32)
        if with_skip:
            below = below + rest[0][b].astype(BF16).astype(F32)
        low_centred = (lower_ref[b] - low_mean) * low_std
        value = low_centred * scale_ref[norm_at - 1 : norm_at] + shift_ref[norm_at - 1 : norm_at]
        gate = sigmoid(value)
        upstream = below * live * (gate * (1.0 + value * (1.0 - gate)))
        next_ref[b] = upstream
        add_sums(sums_ref, col_sum(upstream), col_sum(upstream * low_centred), own_count)

    each_bucket(hidden_ref.shape[0], bucket, with_skip)
    put_halves(where_ref, grad_ref, keep_ref, send_ref)


def last_kernel(ways, where_ref, upstream_ref, hidden_ref, kids_ref, near_ref, scale_ref, *refs):
    rows_ref, keep_ref, send_ref, norms_ref, grad_ref = refs[4 * ways :]
    mean_row, inv_std, count = moments(sum_refs(refs[:ways]))
    backs = [sum_refs(refs[i * ways : (i + 1) * ways]) for i in (1, 2, 3)]
    back = backs[0]
    rows = [totals[0:2] for totals in backs]
    norms_ref[...] = jnp.concatenate(rows + [jnp.zeros_like(rows[0])], axis=0)
    channels = hidden_ref.shape[2]
    used = kids_ref.shape[1]
    if grad_ref.shape[0] > used:
        grad_ref[used:] = jnp.zeros((grad_ref.shape[0] - used, channels), F32)
    total = None
    for b in range(hidden_ref.shape[0]):
        live, _ = live_mask(near_ref, b, channels)
        centred = (hidden_ref[b] - mean_row) * inv_std
        rows_grad = norm_back(
            upstream_ref[b], centred, live, inv_std, scale_ref[0:1], back, count
        ).astype(BF16)
        rows_ref[b] = rows_grad
        product = mm(kids_ref[b], rows_grad)
        total = product if total is None else total + product
    grad_ref[:used] = total
    put_halves(where_ref, grad_ref, keep_ref, send_ref)


def input_kernel(where_ref, rows_ref, which_ref, tables_ref, weight_ref, own_ref, send_ref):
    in_channels, fine_rows = own_ref.shape
    step = 256
    for b, input_ref in enumerate((own_ref, send_ref)):
        pieces = mm_t(weight_ref[...], rows_ref[b]).astype(BF16)
        first, last = parent_rows(tables_ref[b], fine_rows)
        for at in range(0, fine_rows, step):
            full = mm_t(pieces, parent_hits(first, last, at, step))
            code = jnp.broadcast_to(which_ref[b, 0:1, at : at + step], (in_channels, step))
            out = jnp.zeros((in_channels, step), F32)
            for k in range(full.shape[0] // in_channels):
                out = out + jnp.where(code == float(k + 1), full[in_channels * k : in_channels * (k + 1)], 0.0)
            input_ref[:, at : at + step] = out.astype(BF16)


def place_outputs_kernel(where_ref, own_features, other_features, own_input, other_input, features, inputs, leaving):
    copies = [
        pltpu.make_async_copy(source, target.at[place], leaving.at[i])
        for i, (source, target, place) in enumerate(
            (
                (own_features, features, where_ref[1]),
                (other_features, features, 1 - where_ref[1]),
                (own_input, inputs, where_ref[1]),
                (other_input, inputs, 1 - where_ref[1]),
            )
        )
    ]
    for copy in copies:
        copy.start()
    for copy in copies:
        copy.wait()


def split_kernel(sections, depths, parts, where_ref, *refs):
    pairs, outs = refs[: 2 * len(parts)], refs[2 * len(parts) :]
    total = sum(parts)
    for j in range(sections):
        block = where_ref[2] ^ j
        base = 0
        for i, size in enumerate(parts):
            wide = depths * size
            rows = pl.ds(pl.multiple_of(block * wide, 16), wide)
            both = (pairs[2 * i][rows].astype(F32) + pairs[2 * i + 1][rows].astype(F32)).astype(BF16)
            for z in range(depths):
                outs[j][z * total + base : z * total + base + size] = both[z * size : (z + 1) * size]
            base += size


def spread_kernel(depths, sources, where_ref, *refs):
    blocks, halves, outs = refs[:sources], refs[sources : sources + 2], refs[sources + 2 :]
    small = halves[0].shape[0] // depths
    size = outs[0].shape[0] - small
    for j in range(depths):
        place = where_ref[3] ^ j
        rows = pl.ds(pl.multiple_of(place * size, 16), size)
        outs[j][:size] = tree_sum([ref[rows].astype(F32) for ref in blocks]).astype(BF16)
        rows = pl.ds(pl.multiple_of(place * small, 16), small)
        outs[j][size:] = (halves[0][rows].astype(F32) + halves[1][rows].astype(F32)).astype(BF16)


def add_kernel(where_ref, *refs):
    refs[-1][...] = sum_refs(refs[:-1]).astype(BF16)


def high_and_low(exact):
    high = exact.astype(BF16)
    low = (exact - high.astype(F32)).astype(BF16)
    return jnp.concatenate([high, low], axis=0)


def one_value(high_low):
    rows = high_low.shape[0] // 2
    return high_low[:rows].astype(F32) + high_low[rows:].astype(F32)


def join_kernel(small, where_ref, *refs):
    pieces, norm_refs, out_ref = refs[:-3], refs[-3:-1], refs[-1]
    size = pieces[0].shape[0] - small
    base = len(pieces) * size
    for j, ref in zip(partners(len(pieces)), pieces):
        place = where_ref[3] ^ j
        out_ref[pl.ds(pl.multiple_of(place * size, 16), size)] = ref[:size]
        out_ref[pl.ds(pl.multiple_of(base + place * small, 16), small)] = ref[size:]
    out_ref[base + len(pieces) * small :] = high_and_low(sum_refs(norm_refs))


def settle_blocks(items, parts, depths, sections, where_ref, pieces, outs, staging, leaving):
    total = sum(parts)
    copies = []
    for n, ((flip, j), piece) in enumerate(zip(items, pieces)):
        core = 1 - where_ref[1] if flip else where_ref[1]
        base = 0
        for i, size in enumerate(parts):
            wide = depths * size
            block = core * sections + (where_ref[2] ^ j)
            slot = staging.at[n, i]
            for z in range(depths):
                slot[z * size : (z + 1) * size] = piece[z * total + base : z * total + base + size].astype(F32)
            base += size
            last, rest = divmod(outs[i].shape[0], wide)
            start = pl.multiple_of(block * wide, 16)
            copies.append((block < last, pltpu.make_async_copy(slot, outs[i].at[pl.ds(start, wide)], leaving.at[n, i])))
            pl.when(copies[-1][0])(copies[-1][1].start)
            if rest:
                part_copy = pltpu.make_async_copy(
                    slot.at[pl.ds(0, rest)], outs[i].at[pl.ds(last * wide, rest)], leaving.at[n, i]
                )
                copies.append((block == last, part_copy))
                pl.when(copies[-1][0])(part_copy.start)
    return copies


def finish(copies):
    for when, copy in copies:
        pl.when(when)(copy.wait)


def settle_rest_kernel(items, parts, depths, small, with_norms, where_ref, *refs):
    sections = len(items)
    pieces = refs[:sections]
    staging, down_staging, leaving, down_leaving = refs[-4:]
    outs = refs[-9:-4] if with_norms else refs[-7:-4]
    first, second, down = outs[:3]
    copies = settle_blocks(items, parts, depths, sections, where_ref, pieces, (first, second), staging, leaving)
    base = depths * sum(parts)
    wide = depths * small
    core = where_ref[1] if with_norms else 1 - where_ref[1]
    down_staging[...] = tree_sum([piece[base : base + wide].astype(F32) for piece in pieces])
    down_copy = pltpu.make_async_copy(
        down_staging, down.at[pl.ds(pl.multiple_of(core * wide, 16), wide)], down_leaving.at[0]
    )
    down_copy.start()
    if with_norms:
        sums = tree_sum([one_value(piece[base + wide :]) for piece in pieces])
        outs[4][...] = jnp.concatenate([sums[2 * t : 2 * t + 1] for t in range(3)], axis=0)
        outs[3][...] = jnp.concatenate([sums[2 * t + 1 : 2 * t + 2] for t in range(3)], axis=0)
    finish(copies)
    down_copy.wait()


def run(kernel, where, operands, outs, scratch=(), hbm_in=(), hbm_out=(), aliases=None, flops=0):
    def place(i, hbm):
        return pltpu.HBM if i in hbm else pltpu.VMEM

    return pl.pallas_call(
        kernel,
        in_specs=[pl.BlockSpec(memory_space=pltpu.SMEM)]
        + [pl.BlockSpec(memory_space=place(i, hbm_in)) for i in range(len(operands))],
        out_specs=[pl.BlockSpec(memory_space=place(i, hbm_out)) for i in range(len(outs))],
        out_shape=outs,
        scratch_shapes=list(scratch),
        input_output_aliases=aliases or {},
        compiler_params=pltpu.CompilerParams(vmem_limit_bytes=VMEM_BYTES),
        cost_estimate=pl.CostEstimate(flops=flops, bytes_accessed=(1 << 20) if flops else 1, transcendentals=0),
    )(where, *operands)


def swapped(value, axis, step):
    count = lax.axis_size(axis)
    return lax.ppermute(value, axis, [(i, i ^ step) for i in range(count)])


def partners(count):
    order = [0]
    step = 1
    while len(order) < count:
        order = order + [j ^ (count - step) for j in order]
        step *= 2
    return order


def from_depths(values):
    return [values[j] if j == 0 else swapped(values[j], "dp", 2 * j) for j in partners(len(values))]


def from_sections(values):
    return [values[j] if j == 0 else swapped(values[j], "section", j) for j in partners(len(values))]


def depth_sums(value):
    steps = range(2, lax.axis_size("dp"), 2)
    return [value] + [swapped(value, "dp", step) for step in steps]


def local(
    voxel_feats, down_map, neighbours, w_down, w_first, w_second, bn_scale, bn_shift, out_grad
):
    sections = lax.axis_size("section")
    depths = lax.axis_size("dp") // 2
    mine = voxel_feats.shape[0] // sections
    section, bucket = lax.axis_index("section"), lax.axis_index("dp")
    core = bucket % 2
    base = section * mine
    where = jnp.stack([base + core, core, section, bucket // 2, base + 1 - core]).astype(jnp.int32)
    voxel_feats = jnp.swapaxes(voxel_feats, 1, 2)
    near = jnp.swapaxes(neighbours, 0, 1)
    in_channels, fine_rows = voxel_feats.shape[1:]
    coarse_rows = neighbours.shape[2]
    channels = w_first.shape[2]
    offsets = down_map.shape[1]
    wide = offsets * in_channels
    flat_down = w_down.reshape(wide, channels)
    shape = jax.ShapeDtypeStruct
    rows_f32 = shape((mine, coarse_rows, channels), F32)
    rows_bf16 = shape((mine, coarse_rows, channels), BF16)
    one_bf16 = shape((coarse_rows, channels), BF16)
    sums = shape((8, channels), F32)
    table = shape((offsets, coarse_rows), jnp.int32)
    near_one = shape((w_first.shape[0], coarse_rows), jnp.int32)
    conv_flops = 8 * mine * w_first.shape[0] * coarse_rows * coarse_rows * channels

    def in_hbm(value):
        return pltpu.with_memory_space_constraint(value, pltpu.HBM)

    def cores(value):
        return swapped(value, "dp", 1)

    feats_hbm, down_hbm = in_hbm(voxel_feats), in_hbm(down_map)
    feats_one = shape((in_channels, fine_rows), BF16)
    payload = shape((in_channels + 16, fine_rows), BF16)
    send_feats, own_feats, own_table, weight_down = run(
        pack_kernel, where, [feats_hbm, down_hbm, in_hbm(flat_down)],
        [payload, feats_one, table, shape((wide, channels), BF16)],
        [pltpu.VMEM((offsets, coarse_rows), jnp.int32), pltpu.SemaphoreType.DMA((5,))], hbm_in=(0, 1, 2),
    )
    got_feats = cores(send_feats)
    down_scratch = [pltpu.VMEM((wide, fine_rows), BF16), pltpu.VMEM((fine_rows, coarse_rows), BF16)]
    own_hidden, own_sums, own_kids, own_which, near_own, near_send = run(
        down_kernel, where,
        [own_feats, own_table, weight_down, near],
        [
            shape((coarse_rows, channels), F32), sums, shape((wide, coarse_rows), BF16),
            shape((8, fine_rows), F32), near_one, near_one,
        ],
        down_scratch,
        flops=2 * 10**9,
    )
    hidden_zero, part_zero, kids, which, tables = run(
        down_other_kernel, where,
        [got_feats, weight_down, own_hidden, own_sums, own_kids, own_which, own_table],
        [
            rows_f32, sums, shape((mine, wide, coarse_rows), BF16), shape((mine, 8, fine_rows), F32),
            shape((mine, offsets, coarse_rows), jnp.int32),
        ],
        down_scratch,
        flops=2 * 10**9,
    )
    stats_zero = depth_sums(part_zero)
    ways = len(stats_zero)
    (nears,) = run(
        near_kernel, where, [near_own, cores(near_send)],
        [shape((mine, w_first.shape[0], coarse_rows), jnp.int32)],
    )
    act_zero, hidden_one, part_one = run(
        functools.partial(forward_kernel, 0, False), where,
        [hidden_zero, nears, w_first, bn_scale, bn_shift] + stats_zero,
        [rows_bf16, rows_f32, sums],
        flops=conv_flops,
    )
    stats_one = depth_sums(part_one)
    grad_own, grad_send = run(grad_kernel, where, [out_grad], [one_bf16, one_bf16])
    grad_other = cores(grad_send)
    act_one, hidden_two, part_two = run(
        functools.partial(forward_kernel, 1, True), where,
        [hidden_one, nears, w_second, bn_scale, bn_shift] + stats_one,
        [rows_bf16, rows_bf16, sums],
        flops=conv_flops,
    )
    stats_two = depth_sums(part_two)
    features_own, features_send, up_two, back_part = run(
        output_kernel, where,
        [hidden_two, act_zero, grad_own, grad_other, nears, bn_scale, bn_shift] + stats_two,
        [one_bf16, one_bf16, rows_f32, sums],
        flops=10**9,
    )
    back_two = depth_sums(back_part)

    def part_rows(rows, pieces):
        return -(-rows // (pieces * 16)) * 16

    def half_shape(rows):
        return shape((rows, channels), BF16)

    def accumulator(rows):
        return [pltpu.VMEM((2 * rows, channels), F32)]

    blocks = sections * depths
    conv_rows = w_first.shape[0] * channels
    parts = [part_rows(conv_rows, 2 * blocks)] * 2
    small = part_rows(wide, 2 * depths)
    total = sum(parts)
    half = half_shape(blocks * parts[0])
    small_half = half_shape(depths * small)
    up_one, back_part, keep_second, send_second = run(
        functools.partial(backward_kernel, 2, False, ways), where,
        [up_two, hidden_two, hidden_one, act_one, nears, w_second, bn_scale, bn_shift]
        + stats_two + back_two + stats_one,
        [rows_f32, sums, half, half],
        accumulator(half.shape[0]),
        flops=conv_flops,
    )
    back_one = depth_sums(back_part)
    got_second = cores(send_second)
    features_other = cores(features_send)
    features_other, up_one = lax.optimization_barrier((features_other, up_one))
    up_zero, back_part, keep_first, send_first = run(
        functools.partial(backward_kernel, 1, True, ways), where,
        [up_one, hidden_one, hidden_zero, act_zero, nears, w_first, bn_scale, bn_shift]
        + stats_one + back_one + stats_zero + [up_two],
        [rows_f32, sums, half, half],
        accumulator(half.shape[0]),
        flops=conv_flops,
    )
    got_first = cores(send_first)
    section_out = run(
        functools.partial(split_kernel, sections, depths, parts), where,
        [keep_second, got_second, keep_first, got_first],
        [half_shape(depths * total)] * sections,
    )
    arrived = from_sections(section_out)
    back_zero = depth_sums(back_part)
    rows_zero, keep_down, send_down, norm_rows = run(
        functools.partial(last_kernel, ways), where,
        [up_zero, hidden_zero, kids, nears, bn_scale] + stats_zero + back_zero + back_one + back_two,
        [rows_bf16, small_half, small_half, sums],
        accumulator(small_half.shape[0]),
        flops=10**9,
    )
    got_down = cores(send_down)
    depth_out = run(
        functools.partial(spread_kernel, depths, sections), where, arrived + [keep_down, got_down],
        [half_shape(total + small)] * depths,
    )
    depth_out, rows_zero = lax.optimization_barrier((depth_out, rows_zero))
    arrived = from_depths(depth_out)
    input_own, input_send = run(
        input_kernel, where, [rows_zero, which, tables, weight_down], [feats_one, feats_one],
    )
    arrived, input_own, input_send = lax.optimization_barrier((arrived, input_own, input_send))
    (summed,) = run(add_kernel, where, arrived, [half_shape(total + small)])
    arrived = from_depths([summed] * depths)
    (joined,) = run(
        functools.partial(join_kernel, small), where, arrived + [norm_rows, cores(norm_rows)],
        [half_shape(depths * (total + small) + 16)],
    )
    arrived = from_sections([joined] * sections)
    across = cores(joined)
    features, input_grad = run(
        place_outputs_kernel, where,
        [features_own, features_other, input_own, cores(input_send)],
        [rows_bf16, shape((mine, in_channels, fine_rows), BF16)],
        [pltpu.SemaphoreType.DMA((4,))],
        hbm_out=(0, 1),
    )
    block = (2, depths * parts[0], channels)
    convs = [shape((conv_rows, channels), F32)] * 2
    down_shape = shape((wide, channels), F32)
    norms = shape(bn_scale.shape, F32)

    def staging(count):
        return [pltpu.VMEM((count,) + block, F32)]

    def rest_scratch():
        return staging(sections) + [
            pltpu.VMEM((depths * small, channels), F32),
            pltpu.SemaphoreType.DMA((sections, 2)),
            pltpu.SemaphoreType.DMA((1,)),
        ]

    arrived, features, input_grad = lax.optimization_barrier((arrived, features, input_grad))
    others = [across] + [cores(piece) for piece in arrived[1:]]
    items = [(False, j) for j in partners(sections)]
    grad_second, grad_first, grad_down, grad_scale, grad_shift = run(
        functools.partial(settle_rest_kernel, items, parts, depths, small, True), where,
        arrived, convs + [down_shape, norms, norms], rest_scratch(),
        hbm_out=(0, 1, 2), flops=10**9,
    )
    items = [(True, j) for j in partners(sections)]
    grad_second, grad_first, grad_down = run(
        functools.partial(settle_rest_kernel, items, parts, depths, small, False), where,
        others + [grad_second, grad_first, grad_down], convs + [down_shape], rest_scratch(),
        hbm_in=(sections, sections + 1, sections + 2), hbm_out=(0, 1, 2),
        aliases={1 + sections: 0, 2 + sections: 1, 3 + sections: 2}, flops=10**9,
    )
    return (
        features,
        jnp.swapaxes(input_grad, 1, 2),
        grad_down.reshape(w_down.shape),
        grad_first.reshape(w_first.shape),
        grad_second.reshape(w_second.shape),
        grad_scale,
        grad_shift,
    )


def solution(mesh):
    in_specs = (
        P(None, "dp", None),
        P(None, None, "dp"),
        P(None, None, "dp"),
        P(),
        P(),
        P(),
        P(),
        P(),
        P(None, "dp", None),
    )
    out_specs = (P("section", "dp", None), P("section", "dp", None), P(), P(), P(), P(), P())
    return jax.shard_map(local, mesh=mesh, in_specs=in_specs, out_specs=out_specs, check_vma=False)
```

```python
import functools

import jax
import jax.numpy as jnp
from jax import lax
from jax.experimental import pallas as pl
from jax.experimental.pallas import tpu as pltpu
from jax.sharding import PartitionSpec as P

EPSILON = 1e-05
F32 = jnp.float32
BF16 = jnp.bfloat16
F8 = jnp.float8_e4m3fn
VMEM_BYTES = 40 << 20
GROUPS = ((0, 1, 2, 3, 4, 5, 6), (7, 8, 9, 10, 11, 12, 13))


def mm(left, right):
    return jnp.dot(left, right, preferred_element_type=F32)


def mm_t(left, right):
    return lax.dot_general(left, right, (((1,), (1,)), ((), ())), preferred_element_type=F32)


def col_sum(values):
    return jnp.sum(values, axis=0, keepdims=True)


def sigmoid(values):
    return 1.0 / (1.0 + jnp.exp(-values))


def tree_sum(parts):
    parts = list(parts)
    while len(parts) > 1:
        parts = [parts[i] + parts[i + 1] for i in range(0, len(parts), 2)]
    return parts[0]


def sum_refs(refs):
    return tree_sum([ref[...].astype(F32) for ref in refs])


def hits(index_row, rows):
    places = lax.broadcasted_iota(jnp.int16, (rows, index_row.shape[1]), 0)
    return jnp.where(places == index_row, jnp.ones(places.shape, F8), jnp.zeros(places.shape, F8))


def live_mask(near_ref, bucket, channels):
    rows = near_ref.shape[2]
    centre = near_ref[bucket, 13:14, :]
    count = jnp.sum((centre < rows).astype(F32), axis=1, keepdims=True)
    places = lax.broadcasted_iota(jnp.int32, (rows, channels), 0).astype(F32)
    return (places < count).astype(F32), count


def power_for(largest):
    power = jnp.full_like(largest, 2.0**-60)
    for exponent in (64, 32, 16, 8, 4, 2, 1):
        raised = power * (2.0**exponent)
        power = jnp.where(largest * raised <= 224.0, raised, power)
    return power


def two_parts(scaled):
    high = scaled.astype(F8)
    low = (scaled - high.astype(F32)).astype(F8)
    return jnp.concatenate([high, low], axis=1)


def moved_rows(near_ref, bucket, offset, pair):
    row = near_ref[bucket, offset : offset + 1, :]
    both = mm(hits(row.astype(jnp.int16), row.shape[1]), pair)
    channels = pair.shape[1] // 2
    return (both[:, :channels] + both[:, channels:]).astype(BF16)


def group_offsets(group):
    return [k for j in group for k in ((j, 26 - j) if j < 13 else (13,))]


def moments(totals):
    count = totals[2:3]
    mean_row = totals[0:1] / count
    square = totals[1:2] / count
    return mean_row, lax.rsqrt(square - mean_row * mean_row + EPSILON), count


def add_sums(out_ref, first, second, count):
    third = jnp.broadcast_to(count, first.shape)
    rows = [first, second, third, jnp.zeros((out_ref.shape[0] - 3, first.shape[1]), F32)]
    out_ref[...] += jnp.concatenate(rows, axis=0)


def norm_back(upstream, centred, live, inv_std, gain_row, back, count):
    return live * (inv_std * gain_row) * (upstream - back[0:1] / count - centred * (back[1:2] / count))


def parent_rows(table, fine_rows):
    first = jnp.min(table, axis=0, keepdims=True)
    children = jnp.sum((table < fine_rows).astype(jnp.int32), axis=0, keepdims=True)
    return first, first + children


def parent_hits(first, last, at, size):
    places = lax.broadcasted_iota(jnp.int16, (size, first.shape[1]), 0) + jnp.int16(at)
    inside = (places >= first.astype(jnp.int16)) & (places < last.astype(jnp.int16))
    return jnp.where(inside, jnp.bfloat16(1), jnp.bfloat16(0))


def pack_kernel(
    where_ref, feats_hbm, down_hbm, weight_hbm,
    send_ref, feats_own, table_own, weight_ref, table_ref, arrivals,
):
    channels, fine_rows = feats_own.shape
    copies = [
        pltpu.make_async_copy(source, target, arrivals.at[i])
        for i, (source, target) in enumerate(
            (
                (down_hbm.at[where_ref[4]], table_ref),
                (feats_hbm.at[where_ref[4]], send_ref.at[pl.ds(0, channels)]),
                (down_hbm.at[where_ref[0]], table_own),
                (feats_hbm.at[where_ref[0]], feats_own),
                (weight_hbm, weight_ref),
            )
        )
    ]
    for copy in copies:
        copy.start()
    copies[0].wait()
    table = table_ref[...]
    rows = [table // 16, table % 16]
    rows.append(jnp.zeros((table.shape[0], fine_rows - 2 * table.shape[1]), jnp.int32))
    rows = jnp.concatenate(rows, axis=1).astype(F32)
    rows = jnp.concatenate([rows, jnp.zeros((16 - table.shape[0], fine_rows), F32)], axis=0)
    send_ref[channels:] = rows.astype(BF16)
    for copy in copies[1:]:
        copy.wait()


def down_rows(table, feats_ref, weight_ref, which_ref, spread_ref, parent_ref):
    in_channels, fine_rows = feats_ref.shape
    offsets, coarse_rows = table.shape
    first, last = parent_rows(table, fine_rows)
    rank = table - first
    numbers = lax.broadcasted_iota(jnp.int32, (offsets, coarse_rows), 0) + 1
    rows = [jnp.sum(jnp.where(rank == r, numbers, 0), axis=0, keepdims=True) for r in range(8)]
    safe_first = jnp.where(first < fine_rows, first, 0)
    rows += [(safe_first // 16) * 16, safe_first % 16] + [jnp.zeros_like(first)] * 6
    lookup = jnp.concatenate(rows, axis=0).astype(F32).astype(BF16)
    step = 512
    for at in range(0, fine_rows, step):
        parent_ref[at : at + step] = parent_hits(first, last, at, step)
    found = mm_t(lookup, parent_ref[...])
    place = lax.broadcasted_iota(jnp.int32, (8, fine_rows), 1).astype(F32) - (found[8:9] + found[9:10])
    column = lax.broadcasted_iota(jnp.int32, (8, fine_rows), 0).astype(F32)
    which = jnp.sum(jnp.where(column == place, found[:8], 0.0), axis=0, keepdims=True)
    which_ref[...] = jnp.broadcast_to(which, which_ref.shape)
    code = jnp.broadcast_to(which, (in_channels, fine_rows)).astype(BF16)
    feats = feats_ref[...]
    for k in range(offsets):
        spread_ref[in_channels * k : in_channels * (k + 1)] = jnp.where(
            code == jnp.bfloat16(k + 1), feats, jnp.zeros_like(feats)
        )
    kids = mm(spread_ref[...], parent_ref[...]).astype(BF16)
    hidden = jnp.transpose(mm(jnp.transpose(weight_ref[...]), kids))
    count = jnp.sum((last > first).astype(F32), axis=1, keepdims=True)
    return kids, hidden, count


def down_kernel(
    where_ref, feats_ref, table_ref, weight_ref, near_ref,
    hidden_ref, sums_ref, kids_ref, which_ref, near_own, near_send,
    spread_ref, parent_ref,
):
    for k in range(near_own.shape[0]):
        near_own[k : k + 1] = near_ref[k, pl.ds(where_ref[0], 1), :]
        near_send[k : k + 1] = near_ref[k, pl.ds(where_ref[4], 1), :]
    kids, hidden, count = down_rows(
        table_ref[...], feats_ref, weight_ref, which_ref, spread_ref, parent_ref
    )
    kids_ref[...] = kids
    hidden_ref[...] = hidden
    sums_ref[...] = jnp.zeros_like(sums_ref)
    add_sums(sums_ref, col_sum(hidden), col_sum(hidden * hidden), count)


def down_other_kernel(
    where_ref, got_ref, weight_ref, own_hidden, own_sums, own_kids, own_which, own_table,
    hidden_ref, sums_ref, kids_ref, which_ref, tables_ref,
    spread_ref, parent_ref,
):
    offsets, coarse_rows = own_table.shape
    channels = got_ref.shape[0] - 16
    coded = got_ref[channels:].astype(F32)[:offsets, : 2 * coarse_rows]
    table = (coded[:, :coarse_rows] * 16.0 + coded[:, coarse_rows:]).astype(jnp.int32)
    kids, hidden, count = down_rows(
        table, got_ref.at[pl.ds(0, channels)], weight_ref, which_ref.at[1], spread_ref, parent_ref
    )
    kids_ref[1] = kids
    hidden_ref[1] = hidden
    tables_ref[1] = table
    for both, own in ((kids_ref, own_kids), (hidden_ref, own_hidden), (which_ref, own_which), (tables_ref, own_table)):
        both[0] = own[...]
    sums_ref[...] = own_sums[...]
    add_sums(sums_ref, col_sum(hidden), col_sum(hidden * hidden), count)


def conv_all(source, near_ref, bucket, weight_ref):
    values = source.astype(F32)
    largest = jnp.max(jnp.max(jnp.abs(values), axis=0, keepdims=True), axis=1, keepdims=True)
    power = power_for(largest)
    scaled = values * power
    pair = two_parts(scaled)
    out = None
    for group in GROUPS:
        offsets = group_offsets(group)
        rows = [
            scaled.astype(BF16) if k == 13 else moved_rows(near_ref, bucket, 26 - k, pair)
            for k in offsets
        ]
        weight = jnp.concatenate([weight_ref[k] for k in offsets], axis=0)
        term = mm(jnp.concatenate(rows, axis=1), weight)
        out = term if out is None else out + term
    return out * (1.0 / power)


def each_bucket(count, body, unrolled):
    if unrolled:
        for b in range(count):
            body(b)
        return

    def step(b, carry):
        body(b)
        return carry

    lax.fori_loop(0, count, step, 0)


def near_kernel(where_ref, own_ref, other_ref, near_ref):
    near_ref[0] = own_ref[...]
    near_ref[1] = other_ref[...]


def forward_kernel(norm_at, rounded, where_ref, hidden_ref, near_ref, weight_ref, scale_ref, shift_ref, *refs):
    part_refs, (act_ref, next_ref, sums_ref) = refs[:-3], refs[-3:]
    mean_row, inv_std, _ = moments(sum_refs(part_refs))
    sums_ref[...] = jnp.zeros_like(sums_ref)

    def bucket(b):
        live, count = live_mask(near_ref, b, hidden_ref.shape[2])
        centred = (hidden_ref[b] - mean_row) * inv_std
        value = centred * scale_ref[norm_at : norm_at + 1] + shift_ref[norm_at : norm_at + 1]
        act = (live * (value * sigmoid(value))).astype(BF16)
        act_ref[b] = act
        hidden = conv_all(act, near_ref, b, weight_ref)
        if rounded:
            hidden = hidden.astype(BF16)
        next_ref[b] = hidden
        hidden = hidden.astype(F32)
        add_sums(sums_ref, col_sum(hidden), col_sum(hidden * hidden), count)

    each_bucket(hidden_ref.shape[0], bucket, True)


def grad_kernel(where_ref, grad_ref, own_ref, send_ref):
    own_ref[...] = grad_ref[where_ref[0]]
    send_ref[...] = grad_ref[where_ref[4]]


def output_kernel(where_ref, hidden_ref, act_ref, own_grad, other_grad, near_ref, scale_ref, shift_ref, *refs):
    part_refs, (own_ref, send_ref, slope_ref, sums_ref) = refs[:-4], refs[-4:]
    mean_row, inv_std, _ = moments(sum_refs(part_refs))
    sums_ref[...] = jnp.zeros_like(sums_ref)
    for b, (grad_ref, features_ref) in enumerate(((own_grad, own_ref), (other_grad, send_ref))):
        live, count = live_mask(near_ref, b, hidden_ref.shape[2])
        centred = (hidden_ref[b].astype(F32) - mean_row) * inv_std
        value = centred * scale_ref[2:3] + shift_ref[2:3] + act_ref[b].astype(F32)
        gate = sigmoid(value)
        features_ref[...] = (live * (value * gate)).astype(BF16)
        upstream = grad_ref[...].astype(F32) * live * (gate * (1.0 + value * (1.0 - gate)))
        slope_ref[b] = upstream
        add_sums(sums_ref, col_sum(upstream), col_sum(upstream * centred), count)


def put_halves(where_ref, grad_ref, keep_ref, send_ref):
    half = keep_ref.shape[0]
    core = where_ref[1]
    keep_ref[...] = grad_ref[pl.ds(pl.multiple_of(core * half, 16), half)].astype(BF16)
    send_ref[...] = grad_ref[pl.ds(pl.multiple_of((1 - core) * half, 16), half)].astype(BF16)


def backward_kernel(norm_at, with_skip, ways, where_ref, *refs):
    upstream_ref, hidden_ref, lower_ref, act_ref, near_ref, weight_ref, scale_ref, shift_ref = refs[:8]
    own, back, low = (sum_refs(refs[8 + i * ways : 8 + (i + 1) * ways]) for i in range(3))
    rest = refs[8 + 3 * ways :]
    next_ref, sums_ref, keep_ref, send_ref, grad_ref = rest[-5:]
    mean_row, inv_std, count = moments(own)
    low_mean, low_std, _ = moments(low)
    channels = hidden_ref.shape[2]
    sums_ref[...] = jnp.zeros_like(sums_ref)
    grad_ref[...] = jnp.zeros_like(grad_ref)

    def bucket(b):
        live, own_count = live_mask(near_ref, b, channels)
        centred = (hidden_ref[b].astype(F32) - mean_row) * inv_std
        rows_grad = norm_back(
            upstream_ref[b], centred, live, inv_std, scale_ref[norm_at : norm_at + 1], back, count
        ).astype(BF16)
        act_t = jnp.transpose(act_ref[b])
        values = rows_grad.astype(F32)
        power = power_for(jnp.max(jnp.abs(values), axis=0, keepdims=True))
        undo = 1.0 / power
        undo_low = undo.astype(BF16)
        scaled = values * power
        pair = two_parts(scaled)
        below = None
        for group in GROUPS:
            offsets = group_offsets(group)
            rows = [
                scaled.astype(BF16) if k == 13 else moved_rows(near_ref, b, k, pair)
                for k in offsets
            ]
            moved = jnp.concatenate(rows, axis=1)
            weight = jnp.concatenate([weight_ref[k] * undo_low for k in offsets], axis=1)
            term = mm_t(moved, weight)
            below = term if below is None else below + term
            products = mm(act_t, moved)
            for i, k in enumerate(offsets):
                grad_ref[k * channels : (k + 1) * channels] += (
                    products[:, i * channels : (i + 1) * channels] * undo
                )
        below = below.astype(BF16).astype(F32)
        if with_skip:
            below = below + rest[0][b].astype(BF16).astype(F32)
        low_centred = (lower_ref[b] - low_mean) * low_std
        value = low_centred * scale_ref[norm_at - 1 : norm_at] + shift_ref[norm_at - 1 : norm_at]
        gate = sigmoid(value)
        upstream = below * live * (gate * (1.0 + value * (1.0 - gate)))
        next_ref[b] = upstream
        add_sums(sums_ref, col_sum(upstream), col_sum(upstream * low_centred), own_count)

    each_bucket(hidden_ref.shape[0], bucket, with_skip)
    put_halves(where_ref, grad_ref, keep_ref, send_ref)


def last_kernel(ways, where_ref, upstream_ref, hidden_ref, kids_ref, near_ref, scale_ref, *refs):
    rows_ref, keep_ref, send_ref, norms_ref, grad_ref = refs[4 * ways :]
    mean_row, inv_std, count = moments(sum_refs(refs[:ways]))
    backs = [sum_refs(refs[i * ways : (i + 1) * ways]) for i in (1, 2, 3)]
    back = backs[0]
    rows = [totals[0:2] for totals in backs]
    norms_ref[...] = jnp.concatenate(rows + [jnp.zeros_like(rows[0])], axis=0)
    channels = hidden_ref.shape[2]
    used = kids_ref.shape[1]
    if grad_ref.shape[0] > used:
        grad_ref[used:] = jnp.zeros((grad_ref.shape[0] - used, channels), F32)
    total = None
    for b in range(hidden_ref.shape[0]):
        live, _ = live_mask(near_ref, b, channels)
        centred = (hidden_ref[b] - mean_row) * inv_std
        rows_grad = norm_back(
            upstream_ref[b], centred, live, inv_std, scale_ref[0:1], back, count
        ).astype(BF16)
        rows_ref[b] = rows_grad
        product = mm(kids_ref[b], rows_grad)
        total = product if total is None else total + product
    grad_ref[:used] = total
    put_halves(where_ref, grad_ref, keep_ref, send_ref)


def input_kernel(where_ref, rows_ref, which_ref, tables_ref, weight_ref, own_ref, send_ref):
    in_channels, fine_rows = own_ref.shape
    step = 256
    for b, input_ref in enumerate((own_ref, send_ref)):
        pieces = mm_t(weight_ref[...], rows_ref[b]).astype(BF16)
        first, last = parent_rows(tables_ref[b], fine_rows)
        for at in range(0, fine_rows, step):
            full = mm_t(pieces, parent_hits(first, last, at, step))
            code = jnp.broadcast_to(which_ref[b, 0:1, at : at + step], (in_channels, step))
            out = jnp.zeros((in_channels, step), F32)
            for k in range(full.shape[0] // in_channels):
                out = out + jnp.where(code == float(k + 1), full[in_channels * k : in_channels * (k + 1)], 0.0)
            input_ref[:, at : at + step] = out.astype(BF16)


def place_outputs_kernel(where_ref, own_features, other_features, own_input, other_input, features, inputs, leaving):
    copies = [
        pltpu.make_async_copy(source, target.at[place], leaving.at[i])
        for i, (source, target, place) in enumerate(
            (
                (own_features, features, where_ref[1]),
                (other_features, features, 1 - where_ref[1]),
                (own_input, inputs, where_ref[1]),
                (other_input, inputs, 1 - where_ref[1]),
            )
        )
    ]
    for copy in copies:
        copy.start()
    for copy in copies:
        copy.wait()


def split_kernel(sections, depths, parts, where_ref, *refs):
    pairs, outs = refs[: 2 * len(parts)], refs[2 * len(parts) :]
    total = sum(parts)
    for j in range(sections):
        block = where_ref[2] ^ j
        base = 0
        for i, size in enumerate(parts):
            wide = depths * size
            rows = pl.ds(pl.multiple_of(block * wide, 16), wide)
            both = (pairs[2 * i][rows].astype(F32) + pairs[2 * i + 1][rows].astype(F32)).astype(BF16)
            for z in range(depths):
                outs[j][z * total + base : z * total + base + size] = both[z * size : (z + 1) * size]
            base += size


def spread_kernel(depths, sources, where_ref, *refs):
    blocks, halves, outs = refs[:sources], refs[sources : sources + 2], refs[sources + 2 :]
    small = halves[0].shape[0] // depths
    size = outs[0].shape[0] - small
    for j in range(depths):
        place = where_ref[3] ^ j
        rows = pl.ds(pl.multiple_of(place * size, 16), size)
        outs[j][:size] = tree_sum([ref[rows].astype(F32) for ref in blocks]).astype(BF16)
        rows = pl.ds(pl.multiple_of(place * small, 16), small)
        outs[j][size:] = (halves[0][rows].astype(F32) + halves[1][rows].astype(F32)).astype(BF16)


def add_kernel(where_ref, *refs):
    refs[-1][...] = sum_refs(refs[:-1]).astype(BF16)


def high_and_low(exact):
    high = exact.astype(BF16)
    low = (exact - high.astype(F32)).astype(BF16)
    return jnp.concatenate([high, low], axis=0)


def one_value(high_low):
    rows = high_low.shape[0] // 2
    return high_low[:rows].astype(F32) + high_low[rows:].astype(F32)


def join_kernel(small, where_ref, *refs):
    pieces, norm_refs, out_ref = refs[:-3], refs[-3:-1], refs[-1]
    size = pieces[0].shape[0] - small
    base = len(pieces) * size
    for j, ref in zip(partners(len(pieces)), pieces):
        place = where_ref[3] ^ j
        out_ref[pl.ds(pl.multiple_of(place * size, 16), size)] = ref[:size]
        out_ref[pl.ds(pl.multiple_of(base + place * small, 16), small)] = ref[size:]
    out_ref[base + len(pieces) * small :] = high_and_low(sum_refs(norm_refs))


def settle_blocks(items, parts, depths, sections, where_ref, pieces, outs, staging, leaving):
    total = sum(parts)
    copies = []
    for n, ((flip, j), piece) in enumerate(zip(items, pieces)):
        core = 1 - where_ref[1] if flip else where_ref[1]
        base = 0
        for i, size in enumerate(parts):
            wide = depths * size
            block = core * sections + (where_ref[2] ^ j)
            slot = staging.at[n, i]
            for z in range(depths):
                slot[z * size : (z + 1) * size] = piece[z * total + base : z * total + base + size].astype(F32)
            base += size
            last, rest = divmod(outs[i].shape[0], wide)
            start = pl.multiple_of(block * wide, 16)
            copies.append((block < last, pltpu.make_async_copy(slot, outs[i].at[pl.ds(start, wide)], leaving.at[n, i])))
            pl.when(copies[-1][0])(copies[-1][1].start)
            if rest:
                part_copy = pltpu.make_async_copy(
                    slot.at[pl.ds(0, rest)], outs[i].at[pl.ds(last * wide, rest)], leaving.at[n, i]
                )
                copies.append((block == last, part_copy))
                pl.when(copies[-1][0])(part_copy.start)
    return copies


def finish(copies):
    for when, copy in copies:
        pl.when(when)(copy.wait)


def settle_rest_kernel(items, parts, depths, small, with_norms, where_ref, *refs):
    sections = len(items)
    pieces = refs[:sections]
    staging, down_staging, leaving, down_leaving = refs[-4:]
    outs = refs[-9:-4] if with_norms else refs[-7:-4]
    first, second, down = outs[:3]
    copies = settle_blocks(items, parts, depths, sections, where_ref, pieces, (first, second), staging, leaving)
    base = depths * sum(parts)
    wide = depths * small
    core = where_ref[1] if with_norms else 1 - where_ref[1]
    down_staging[...] = tree_sum([piece[base : base + wide].astype(F32) for piece in pieces])
    down_copy = pltpu.make_async_copy(
        down_staging, down.at[pl.ds(pl.multiple_of(core * wide, 16), wide)], down_leaving.at[0]
    )
    down_copy.start()
    if with_norms:
        sums = tree_sum([one_value(piece[base + wide :]) for piece in pieces])
        outs[4][...] = jnp.concatenate([sums[2 * t : 2 * t + 1] for t in range(3)], axis=0)
        outs[3][...] = jnp.concatenate([sums[2 * t + 1 : 2 * t + 2] for t in range(3)], axis=0)
    finish(copies)
    down_copy.wait()


def run(kernel, where, operands, outs, scratch=(), hbm_in=(), hbm_out=(), aliases=None, flops=0):
    def place(i, hbm):
        return pltpu.HBM if i in hbm else pltpu.VMEM

    return pl.pallas_call(
        kernel,
        in_specs=[pl.BlockSpec(memory_space=pltpu.SMEM)]
        + [pl.BlockSpec(memory_space=place(i, hbm_in)) for i in range(len(operands))],
        out_specs=[pl.BlockSpec(memory_space=place(i, hbm_out)) for i in range(len(outs))],
        out_shape=outs,
        scratch_shapes=list(scratch),
        input_output_aliases=aliases or {},
        compiler_params=pltpu.CompilerParams(vmem_limit_bytes=VMEM_BYTES),
        cost_estimate=pl.CostEstimate(flops=flops, bytes_accessed=(1 << 20) if flops else 1, transcendentals=0),
    )(where, *operands)


def swapped(value, axis, step):
    count = lax.axis_size(axis)
    return lax.ppermute(value, axis, [(i, i ^ step) for i in range(count)])


def partners(count):
    order = [0]
    step = 1
    while len(order) < count:
        order = order + [j ^ (count - step) for j in order]
        step *= 2
    return order


def from_depths(values):
    return [values[j] if j == 0 else swapped(values[j], "dp", 2 * j) for j in partners(len(values))]


def from_sections(values):
    return [values[j] if j == 0 else swapped(values[j], "section", j) for j in partners(len(values))]


def depth_sums(value):
    steps = range(2, lax.axis_size("dp"), 2)
    return [value] + [swapped(value, "dp", step) for step in steps]


def local(
    voxel_feats, down_map, neighbours, w_down, w_first, w_second, bn_scale, bn_shift, out_grad
):
    sections = lax.axis_size("section")
    depths = lax.axis_size("dp") // 2
    mine = voxel_feats.shape[0] // sections
    section, bucket = lax.axis_index("section"), lax.axis_index("dp")
    core = bucket % 2
    base = section * mine
    where = jnp.stack([base + core, core, section, bucket // 2, base + 1 - core]).astype(jnp.int32)
    voxel_feats = jnp.swapaxes(voxel_feats, 1, 2)
    near = jnp.swapaxes(neighbours, 0, 1)
    in_channels, fine_rows = voxel_feats.shape[1:]
    coarse_rows = neighbours.shape[2]
    channels = w_first.shape[2]
    offsets = down_map.shape[1]
    wide = offsets * in_channels
    flat_down = w_down.reshape(wide, channels)
    shape = jax.ShapeDtypeStruct
    rows_f32 = shape((mine, coarse_rows, channels), F32)
    rows_bf16 = shape((mine, coarse_rows, channels), BF16)
    one_bf16 = shape((coarse_rows, channels), BF16)
    sums = shape((8, channels), F32)
    table = shape((offsets, coarse_rows), jnp.int32)
    near_one = shape((w_first.shape[0], coarse_rows), jnp.int32)
    conv_flops = 8 * mine * w_first.shape[0] * coarse_rows * coarse_rows * channels

    def in_hbm(value):
        return pltpu.with_memory_space_constraint(value, pltpu.HBM)

    def cores(value):
        return swapped(value, "dp", 1)

    feats_hbm, down_hbm = in_hbm(voxel_feats), in_hbm(down_map)
    feats_one = shape((in_channels, fine_rows), BF16)
    payload = shape((in_channels + 16, fine_rows), BF16)
    send_feats, own_feats, own_table, weight_down = run(
        pack_kernel, where, [feats_hbm, down_hbm, in_hbm(flat_down)],
        [payload, feats_one, table, shape((wide, channels), BF16)],
        [pltpu.VMEM((offsets, coarse_rows), jnp.int32), pltpu.SemaphoreType.DMA((5,))], hbm_in=(0, 1, 2),
    )
    got_feats = cores(send_feats)
    down_scratch = [pltpu.VMEM((wide, fine_rows), BF16), pltpu.VMEM((fine_rows, coarse_rows), BF16)]
    own_hidden, own_sums, own_kids, own_which, near_own, near_send = run(
        down_kernel, where,
        [own_feats, own_table, weight_down, near],
        [
            shape((coarse_rows, channels), F32), sums, shape((wide, coarse_rows), BF16),
            shape((8, fine_rows), F32), near_one, near_one,
        ],
        down_scratch,
        flops=2 * 10**9,
    )
    hidden_zero, part_zero, kids, which, tables = run(
        down_other_kernel, where,
        [got_feats, weight_down, own_hidden, own_sums, own_kids, own_which, own_table],
        [
            rows_f32, sums, shape((mine, wide, coarse_rows), BF16), shape((mine, 8, fine_rows), F32),
            shape((mine, offsets, coarse_rows), jnp.int32),
        ],
        down_scratch,
        flops=2 * 10**9,
    )
    stats_zero = depth_sums(part_zero)
    ways = len(stats_zero)
    (nears,) = run(
        near_kernel, where, [near_own, cores(near_send)],
        [shape((mine, w_first.shape[0], coarse_rows), jnp.int32)],
    )
    act_zero, hidden_one, part_one = run(
        functools.partial(forward_kernel, 0, False), where,
        [hidden_zero, nears, w_first, bn_scale, bn_shift] + stats_zero,
        [rows_bf16, rows_f32, sums],
        flops=conv_flops,
    )
    stats_one = depth_sums(part_one)
    grad_own, grad_send = run(grad_kernel, where, [out_grad], [one_bf16, one_bf16])
    grad_other = cores(grad_send)
    act_one, hidden_two, part_two = run(
        functools.partial(forward_kernel, 1, True), where,
        [hidden_one, nears, w_second, bn_scale, bn_shift] + stats_one,
        [rows_bf16, rows_bf16, sums],
        flops=conv_flops,
    )
    stats_two = depth_sums(part_two)
    features_own, features_send, up_two, back_part = run(
        output_kernel, where,
        [hidden_two, act_zero, grad_own, grad_other, nears, bn_scale, bn_shift] + stats_two,
        [one_bf16, one_bf16, rows_f32, sums],
        flops=10**9,
    )
    back_two = depth_sums(back_part)

    def part_rows(rows, pieces):
        return -(-rows // (pieces * 16)) * 16

    def half_shape(rows):
        return shape((rows, channels), BF16)

    def accumulator(rows):
        return [pltpu.VMEM((2 * rows, channels), F32)]

    blocks = sections * depths
    conv_rows = w_first.shape[0] * channels
    parts = [part_rows(conv_rows, 2 * blocks)] * 2
    small = part_rows(wide, 2 * depths)
    total = sum(parts)
    half = half_shape(blocks * parts[0])
    small_half = half_shape(depths * small)
    up_one, back_part, keep_second, send_second = run(
        functools.partial(backward_kernel, 2, False, ways), where,
        [up_two, hidden_two, hidden_one, act_one, nears, w_second, bn_scale, bn_shift]
        + stats_two + back_two + stats_one,
        [rows_f32, sums, half, half],
        accumulator(half.shape[0]),
        flops=conv_flops,
    )
    back_one = depth_sums(back_part)
    got_second = cores(send_second)
    features_other = cores(features_send)
    features_other, up_one = lax.optimization_barrier((features_other, up_one))
    up_zero, back_part, keep_first, send_first = run(
        functools.partial(backward_kernel, 1, True, ways), where,
        [up_one, hidden_one, hidden_zero, act_zero, nears, w_first, bn_scale, bn_shift]
        + stats_one + back_one + stats_zero + [up_two],
        [rows_f32, sums, half, half],
        accumulator(half.shape[0]),
        flops=conv_flops,
    )
    got_first = cores(send_first)
    section_out = run(
        functools.partial(split_kernel, sections, depths, parts), where,
        [keep_second, got_second, keep_first, got_first],
        [half_shape(depths * total)] * sections,
    )
    arrived = from_sections(section_out)
    back_zero = depth_sums(back_part)
    rows_zero, keep_down, send_down, norm_rows = run(
        functools.partial(last_kernel, ways), where,
        [up_zero, hidden_zero, kids, nears, bn_scale] + stats_zero + back_zero + back_one + back_two,
        [rows_bf16, small_half, small_half, sums],
        accumulator(small_half.shape[0]),
        flops=10**9,
    )
    got_down = cores(send_down)
    depth_out = run(
        functools.partial(spread_kernel, depths, sections), where, arrived + [keep_down, got_down],
        [half_shape(total + small)] * depths,
    )
    depth_out, rows_zero = lax.optimization_barrier((depth_out, rows_zero))
    arrived = from_depths(depth_out)
    input_own, input_send = run(
        input_kernel, where, [rows_zero, which, tables, weight_down], [feats_one, feats_one],
    )
    arrived, input_own, input_send = lax.optimization_barrier((arrived, input_own, input_send))
    (summed,) = run(add_kernel, where, arrived, [half_shape(total + small)])
    arrived = from_depths([summed] * depths)
    (joined,) = run(
        functools.partial(join_kernel, small), where, arrived + [norm_rows, cores(norm_rows)],
        [half_shape(depths * (total + small) + 16)],
    )
    arrived = from_sections([joined] * sections)
    across = cores(joined)
    features, input_grad = run(
        place_outputs_kernel, where,
        [features_own, features_other, input_own, cores(input_send)],
        [rows_bf16, shape((mine, in_channels, fine_rows), BF16)],
        [pltpu.SemaphoreType.DMA((4,))],
        hbm_out=(0, 1),
    )
    block = (2, depths * parts[0], channels)
    convs = [shape((conv_rows, channels), F32)] * 2
    down_shape = shape((wide, channels), F32)
    norms = shape(bn_scale.shape, F32)

    def staging(count):
        return [pltpu.VMEM((count,) + block, F32)]

    def rest_scratch():
        return staging(sections) + [
            pltpu.VMEM((depths * small, channels), F32),
            pltpu.SemaphoreType.DMA((sections, 2)),
            pltpu.SemaphoreType.DMA((1,)),
        ]

    arrived, features, input_grad = lax.optimization_barrier((arrived, features, input_grad))
    others = [across] + [cores(piece) for piece in arrived[1:]]
    items = [(False, j) for j in partners(sections)]
    grad_second, grad_first, grad_down, grad_scale, grad_shift = run(
        functools.partial(settle_rest_kernel, items, parts, depths, small, True), where,
        arrived, convs + [down_shape, norms, norms], rest_scratch(),
        hbm_out=(0, 1, 2), flops=10**9,
    )
    items = [(True, j) for j in partners(sections)]
    grad_second, grad_first, grad_down = run(
        functools.partial(settle_rest_kernel, items, parts, depths, small, False), where,
        others + [grad_second, grad_first, grad_down], convs + [down_shape], rest_scratch(),
        hbm_in=(sections, sections + 1, sections + 2), hbm_out=(0, 1, 2),
        aliases={1 + sections: 0, 2 + sections: 1, 3 + sections: 2}, flops=10**9,
    )
    return (
        features,
        jnp.swapaxes(input_grad, 1, 2),
        grad_down.reshape(w_down.shape),
        grad_first.reshape(w_first.shape),
        grad_second.reshape(w_second.shape),
        grad_scale,
        grad_shift,
    )


def solution(mesh):
    in_specs = (
        P(None, "dp", None),
        P(None, None, "dp"),
        P(None, None, "dp"),
        P(),
        P(),
        P(),
        P(),
        P(),
        P(None, "dp", None),
    )
    out_specs = (P("section", "dp", None), P("section", "dp", None), P(), P(), P(), P(), P())
    return jax.shard_map(local, mesh=mesh, in_specs=in_specs, out_specs=out_specs, check_vma=False)
```

```python
import functools

import jax
import jax.numpy as jnp
from jax import lax
from jax.experimental import pallas as pl
from jax.experimental.pallas import tpu as pltpu
from jax.sharding import PartitionSpec as P

EPSILON = 1e-05
F32 = jnp.float32
BF16 = jnp.bfloat16
F8 = jnp.float8_e4m3fn
VMEM_BYTES = 40 << 20
GROUPS = ((0, 1, 2, 3, 4, 5, 6), (7, 8, 9, 10, 11, 12, 13))


def mm(left, right):
    return jnp.dot(left, right, preferred_element_type=F32)


def mm_t(left, right):
    return lax.dot_general(left, right, (((1,), (1,)), ((), ())), preferred_element_type=F32)


def col_sum(values):
    return jnp.sum(values, axis=0, keepdims=True)


def sigmoid(values):
    return 1.0 / (1.0 + jnp.exp(-values))


def tree_sum(parts):
    parts = list(parts)
    while len(parts) > 1:
        parts = [parts[i] + parts[i + 1] for i in range(0, len(parts), 2)]
    return parts[0]


def sum_refs(refs):
    return tree_sum([ref[...].astype(F32) for ref in refs])


def hits(index_row, rows):
    places = lax.broadcasted_iota(jnp.int16, (rows, index_row.shape[1]), 0)
    return jnp.where(places == index_row, jnp.ones(places.shape, F8), jnp.zeros(places.shape, F8))


def live_mask(near_ref, bucket, channels):
    rows = near_ref.shape[2]
    centre = near_ref[bucket, 13:14, :]
    count = jnp.sum((centre < rows).astype(F32), axis=1, keepdims=True)
    places = lax.broadcasted_iota(jnp.int32, (rows, channels), 0).astype(F32)
    return (places < count).astype(F32), count


def power_for(largest):
    power = jnp.full_like(largest, 2.0**-60)
    for exponent in (64, 32, 16, 8, 4, 2, 1):
        raised = power * (2.0**exponent)
        power = jnp.where(largest * raised <= 224.0, raised, power)
    return power


def two_parts(scaled):
    high = scaled.astype(F8)
    low = (scaled - high.astype(F32)).astype(F8)
    return jnp.concatenate([high, low], axis=1)


def moved_rows(near_ref, bucket, offset, pair):
    row = near_ref[bucket, offset : offset + 1, :]
    both = mm(hits(row.astype(jnp.int16), row.shape[1]), pair)
    channels = pair.shape[1] // 2
    return (both[:, :channels] + both[:, channels:]).astype(BF16)


def group_offsets(group):
    return [k for j in group for k in ((j, 26 - j) if j < 13 else (13,))]


def moments(totals):
    count = totals[2:3]
    mean_row = totals[0:1] / count
    square = totals[1:2] / count
    return mean_row, lax.rsqrt(square - mean_row * mean_row + EPSILON), count


def add_sums(out_ref, first, second, count):
    third = jnp.broadcast_to(count, first.shape)
    rows = [first, second, third, jnp.zeros((out_ref.shape[0] - 3, first.shape[1]), F32)]
    out_ref[...] += jnp.concatenate(rows, axis=0)


def norm_back(upstream, centred, live, inv_std, gain_row, back, count):
    return live * (inv_std * gain_row) * (upstream - back[0:1] / count - centred * (back[1:2] / count))


def parent_rows(table, fine_rows):
    first = jnp.min(table, axis=0, keepdims=True)
    children = jnp.sum((table < fine_rows).astype(jnp.int32), axis=0, keepdims=True)
    return first, first + children


def parent_hits(first, last, at, size):
    places = lax.broadcasted_iota(jnp.int16, (size, first.shape[1]), 0) + jnp.int16(at)
    inside = (places >= first.astype(jnp.int16)) & (places < last.astype(jnp.int16))
    return jnp.where(inside, jnp.bfloat16(1), jnp.bfloat16(0))


def pack_kernel(
    where_ref, feats_hbm, down_hbm, weight_hbm,
    send_ref, feats_own, table_own, weight_ref, table_ref, arrivals,
):
    channels, fine_rows = feats_own.shape
    copies = [
        pltpu.make_async_copy(source, target, arrivals.at[i])
        for i, (source, target) in enumerate(
            (
                (down_hbm.at[where_ref[4]], table_ref),
                (feats_hbm.at[where_ref[4]], send_ref.at[pl.ds(0, channels)]),
                (down_hbm.at[where_ref[0]], table_own),
                (feats_hbm.at[where_ref[0]], feats_own),
                (weight_hbm, weight_ref),
            )
        )
    ]
    for copy in copies:
        copy.start()
    copies[0].wait()
    table = table_ref[...]
    rows = [table // 16, table % 16]
    rows.append(jnp.zeros((table.shape[0], fine_rows - 2 * table.shape[1]), jnp.int32))
    rows = jnp.concatenate(rows, axis=1).astype(F32)
    rows = jnp.concatenate([rows, jnp.zeros((16 - table.shape[0], fine_rows), F32)], axis=0)
    send_ref[channels:] = rows.astype(BF16)
    for copy in copies[1:]:
        copy.wait()


def down_rows(table, feats_ref, weight_ref, which_ref, spread_ref, parent_ref):
    in_channels, fine_rows = feats_ref.shape
    offsets, coarse_rows = table.shape
    first, last = parent_rows(table, fine_rows)
    rank = table - first
    numbers = lax.broadcasted_iota(jnp.int32, (offsets, coarse_rows), 0) + 1
    rows = [jnp.sum(jnp.where(rank == r, numbers, 0), axis=0, keepdims=True) for r in range(8)]
    safe_first = jnp.where(first < fine_rows, first, 0)
    rows += [(safe_first // 16) * 16, safe_first % 16] + [jnp.zeros_like(first)] * 6
    lookup = jnp.concatenate(rows, axis=0).astype(F32).astype(BF16)
    step = 512
    for at in range(0, fine_rows, step):
        parent_ref[at : at + step] = parent_hits(first, last, at, step)
    found = mm_t(lookup, parent_ref[...])
    place = lax.broadcasted_iota(jnp.int32, (8, fine_rows), 1).astype(F32) - (found[8:9] + found[9:10])
    column = lax.broadcasted_iota(jnp.int32, (8, fine_rows), 0).astype(F32)
    which = jnp.sum(jnp.where(column == place, found[:8], 0.0), axis=0, keepdims=True)
    which_ref[...] = jnp.broadcast_to(which, which_ref.shape)
    code = jnp.broadcast_to(which, (in_channels, fine_rows)).astype(BF16)
    feats = feats_ref[...]
    for k in range(offsets):
        spread_ref[in_channels * k : in_channels * (k + 1)] = jnp.where(
            code == jnp.bfloat16(k + 1), feats, jnp.zeros_like(feats)
        )
    kids = mm(spread_ref[...], parent_ref[...]).astype(BF16)
    hidden = jnp.transpose(mm(jnp.transpose(weight_ref[...]), kids))
    count = jnp.sum((last > first).astype(F32), axis=1, keepdims=True)
    return kids, hidden, count


def down_kernel(
    where_ref, feats_ref, table_ref, weight_ref, near_ref,
    hidden_ref, sums_ref, kids_ref, which_ref, near_own, near_send,
    spread_ref, parent_ref,
):
    for k in range(near_own.shape[0]):
        near_own[k : k + 1] = near_ref[k, pl.ds(where_ref[0], 1), :]
        near_send[k : k + 1] = near_ref[k, pl.ds(where_ref[4], 1), :]
    kids, hidden, count = down_rows(
        table_ref[...], feats_ref, weight_ref, which_ref, spread_ref, parent_ref
    )
    kids_ref[...] = kids
    hidden_ref[...] = hidden
    sums_ref[...] = jnp.zeros_like(sums_ref)
    add_sums(sums_ref, col_sum(hidden), col_sum(hidden * hidden), count)


def down_other_kernel(
    where_ref, got_ref, weight_ref, own_hidden, own_sums, own_kids, own_which, own_table,
    hidden_ref, sums_ref, kids_ref, which_ref, tables_ref,
    spread_ref, parent_ref,
):
    offsets, coarse_rows = own_table.shape
    channels = got_ref.shape[0] - 16
    coded = got_ref[channels:].astype(F32)[:offsets, : 2 * coarse_rows]
    table = (coded[:, :coarse_rows] * 16.0 + coded[:, coarse_rows:]).astype(jnp.int32)
    kids, hidden, count = down_rows(
        table, got_ref.at[pl.ds(0, channels)], weight_ref, which_ref.at[1], spread_ref, parent_ref
    )
    kids_ref[1] = kids
    hidden_ref[1] = hidden
    tables_ref[1] = table
    for both, own in ((kids_ref, own_kids), (hidden_ref, own_hidden), (which_ref, own_which), (tables_ref, own_table)):
        both[0] = own[...]
    sums_ref[...] = own_sums[...]
    add_sums(sums_ref, col_sum(hidden), col_sum(hidden * hidden), count)


def conv_all(source, near_ref, bucket, weight_ref):
    values = source.astype(F32)
    largest = jnp.max(jnp.max(jnp.abs(values), axis=0, keepdims=True), axis=1, keepdims=True)
    power = power_for(largest)
    scaled = values * power
    pair = two_parts(scaled)
    out = None
    for group in GROUPS:
        offsets = group_offsets(group)
        rows = [
            scaled.astype(BF16) if k == 13 else moved_rows(near_ref, bucket, 26 - k, pair)
            for k in offsets
        ]
        weight = jnp.concatenate([weight_ref[k] for k in offsets], axis=0)
        term = mm(jnp.concatenate(rows, axis=1), weight)
        out = term if out is None else out + term
    return out * (1.0 / power)


def each_bucket(count, body, unrolled):
    if unrolled:
        for b in range(count):
            body(b)
        return

    def step(b, carry):
        body(b)
        return carry

    lax.fori_loop(0, count, step, 0)


def near_kernel(where_ref, own_ref, other_ref, near_ref):
    near_ref[0] = own_ref[...]
    near_ref[1] = other_ref[...]


def forward_kernel(norm_at, rounded, where_ref, hidden_ref, near_ref, weight_ref, scale_ref, shift_ref, *refs):
    part_refs, (act_ref, next_ref, sums_ref) = refs[:-3], refs[-3:]
    mean_row, inv_std, _ = moments(sum_refs(part_refs))
    sums_ref[...] = jnp.zeros_like(sums_ref)

    def bucket(b):
        live, count = live_mask(near_ref, b, hidden_ref.shape[2])
        centred = (hidden_ref[b] - mean_row) * inv_std
        value = centred * scale_ref[norm_at : norm_at + 1] + shift_ref[norm_at : norm_at + 1]
        act = (live * (value * sigmoid(value))).astype(BF16)
        act_ref[b] = act
        hidden = conv_all(act, near_ref, b, weight_ref)
        if rounded:
            hidden = hidden.astype(BF16)
        next_ref[b] = hidden
        hidden = hidden.astype(F32)
        add_sums(sums_ref, col_sum(hidden), col_sum(hidden * hidden), count)

    each_bucket(hidden_ref.shape[0], bucket, True)


def grad_kernel(where_ref, grad_ref, own_ref, send_ref):
    own_ref[...] = grad_ref[where_ref[0]]
    send_ref[...] = grad_ref[where_ref[4]]


def output_kernel(where_ref, hidden_ref, act_ref, own_grad, other_grad, near_ref, scale_ref, shift_ref, *refs):
    part_refs, (own_ref, send_ref, slope_ref, sums_ref) = refs[:-4], refs[-4:]
    mean_row, inv_std, _ = moments(sum_refs(part_refs))
    sums_ref[...] = jnp.zeros_like(sums_ref)
    for b, (grad_ref, features_ref) in enumerate(((own_grad, own_ref), (other_grad, send_ref))):
        live, count = live_mask(near_ref, b, hidden_ref.shape[2])
        centred = (hidden_ref[b].astype(F32) - mean_row) * inv_std
        value = centred * scale_ref[2:3] + shift_ref[2:3] + act_ref[b].astype(F32)
        gate = sigmoid(value)
        features_ref[...] = (live * (value * gate)).astype(BF16)
        upstream = grad_ref[...].astype(F32) * live * (gate * (1.0 + value * (1.0 - gate)))
        slope_ref[b] = upstream
        add_sums(sums_ref, col_sum(upstream), col_sum(upstream * centred), count)


def put_halves(where_ref, grad_ref, keep_ref, send_ref):
    half = keep_ref.shape[0]
    core = where_ref[1]
    keep_ref[...] = grad_ref[pl.ds(pl.multiple_of(core * half, 16), half)].astype(BF16)
    send_ref[...] = grad_ref[pl.ds(pl.multiple_of((1 - core) * half, 16), half)].astype(BF16)


def backward_kernel(norm_at, with_skip, ways, where_ref, *refs):
    upstream_ref, hidden_ref, lower_ref, act_ref, near_ref, weight_ref, scale_ref, shift_ref = refs[:8]
    own, back, low = (sum_refs(refs[8 + i * ways : 8 + (i + 1) * ways]) for i in range(3))
    rest = refs[8 + 3 * ways :]
    next_ref, sums_ref, keep_ref, send_ref, grad_ref = rest[-5:]
    mean_row, inv_std, count = moments(own)
    low_mean, low_std, _ = moments(low)
    channels = hidden_ref.shape[2]
    sums_ref[...] = jnp.zeros_like(sums_ref)
    grad_ref[...] = jnp.zeros_like(grad_ref)

    def bucket(b):
        live, own_count = live_mask(near_ref, b, channels)
        centred = (hidden_ref[b].astype(F32) - mean_row) * inv_std
        rows_grad = norm_back(
            upstream_ref[b], centred, live, inv_std, scale_ref[norm_at : norm_at + 1], back, count
        ).astype(BF16)
        act_t = jnp.transpose(act_ref[b])
        values = rows_grad.astype(F32)
        power = power_for(jnp.max(jnp.abs(values), axis=0, keepdims=True))
        undo = 1.0 / power
        undo_low = undo.astype(BF16)
        scaled = values * power
        pair = two_parts(scaled)
        below = None
        for group in GROUPS:
            offsets = group_offsets(group)
            rows = [
                scaled.astype(BF16) if k == 13 else moved_rows(near_ref, b, k, pair)
                for k in offsets
            ]
            moved = jnp.concatenate(rows, axis=1)
            weight = jnp.concatenate([weight_ref[k] * undo_low for k in offsets], axis=1)
            term = mm_t(moved, weight)
            below = term if below is None else below + term
            products = mm(act_t, moved)
            for i, k in enumerate(offsets):
                grad_ref[k * channels : (k + 1) * channels] += (
                    products[:, i * channels : (i + 1) * channels] * undo
                )
        below = below.astype(BF16).astype(F32)
        if with_skip:
            below = below + rest[0][b].astype(BF16).astype(F32)
        low_centred = (lower_ref[b] - low_mean) * low_std
        value = low_centred * scale_ref[norm_at - 1 : norm_at] + shift_ref[norm_at - 1 : norm_at]
        gate = sigmoid(value)
        upstream = below * live * (gate * (1.0 + value * (1.0 - gate)))
        next_ref[b] = upstream
        add_sums(sums_ref, col_sum(upstream), col_sum(upstream * low_centred), own_count)

    each_bucket(hidden_ref.shape[0], bucket, True)
    put_halves(where_ref, grad_ref, keep_ref, send_ref)


def last_kernel(ways, where_ref, upstream_ref, hidden_ref, kids_ref, near_ref, scale_ref, *refs):
    rows_ref, keep_ref, send_ref, norms_ref, grad_ref = refs[4 * ways :]
    mean_row, inv_std, count = moments(sum_refs(refs[:ways]))
    backs = [sum_refs(refs[i * ways : (i + 1) * ways]) for i in (1, 2, 3)]
    back = backs[0]
    rows = [totals[0:2] for totals in backs]
    norms_ref[...] = jnp.concatenate(rows + [jnp.zeros_like(rows[0])], axis=0)
    channels = hidden_ref.shape[2]
    used = kids_ref.shape[1]
    if grad_ref.shape[0] > used:
        grad_ref[used:] = jnp.zeros((grad_ref.shape[0] - used, channels), F32)
    total = None
    for b in range(hidden_ref.shape[0]):
        live, _ = live_mask(near_ref, b, channels)
        centred = (hidden_ref[b] - mean_row) * inv_std
        rows_grad = norm_back(
            upstream_ref[b], centred, live, inv_std, scale_ref[0:1], back, count
        ).astype(BF16)
        rows_ref[b] = rows_grad
        product = mm(kids_ref[b], rows_grad)
        total = product if total is None else total + product
    grad_ref[:used] = total
    put_halves(where_ref, grad_ref, keep_ref, send_ref)


def input_kernel(where_ref, rows_ref, which_ref, tables_ref, weight_ref, own_ref, send_ref):
    in_channels, fine_rows = own_ref.shape
    step = 256
    for b, input_ref in enumerate((own_ref, send_ref)):
        pieces = mm_t(weight_ref[...], rows_ref[b]).astype(BF16)
        first, last = parent_rows(tables_ref[b], fine_rows)
        for at in range(0, fine_rows, step):
            full = mm_t(pieces, parent_hits(first, last, at, step))
            code = jnp.broadcast_to(which_ref[b, 0:1, at : at + step], (in_channels, step))
            out = jnp.zeros((in_channels, step), F32)
            for k in range(full.shape[0] // in_channels):
                out = out + jnp.where(code == float(k + 1), full[in_channels * k : in_channels * (k + 1)], 0.0)
            input_ref[:, at : at + step] = out.astype(BF16)


def place_outputs_kernel(where_ref, own_features, other_features, own_input, other_input, features, inputs, leaving):
    copies = [
        pltpu.make_async_copy(source, target.at[place], leaving.at[i])
        for i, (source, target, place) in enumerate(
            (
                (own_features, features, where_ref[1]),
                (other_features, features, 1 - where_ref[1]),
                (own_input, inputs, where_ref[1]),
                (other_input, inputs, 1 - where_ref[1]),
            )
        )
    ]
    for copy in copies:
        copy.start()
    for copy in copies:
        copy.wait()


def split_kernel(sections, depths, parts, where_ref, *refs):
    pairs, outs = refs[: 2 * len(parts)], refs[2 * len(parts) :]
    total = sum(parts)
    for j in range(sections):
        block = where_ref[2] ^ j
        base = 0
        for i, size in enumerate(parts):
            wide = depths * size
            rows = pl.ds(pl.multiple_of(block * wide, 16), wide)
            both = (pairs[2 * i][rows].astype(F32) + pairs[2 * i + 1][rows].astype(F32)).astype(BF16)
            for z in range(depths):
                outs[j][z * total + base : z * total + base + size] = both[z * size : (z + 1) * size]
            base += size


def spread_kernel(depths, sources, where_ref, *refs):
    blocks, halves, outs = refs[:sources], refs[sources : sources + 2], refs[sources + 2 :]
    small = halves[0].shape[0] // depths
    size = outs[0].shape[0] - small
    for j in range(depths):
        place = where_ref[3] ^ j
        rows = pl.ds(pl.multiple_of(place * size, 16), size)
        outs[j][:size] = tree_sum([ref[rows].astype(F32) for ref in blocks]).astype(BF16)
        rows = pl.ds(pl.multiple_of(place * small, 16), small)
        outs[j][size:] = (halves[0][rows].astype(F32) + halves[1][rows].astype(F32)).astype(BF16)


def add_kernel(where_ref, *refs):
    refs[-1][...] = sum_refs(refs[:-1]).astype(BF16)


def high_and_low(exact):
    high = exact.astype(BF16)
    low = (exact - high.astype(F32)).astype(BF16)
    return jnp.concatenate([high, low], axis=0)


def one_value(high_low):
    rows = high_low.shape[0] // 2
    return high_low[:rows].astype(F32) + high_low[rows:].astype(F32)


def join_kernel(small, where_ref, *refs):
    pieces, norm_refs, out_ref = refs[:-3], refs[-3:-1], refs[-1]
    size = pieces[0].shape[0] - small
    base = len(pieces) * size
    for j, ref in zip(partners(len(pieces)), pieces):
        place = where_ref[3] ^ j
        out_ref[pl.ds(pl.multiple_of(place * size, 16), size)] = ref[:size]
        out_ref[pl.ds(pl.multiple_of(base + place * small, 16), small)] = ref[size:]
    out_ref[base + len(pieces) * small :] = high_and_low(sum_refs(norm_refs))


def settle_blocks(items, parts, depths, sections, where_ref, pieces, outs, staging, leaving):
    total = sum(parts)
    copies = []
    for n, ((flip, j), piece) in enumerate(zip(items, pieces)):
        core = 1 - where_ref[1] if flip else where_ref[1]
        base = 0
        for i, size in enumerate(parts):
            wide = depths * size
            block = core * sections + (where_ref[2] ^ j)
            slot = staging.at[n, i]
            for z in range(depths):
                slot[z * size : (z + 1) * size] = piece[z * total + base : z * total + base + size].astype(F32)
            base += size
            last, rest = divmod(outs[i].shape[0], wide)
            start = pl.multiple_of(block * wide, 16)
            copies.append((block < last, pltpu.make_async_copy(slot, outs[i].at[pl.ds(start, wide)], leaving.at[n, i])))
            pl.when(copies[-1][0])(copies[-1][1].start)
            if rest:
                part_copy = pltpu.make_async_copy(
                    slot.at[pl.ds(0, rest)], outs[i].at[pl.ds(last * wide, rest)], leaving.at[n, i]
                )
                copies.append((block == last, part_copy))
                pl.when(copies[-1][0])(part_copy.start)
    return copies


def finish(copies):
    for when, copy in copies:
        pl.when(when)(copy.wait)


def settle_rest_kernel(items, parts, depths, small, with_norms, where_ref, *refs):
    sections = len(items)
    pieces = refs[:sections]
    staging, down_staging, leaving, down_leaving = refs[-4:]
    outs = refs[-9:-4] if with_norms else refs[-7:-4]
    first, second, down = outs[:3]
    copies = settle_blocks(items, parts, depths, sections, where_ref, pieces, (first, second), staging, leaving)
    base = depths * sum(parts)
    wide = depths * small
    core = where_ref[1] if with_norms else 1 - where_ref[1]
    down_staging[...] = tree_sum([piece[base : base + wide].astype(F32) for piece in pieces])
    down_copy = pltpu.make_async_copy(
        down_staging, down.at[pl.ds(pl.multiple_of(core * wide, 16), wide)], down_leaving.at[0]
    )
    down_copy.start()
    if with_norms:
        sums = tree_sum([one_value(piece[base + wide :]) for piece in pieces])
        outs[4][...] = jnp.concatenate([sums[2 * t : 2 * t + 1] for t in range(3)], axis=0)
        outs[3][...] = jnp.concatenate([sums[2 * t + 1 : 2 * t + 2] for t in range(3)], axis=0)
    finish(copies)
    down_copy.wait()


def run(kernel, where, operands, outs, scratch=(), hbm_in=(), hbm_out=(), aliases=None, flops=0):
    def place(i, hbm):
        return pltpu.HBM if i in hbm else pltpu.VMEM

    return pl.pallas_call(
        kernel,
        in_specs=[pl.BlockSpec(memory_space=pltpu.SMEM)]
        + [pl.BlockSpec(memory_space=place(i, hbm_in)) for i in range(len(operands))],
        out_specs=[pl.BlockSpec(memory_space=place(i, hbm_out)) for i in range(len(outs))],
        out_shape=outs,
        scratch_shapes=list(scratch),
        input_output_aliases=aliases or {},
        compiler_params=pltpu.CompilerParams(vmem_limit_bytes=VMEM_BYTES),
        cost_estimate=pl.CostEstimate(flops=flops, bytes_accessed=(1 << 20) if flops else 1, transcendentals=0),
    )(where, *operands)


def swapped(value, axis, step):
    count = lax.axis_size(axis)
    return lax.ppermute(value, axis, [(i, i ^ step) for i in range(count)])


def partners(count):
    order = [0]
    step = 1
    while len(order) < count:
        order = order + [j ^ (count - step) for j in order]
        step *= 2
    return order


def from_depths(values):
    return [values[j] if j == 0 else swapped(values[j], "dp", 2 * j) for j in partners(len(values))]


def from_sections(values):
    return [values[j] if j == 0 else swapped(values[j], "section", j) for j in partners(len(values))]


def depth_sums(value):
    steps = range(2, lax.axis_size("dp"), 2)
    return [value] + [swapped(value, "dp", step) for step in steps]


def local(
    voxel_feats, down_map, neighbours, w_down, w_first, w_second, bn_scale, bn_shift, out_grad
):
    sections = lax.axis_size("section")
    depths = lax.axis_size("dp") // 2
    mine = voxel_feats.shape[0] // sections
    section, bucket = lax.axis_index("section"), lax.axis_index("dp")
    core = bucket % 2
    base = section * mine
    where = jnp.stack([base + core, core, section, bucket // 2, base + 1 - core]).astype(jnp.int32)
    voxel_feats = jnp.swapaxes(voxel_feats, 1, 2)
    near = jnp.swapaxes(neighbours, 0, 1)
    in_channels, fine_rows = voxel_feats.shape[1:]
    coarse_rows = neighbours.shape[2]
    channels = w_first.shape[2]
    offsets = down_map.shape[1]
    wide = offsets * in_channels
    flat_down = w_down.reshape(wide, channels)
    shape = jax.ShapeDtypeStruct
    rows_f32 = shape((mine, coarse_rows, channels), F32)
    rows_bf16 = shape((mine, coarse_rows, channels), BF16)
    one_bf16 = shape((coarse_rows, channels), BF16)
    sums = shape((8, channels), F32)
    table = shape((offsets, coarse_rows), jnp.int32)
    near_one = shape((w_first.shape[0], coarse_rows), jnp.int32)
    conv_flops = 8 * mine * w_first.shape[0] * coarse_rows * coarse_rows * channels

    def in_hbm(value):
        return pltpu.with_memory_space_constraint(value, pltpu.HBM)

    def cores(value):
        return swapped(value, "dp", 1)

    feats_hbm, down_hbm = in_hbm(voxel_feats), in_hbm(down_map)
    feats_one = shape((in_channels, fine_rows), BF16)
    payload = shape((in_channels + 16, fine_rows), BF16)
    send_feats, own_feats, own_table, weight_down = run(
        pack_kernel, where, [feats_hbm, down_hbm, in_hbm(flat_down)],
        [payload, feats_one, table, shape((wide, channels), BF16)],
        [pltpu.VMEM((offsets, coarse_rows), jnp.int32), pltpu.SemaphoreType.DMA((5,))], hbm_in=(0, 1, 2),
    )
    got_feats = cores(send_feats)
    down_scratch = [pltpu.VMEM((wide, fine_rows), BF16), pltpu.VMEM((fine_rows, coarse_rows), BF16)]
    own_hidden, own_sums, own_kids, own_which, near_own, near_send = run(
        down_kernel, where,
        [own_feats, own_table, weight_down, near],
        [
            shape((coarse_rows, channels), F32), sums, shape((wide, coarse_rows), BF16),
            shape((8, fine_rows), F32), near_one, near_one,
        ],
        down_scratch,
        flops=2 * 10**9,
    )
    hidden_zero, part_zero, kids, which, tables = run(
        down_other_kernel, where,
        [got_feats, weight_down, own_hidden, own_sums, own_kids, own_which, own_table],
        [
            rows_f32, sums, shape((mine, wide, coarse_rows), BF16), shape((mine, 8, fine_rows), F32),
            shape((mine, offsets, coarse_rows), jnp.int32),
        ],
        down_scratch,
        flops=2 * 10**9,
    )
    stats_zero = depth_sums(part_zero)
    ways = len(stats_zero)
    (nears,) = run(
        near_kernel, where, [near_own, cores(near_send)],
        [shape((mine, w_first.shape[0], coarse_rows), jnp.int32)],
    )
    act_zero, hidden_one, part_one = run(
        functools.partial(forward_kernel, 0, False), where,
        [hidden_zero, nears, w_first, bn_scale, bn_shift] + stats_zero,
        [rows_bf16, rows_f32, sums],
        flops=conv_flops,
    )
    stats_one = depth_sums(part_one)
    grad_own, grad_send = run(grad_kernel, where, [out_grad], [one_bf16, one_bf16])
    grad_other = cores(grad_send)
    act_one, hidden_two, part_two = run(
        functools.partial(forward_kernel, 1, True), where,
        [hidden_one, nears, w_second, bn_scale, bn_shift] + stats_one,
        [rows_bf16, rows_bf16, sums],
        flops=conv_flops,
    )
    stats_two = depth_sums(part_two)
    features_own, features_send, up_two, back_part = run(
        output_kernel, where,
        [hidden_two, act_zero, grad_own, grad_other, nears, bn_scale, bn_shift] + stats_two,
        [one_bf16, one_bf16, rows_f32, sums],
        flops=10**9,
    )
    back_two = depth_sums(back_part)

    def part_rows(rows, pieces):
        return -(-rows // (pieces * 16)) * 16

    def half_shape(rows):
        return shape((rows, channels), BF16)

    def accumulator(rows):
        return [pltpu.VMEM((2 * rows, channels), F32)]

    blocks = sections * depths
    conv_rows = w_first.shape[0] * channels
    parts = [part_rows(conv_rows, 2 * blocks)] * 2
    small = part_rows(wide, 2 * depths)
    total = sum(parts)
    half = half_shape(blocks * parts[0])
    small_half = half_shape(depths * small)
    up_one, back_part, keep_second, send_second = run(
        functools.partial(backward_kernel, 2, False, ways), where,
        [up_two, hidden_two, hidden_one, act_one, nears, w_second, bn_scale, bn_shift]
        + stats_two + back_two + stats_one,
        [rows_f32, sums, half, half],
        accumulator(half.shape[0]),
        flops=conv_flops,
    )
    back_one = depth_sums(back_part)
    got_second = cores(send_second)
    features_other = cores(features_send)
    features_other, up_one = lax.optimization_barrier((features_other, up_one))
    up_zero, back_part, keep_first, send_first = run(
        functools.partial(backward_kernel, 1, True, ways), where,
        [up_one, hidden_one, hidden_zero, act_zero, nears, w_first, bn_scale, bn_shift]
        + stats_one + back_one + stats_zero + [up_two],
        [rows_f32, sums, half, half],
        accumulator(half.shape[0]),
        flops=conv_flops,
    )
    got_first = cores(send_first)
    section_out = run(
        functools.partial(split_kernel, sections, depths, parts), where,
        [keep_second, got_second, keep_first, got_first],
        [half_shape(depths * total)] * sections,
    )
    arrived = from_sections(section_out)
    back_zero = depth_sums(back_part)
    rows_zero, keep_down, send_down, norm_rows = run(
        functools.partial(last_kernel, ways), where,
        [up_zero, hidden_zero, kids, nears, bn_scale] + stats_zero + back_zero + back_one + back_two,
        [rows_bf16, small_half, small_half, sums],
        accumulator(small_half.shape[0]),
        flops=10**9,
    )
    got_down = cores(send_down)
    depth_out = run(
        functools.partial(spread_kernel, depths, sections), where, arrived + [keep_down, got_down],
        [half_shape(total + small)] * depths,
    )
    depth_out, rows_zero = lax.optimization_barrier((depth_out, rows_zero))
    arrived = from_depths(depth_out)
    input_own, input_send = run(
        input_kernel, where, [rows_zero, which, tables, weight_down], [feats_one, feats_one],
    )
    arrived, input_own, input_send = lax.optimization_barrier((arrived, input_own, input_send))
    (summed,) = run(add_kernel, where, arrived, [half_shape(total + small)])
    arrived = from_depths([summed] * depths)
    (joined,) = run(
        functools.partial(join_kernel, small), where, arrived + [norm_rows, cores(norm_rows)],
        [half_shape(depths * (total + small) + 16)],
    )
    arrived = from_sections([joined] * sections)
    across = cores(joined)
    features, input_grad = run(
        place_outputs_kernel, where,
        [features_own, features_other, input_own, cores(input_send)],
        [rows_bf16, shape((mine, in_channels, fine_rows), BF16)],
        [pltpu.SemaphoreType.DMA((4,))],
        hbm_out=(0, 1),
    )
    block = (2, depths * parts[0], channels)
    convs = [shape((conv_rows, channels), F32)] * 2
    down_shape = shape((wide, channels), F32)
    norms = shape(bn_scale.shape, F32)

    def staging(count):
        return [pltpu.VMEM((count,) + block, F32)]

    def rest_scratch():
        return staging(sections) + [
            pltpu.VMEM((depths * small, channels), F32),
            pltpu.SemaphoreType.DMA((sections, 2)),
            pltpu.SemaphoreType.DMA((1,)),
        ]

    arrived, features, input_grad = lax.optimization_barrier((arrived, features, input_grad))
    others = [across] + [cores(piece) for piece in arrived[1:]]
    items = [(False, j) for j in partners(sections)]
    grad_second, grad_first, grad_down, grad_scale, grad_shift = run(
        functools.partial(settle_rest_kernel, items, parts, depths, small, True), where,
        arrived, convs + [down_shape, norms, norms], rest_scratch(),
        hbm_out=(0, 1, 2), flops=10**9,
    )
    items = [(True, j) for j in partners(sections)]
    grad_second, grad_first, grad_down = run(
        functools.partial(settle_rest_kernel, items, parts, depths, small, False), where,
        others + [grad_second, grad_first, grad_down], convs + [down_shape], rest_scratch(),
        hbm_in=(sections, sections + 1, sections + 2), hbm_out=(0, 1, 2),
        aliases={1 + sections: 0, 2 + sections: 1, 3 + sections: 2}, flops=10**9,
    )
    return (
        features,
        jnp.swapaxes(input_grad, 1, 2),
        grad_down.reshape(w_down.shape),
        grad_first.reshape(w_first.shape),
        grad_second.reshape(w_second.shape),
        grad_scale,
        grad_shift,
    )


def solution(mesh):
    in_specs = (
        P(None, "dp", None),
        P(None, None, "dp"),
        P(None, None, "dp"),
        P(),
        P(),
        P(),
        P(),
        P(),
        P(None, "dp", None),
    )
    out_specs = (P("section", "dp", None), P("section", "dp", None), P(), P(), P(), P(), P())
    return jax.shard_map(local, mesh=mesh, in_specs=in_specs, out_specs=out_specs, check_vma=False)
```
